128 devices in a mesh: col: 16 (over x, z_hi, core), row: 8 (over z_lo, y).
Axes of the slice: x: 4, y: 4, z: 4 (z_hi: 2, z_lo: 2; z = z_hi * 2 + z_lo), core: 2. Of those that a mesh axis runs over, the one named last changes fastest.
Arguments:
- noise_bits: int32 [2, 8192, 8192], P(None, 'col', 'row'), may hold values from 0 to 4095
- eigenvalues: float32 [8192, 8192], P('col', 'row'), may hold values from 0.05 to 5
Outputs:
- field: float32 [2, 8192, 8192], P(None, ('col', 'row'))
The draws below stay inside these ranges and needn't reach their ends.
All inputs are finite; a program needn't handle non-finite values.
Results may differ from the reference program's by a relative error of at most 0.000098.
Values sent between devices are 32-bit elements; how exact they have to be, the bound alone decides.
No kernel may reach another device: no remote copies, remote signals or barrier semaphores. Data moves between devices by JAX's collectives and lax.ppermute only.
A program may use at most 128 MiB of HBM per device.

```python
import math
import jax
import jax.numpy as jnp
import numpy as np
from jax import lax

N = 8192
M = 8192
N_COL = 16


def plant(values, stream_key, smallest, largest):
    extent = values.shape
    spot = [jax.random.randint(jax.random.fold_in(stream_key, axis), (), 0, extent[axis]) for axis in range(len(extent))]
    values = values.at[tuple(spot)].set(smallest)
    longest = extent.index(max(extent))
    spot[longest] = (spot[longest] + 1) % extent[longest]
    return values.at[tuple(spot)].set(largest)


def levels(key, dims, cuts, low, high):
    factor_of = 1.0
    for axis_at, blocks in cuts:
        heights = jax.random.uniform(jax.random.fold_in(jax.random.fold_in(key, 6), axis_at), (blocks,), jnp.float32, low / len(cuts), high / len(cuts))
        factor_of = factor_of * jnp.repeat(jnp.exp(heights), dims[axis_at] // blocks).reshape((-1,) + (1,) * (len(dims) - 1 - axis_at))
    return factor_of


def setup_inputs(seed: int = 0) -> dict:
    key_of = jax.random.split(jax.random.key(seed), 3)
    noise_bits = plant(jax.random.randint(key_of[0], (2, N, M), 0, 4096), jax.random.fold_in(key_of[0], 1), 0, 4095).astype(jnp.int32)
    eigenvalues = jnp.clip(jnp.exp(math.log(5.0) - 4.6051702 * jax.random.uniform(key_of[1], (N, M), jnp.float32) ** levels(key_of[1], (N, M), ((0, 16), (1, 8)), -0.2, 0.2)), 0.05, 5.0)
    return {"noise_bits": noise_bits, "eigenvalues": eigenvalues}


def reversed_order(parts):
    digits = parts.bit_length() - 1
    order = []
    for value in range(parts):
        result = 0
        for place in range(digits):
            result = result + ((value >> place & 1) << digits - 1 - place)
        order.append(result)
    return np.array(order, dtype=np.int32)

def reference(noise_bits, eigenvalues):
    inverse = 1.0 / math.sqrt(N * M)
    uniform = (noise_bits.astype(jnp.float32) + 0.5) * 2.0 ** (-12)
    radius = jnp.sqrt(-2.0 * jnp.log(uniform[0])) * jnp.sqrt(eigenvalues) * inverse
    angle = 2.0 * math.pi * uniform[1]
    scaled_re = radius * jnp.cos(angle)
    scaled_im = radius * jnp.sin(angle)
    local_rows = N // N_COL
    order = reversed_order(N_COL)
    values = lax.complex(scaled_re, scaled_im).reshape(N_COL, local_rows, M)
    values = values[order].transpose(1, 0, 2).reshape(N, M)
    spectrum = jnp.fft.fft2(values)
    return jnp.stack([jnp.real(spectrum), jnp.imag(spectrum)]).astype(jnp.float32)
```

```python
import functools
import math

import jax
import jax.numpy as jnp
import ml_dtypes
import numpy as np
from jax import lax
from jax.experimental import pallas as pl
from jax.experimental.pallas import tpu as pltpu
from jax.sharding import Mesh, PartitionSpec as P

N = 8192
M = 8192
LOCAL = 512
WIDTH = 1024
BLOCK = 256

AXES = ("x", "zh", "core", "zl", "y")
SIZES = (4, 2, 2, 2, 4)

F32 = jnp.float32
BF16 = jnp.bfloat16


def halves(table):
    high = table.astype(np.float32).astype(ml_dtypes.bfloat16)
    low = (table - high.astype(np.float64)).astype(np.float32).astype(ml_dtypes.bfloat16)
    return high, low


def split(value):
    high = value.astype(BF16)
    low = (value - high.astype(F32)).astype(BF16)
    return high, low


def complex_table(product, length):
    angle = 2.0 * np.pi * (product % length) / length
    cosine, sine = np.cos(angle), np.sin(angle)
    return np.concatenate(
        [np.concatenate([cosine, sine], 1), np.concatenate([-sine, cosine], 1)], 0
    )


def column_table():
    steps = np.arange(LOCAL)
    return halves(complex_table(np.outer(steps, steps), LOCAL))


def row_tables():
    place = 8 * (4 * np.arange(2)[None, None, :] + np.arange(4)[None, :, None]) + np.arange(8)[:, None, None]
    angle = 2.0 * np.pi * (np.arange(64)[:, None] * place.reshape(1, 64) % 64) / 64
    cosine, sine = np.cos(angle), np.sin(angle)
    real_part = np.stack([cosine, sine], -1).reshape(64, 128)
    imag_part = np.stack([-sine, cosine], -1).reshape(64, 128)
    first = halves(np.concatenate([real_part, imag_part], 0))
    angle = 2.0 * np.pi * (np.outer(np.arange(128), np.arange(128)) % M) / M
    twist = (np.cos(angle).astype(np.float32), (-np.sin(angle)).astype(np.float32))
    second = halves(complex_table(np.outer(np.arange(64), np.arange(128)), 64))
    return first, twist, second


def sine_polynomials():
    nodes = 0.25 * np.cos(np.pi * (np.arange(400) + 0.5) / 800)
    square = np.polynomial.chebyshev.Chebyshev.fit(
        nodes**2, np.sin(2 * np.pi * nodes) / nodes, 4, domain=[0, 1 / 16]
    ).convert(kind=np.polynomial.Polynomial, domain=[-1, 1], window=[-1, 1])
    cosine = np.polynomial.chebyshev.Chebyshev.fit(
        nodes**2, np.cos(2 * np.pi * nodes), 5, domain=[0, 1 / 16]
    ).convert(kind=np.polynomial.Polynomial, domain=[-1, 1], window=[-1, 1])
    return [float(c) for c in square.coef], [float(c) for c in cosine.coef]


SINE, COSINE = sine_polynomials()


def horner(coefficients, value):
    total = jnp.full_like(value, coefficients[-1])
    for coefficient in coefficients[-2::-1]:
        total = total * value + coefficient
    return total


def dot(a, b):
    return jnp.dot(a, b, preferred_element_type=F32)


def dot_nt(a, b):
    return lax.dot_general(a, b, (((1,), (1,)), ((), ())), preferred_element_type=F32)


def draw(bits_0, bits_1, eigen):
    uniform = (bits_0.astype(F32) + 0.5) * 2.0**-12
    radius = jnp.sqrt(jnp.log(uniform) * eigen * (-2.0 / (N * M)))
    past = (bits_1.astype(F32) - 2047.5) * 2.0**-12
    h = jnp.abs(past) - 0.25
    square = h * h
    value_re = radius * (h * horner(SINE, square))
    value_im = jnp.where(past > 0, -radius, radius) * horner(COSINE, square)
    return value_re, value_im


def column_kernel(noise, eigen, high, low, twist, out, data_high, data_low):
    value_re, value_im = draw(noise[0], noise[1], eigen[...])
    for part, value in enumerate((value_re, value_im)):
        data_high[LOCAL * part : LOCAL * (part + 1), :], data_low[LOCAL * part : LOCAL * (part + 1), :] = split(value)

    def rows(place, carry):
        zl, y = place // 4, place % 4
        parts = []
        for part in range(2):
            at = pl.ds(pl.multiple_of(LOCAL * part + 64 * place, 64), 64)
            table = high[at, :]
            parts.append(dot(table, data_high[...]) + dot(low[at, :], data_high[...]) + dot(table, data_low[...]))
        at = pl.ds(pl.multiple_of(64 * place, 64), 64)
        turn_re, turn_im = twist[0, at, :], twist[1, at, :]
        for a in range(BLOCK // 128):
            real, imag = (p[:, 128 * a : 128 * (a + 1)] for p in parts)
            out[a, zl, y, 0] = real * turn_re - imag * turn_im
            out[a, zl, y, 1] = real * turn_im + imag * turn_re
        return carry

    lax.fori_loop(0, 8, rows, 0)


def column_transform(noise, eigen, twist):
    high, low = column_table()
    whole = lambda shape: pl.BlockSpec(shape, lambda i: (0,) * len(shape))
    return pl.pallas_call(
        column_kernel,
        grid=(WIDTH // BLOCK,),
        in_specs=[
            pl.BlockSpec((2, LOCAL, BLOCK), lambda i: (0, 0, i)),
            pl.BlockSpec((LOCAL, BLOCK), lambda i: (0, i)),
            whole((2 * LOCAL, 2 * LOCAL)),
            whole((2 * LOCAL, 2 * LOCAL)),
            whole((2, LOCAL, 128)),
        ],
        out_specs=pl.BlockSpec((BLOCK // 128, 2, 4, 2, 64, 128), lambda i: (i, 0, 0, 0, 0, 0)),
        out_shape=jax.ShapeDtypeStruct((8, 2, 4, 2, 64, 128), F32),
        scratch_shapes=[pltpu.VMEM((2 * LOCAL, BLOCK), BF16), pltpu.VMEM((2 * LOCAL, BLOCK), BF16)],
        compiler_params=pltpu.CompilerParams(vmem_limit_bytes=40 * 2**20),
        cost_estimate=pl.CostEstimate(flops=7 * 10**9, bytes_accessed=14 * 2**20, transcendentals=0),
    )(noise, eigen, jnp.asarray(high), jnp.asarray(low), twist)


def add(a, b):
    return a[0] + b[0], a[1] + b[1]


def sub(a, b):
    return a[0] - b[0], a[1] - b[1]


def turn_back(a):
    return a[1], -a[0]


ROOT = math.sqrt(0.5)


def dft_4(a, b, c, d):
    even, odd = add(a, c), add(b, d)
    less, turned = sub(a, c), turn_back(sub(b, d))
    return add(even, odd), add(less, turned), sub(even, odd), sub(less, turned)


def dft_8(v):
    even = dft_4(v[0], v[2], v[4], v[6])
    odd = dft_4(v[1], v[3], v[5], v[7])
    spun = [
        odd[0],
        ((odd[1][0] + odd[1][1]) * ROOT, (odd[1][1] - odd[1][0]) * ROOT),
        turn_back(odd[2]),
        ((odd[3][1] - odd[3][0]) * ROOT, (odd[3][0] + odd[3][1]) * -ROOT),
    ]
    return [add(e, o) for e, o in zip(even, spun)] + [sub(e, o) for e, o in zip(even, spun)]


def middle_kernel(scalars, mine, other, out):
    sign = scalars[16]
    for row in range(0, 64, 8):
        at = pl.ds(row, 8)
        values = []
        for e in range(8):
            zh, xl, xh = e >> 2, e >> 1 & 1, e & 1
            x = 2 * xh + xl
            re = mine[x, zh, 0, 0, 0, at, :] * sign + other[x, zh, 0, 0, 0, at, :]
            im = mine[x, zh, 0, 0, 1, at, :] * sign + other[x, zh, 0, 0, 1, at, :]
            c, s = scalars[2 * e], scalars[2 * e + 1]
            values.append((re * c - im * s, re * s + im * c))
        for k, (re, im) in enumerate(dft_8(values)):
            zh, xl, xh = k & 1, k >> 1 & 1, k >> 2
            x = 2 * xh + xl
            out[x, zh, 0, 0, 0, at, :] = re
            out[x, zh, 0, 0, 1, at, :] = im


def middle(scalars, mine, other):
    block = (4, 2, 1, 1, 2, 64, 128)
    return pl.pallas_call(
        middle_kernel,
        grid=(2, 4),
        in_specs=[
            pl.BlockSpec(memory_space=pltpu.SMEM),
            pl.BlockSpec(block, lambda i, j: (0, 0, i, j, 0, 0, 0)),
            pl.BlockSpec(block, lambda i, j: (0, 0, i, j, 0, 0, 0)),
        ],
        out_specs=pl.BlockSpec(block, lambda i, j: (0, 0, j, i, 0, 0, 0)),
        out_shape=jax.ShapeDtypeStruct((4, 2, 4, 2, 2, 64, 128), F32),
        cost_estimate=pl.CostEstimate(flops=10**7, bytes_accessed=12 * 2**20, transcendentals=0),
    )(scalars, mine, other)


def row_kernel(x, first_high, first_low, twist, second_high, second_low, out, turned):
    for t in range(8):
        high, low = split(x[:, t, :])
        table = first_high[...]
        step = dot(table, high) + dot(first_low[...], high) + dot(table, low)
        both = []
        for v in range(2):
            re, im = twist[0, 64 * v : 64 * (v + 1), :], twist[1, 64 * v : 64 * (v + 1), :]
            both.append(jnp.concatenate([step[:64] * re - step[64:] * im, step[:64] * im + step[64:] * re], 1))
        high, low = split(jnp.concatenate(both, 0))
        table = second_high[...]
        last = dot_nt(table, high) + dot_nt(second_low[...], high) + dot_nt(table, low)
        turned[pl.ds(t, 128, stride=8), :] = last
    for part in range(2):
        for u in range(64):
            out[part, :, 128 * u : 128 * (u + 1)] = turned[8 * (64 * part + u) : 8 * (64 * part + u) + 8, :]


def row_transform(x):
    first, twist, second = row_tables()
    whole = lambda shape: pl.BlockSpec(shape, lambda i: (0,) * len(shape))
    return pl.pallas_call(
        row_kernel,
        grid=(8,),
        in_specs=[
            pl.BlockSpec((128, 8, 128), lambda i: (0, i, 0)),
            whole((128, 128)),
            whole((128, 128)),
            whole((2, 128, 128)),
            whole((128, 256)),
            whole((128, 256)),
        ],
        out_specs=pl.BlockSpec((2, 8, M), lambda i: (0, i, 0)),
        out_shape=jax.ShapeDtypeStruct((2, 64, M), F32),
        scratch_shapes=[pltpu.VMEM((1024, 128), F32)],
        compiler_params=pltpu.CompilerParams(vmem_limit_bytes=32 * 2**20),
        cost_estimate=pl.CostEstimate(flops=3 * 10**9, bytes_accessed=9 * 2**20, transcendentals=0),
    )(x, *(jnp.asarray(t) for t in first), jnp.stack([jnp.asarray(t) for t in twist]), *(jnp.asarray(t) for t in second))


def on_device(noise, eigen):
    xh, xl = lax.axis_index("x") // 2, lax.axis_index("x") % 2
    zh, core = lax.axis_index("zh"), lax.axis_index("core")
    anchor = 8 * core + 4 * zh + 2 * xl + xh
    angle = (anchor * jnp.arange(LOCAL, dtype=jnp.int32) % N).astype(F32) * (-2.0 * math.pi / N)
    twist = jnp.broadcast_to(jnp.stack([jnp.cos(angle), jnp.sin(angle)])[:, :, None], (2, LOCAL, 128))
    angle = (core * jnp.arange(8, dtype=jnp.int32)).astype(F32) * (-2.0 * math.pi / 16)
    scalars = jnp.concatenate(
        [jnp.stack([jnp.cos(angle), jnp.sin(angle)], 1).reshape(16), (1 - 2 * core).astype(F32)[None]]
    )
    with jax.named_scope("columns"):
        current = column_transform(noise, eigen, twist)
    with jax.named_scope("first_exchange"):
        current = lax.all_to_all(current.reshape(16, 4, 2, 64, 128), ("x", "zh", "zl"), 0, 0, tiled=True)
        current = current.reshape(4, 2, 2, 4, 2, 64, 128)
    with jax.named_scope("core_exchange"):
        other = lax.ppermute(current, "core", [(0, 1), (1, 0)])
    with jax.named_scope("middle"):
        current = middle(scalars, current, other)
    with jax.named_scope("second_exchange"):
        current = lax.all_to_all(current.reshape(32, 2, 2, 64, 128), ("x", "zh", "y"), 0, 0, tiled=True)
        current = current.reshape(128, 64, 128)
    with jax.named_scope("rows"):
        return row_transform(current)


def solution(mesh):
    fine = Mesh(mesh.devices.reshape(SIZES), AXES)
    col, row = AXES[:3], AXES[3:]
    return jax.shard_map(
        on_device,
        mesh=fine,
        in_specs=(P(None, col, row), P(col, row)),
        out_specs=P(None, AXES, None),
        check_vma=False,
    )
```

```python
import functools
import math

import jax
import jax.numpy as jnp
import ml_dtypes
import numpy as np
from jax import lax
from jax.experimental import pallas as pl
from jax.experimental.pallas import tpu as pltpu
from jax.sharding import Mesh, PartitionSpec as P

N = 8192
M = 8192
LOCAL = 512
WIDTH = 1024
KINDS = ("x", "z", "x", "z")
CHUNKS = len(KINDS)
ROWS = 64 // CHUNKS

AXES = ("x", "zh", "core", "zl", "y")
SIZES = (4, 2, 2, 2, 4)

F32 = jnp.float32
BF16 = jnp.bfloat16


def halves(table):
    high = table.astype(np.float32).astype(ml_dtypes.bfloat16)
    low = (table - high.astype(np.float64)).astype(np.float32).astype(ml_dtypes.bfloat16)
    return high, low


def split(value):
    high = value.astype(BF16)
    low = (value - high.astype(F32)).astype(BF16)
    return high, low


def complex_table(product, length):
    angle = 2.0 * np.pi * (product % length) / length
    cosine, sine = np.cos(angle), np.sin(angle)
    return np.concatenate(
        [np.concatenate([cosine, sine], 1), np.concatenate([-sine, cosine], 1)], 0
    )


def column_tables():
    steps = np.arange(LOCAL)
    table = complex_table(np.outer(steps, steps), LOCAL)
    table = table.reshape(2, 2, 4, CHUNKS, ROWS, 2 * LOCAL).transpose(3, 1, 0, 2, 4, 5)
    return np.stack(halves(table.reshape(CHUNKS, 16 * ROWS, 2 * LOCAL)))


def row_tables(kind):
    x, zh, y, first_of = np.arange(4), np.arange(2), np.arange(4), []
    zl = np.arange(2)
    for at_x in range(4):
        for at_zh in range(2):
            for at_y in range(4):
                a_x, a_zh, a_y = x ^ at_x, zh ^ at_zh, y ^ at_y
                if kind == "x":
                    a = 2 * a_x[None, :] + a_zh[:, None]
                else:
                    a = 2 * a_x[:, None] + a_zh[None, :]
                r = 4 * zl[:, None] + a_y[None, :]
                place = (8 * r[None, None] + a[:, :, None, None]).reshape(64)
                angle = 2.0 * np.pi * (np.outer(np.arange(64), place) % 64) / 64
                cosine, sine = np.cos(angle), np.sin(angle)
                real_part = np.stack([cosine, sine], -1).reshape(64, 128)
                imag_part = np.stack([-sine, cosine], -1).reshape(64, 128)
                first_of.append(np.stack(halves(np.concatenate([real_part, imag_part], 0))))
    angle = 2.0 * np.pi * (np.outer(np.arange(128), np.arange(128)) % M) / M
    twist = np.stack([np.cos(angle), -np.sin(angle)]).astype(np.float32)
    second = np.stack(halves(complex_table(np.outer(np.arange(64), np.arange(128)), 64)))
    return np.stack(first_of), twist, second


def sine_polynomials():
    nodes = 0.25 * np.cos(np.pi * (np.arange(400) + 0.5) / 800)
    square = np.polynomial.chebyshev.Chebyshev.fit(
        nodes**2, np.sin(2 * np.pi * nodes) / nodes, 4, domain=[0, 1 / 16]
    ).convert(kind=np.polynomial.Polynomial, domain=[-1, 1], window=[-1, 1])
    cosine = np.polynomial.chebyshev.Chebyshev.fit(
        nodes**2, np.cos(2 * np.pi * nodes), 5, domain=[0, 1 / 16]
    ).convert(kind=np.polynomial.Polynomial, domain=[-1, 1], window=[-1, 1])
    return [float(c) for c in square.coef], [float(c) for c in cosine.coef]


SINE, COSINE = sine_polynomials()


def horner(coefficients, value):
    total = jnp.full_like(value, coefficients[-1])
    for coefficient in coefficients[-2::-1]:
        total = total * value + coefficient
    return total


def dot(a, b):
    return jnp.dot(a, b, preferred_element_type=F32)


def dot_nt(a, b):
    return lax.dot_general(a, b, (((1,), (1,)), ((), ())), preferred_element_type=F32)


def draw(bits_0, bits_1, eigen):
    uniform = (bits_0.astype(F32) + 0.5) * 2.0**-12
    radius = jnp.sqrt(jnp.log(uniform) * eigen * (-2.0 / (N * M)))
    past = (bits_1.astype(F32) - 2047.5) * 2.0**-12
    h = jnp.abs(past) - 0.25
    square = h * h
    value_re = radius * (h * horner(SINE, square))
    value_im = jnp.where(past > 0, -radius, radius) * horner(COSINE, square)
    return value_re, value_im


def draw_kernel(noise, eigen, high, low):
    for part, value in enumerate(draw(noise[0], noise[1], eigen[...])):
        at = slice(LOCAL * part, LOCAL * (part + 1))
        high[at, :], low[at, :] = split(value)


def draw_field(noise, eigen):
    block = 128
    shape = jax.ShapeDtypeStruct((2 * LOCAL, WIDTH), BF16)
    return pl.pallas_call(
        draw_kernel,
        grid=(WIDTH // block,),
        in_specs=[
            pl.BlockSpec((2, LOCAL, block), lambda i: (0, 0, i)),
            pl.BlockSpec((LOCAL, block), lambda i: (0, i)),
        ],
        out_specs=[pl.BlockSpec((2 * LOCAL, block), lambda i: (0, i))] * 2,
        out_shape=[shape, shape],
        compiler_params=pltpu.CompilerParams(vmem_limit_bytes=32 * 2**20),
        cost_estimate=pl.CostEstimate(flops=10**7, bytes_accessed=10 * 2**20, transcendentals=0),
    )(noise, eigen)


def column_kernel(kind, place, high, low, table, twist, *outs):
    x, zh, zl = place[0], place[1], place[3]
    half = 4 * ROWS
    for d in range(4):
        columns = pl.ds(pl.multiple_of(256 * (d ^ x), 256), 256)
        data_high, data_low = high[:, columns], low[:, columns]
        for d_zl in range(2):
            zl_out = d_zl ^ zl
            at = pl.ds(pl.multiple_of(2 * half * zl_out, 2 * half), 2 * half)
            table_high = table[0, at, :]
            both = dot(table_high, data_high) + dot(table[1, at, :], data_high) + dot(table_high, data_low)
            at = pl.ds(pl.multiple_of(half * zl_out, half), half)
            turn_re, turn_im = twist[0, at, :], twist[1, at, :]
            turned = []
            for a in range(2):
                re, im = both[:half, 128 * a : 128 * a + 128], both[half:, 128 * a : 128 * a + 128]
                turned.append((re * turn_re - im * turn_im, re * turn_im + im * turn_re))
            for part in range(2):
                first, second = turned[0][part], turned[1][part]
                for d_zh in range(2):
                    value = jnp.where(zh == d_zh, first, second)
                    value = value.reshape(4, ROWS, 128)
                    for y in range(4):
                        d_y = y ^ place[4]
                        if kind == "x":
                            outs[d][2 * d_zh + d_zl, d_y, part] = value[y]
                        else:
                            outs[2 * d_zh + d_zl][d, d_y, part] = value[y]


IN_VMEM = pl.BlockSpec(memory_space=pltpu.VMEM)
IN_SMEM = pl.BlockSpec(memory_space=pltpu.SMEM)


def column_transform(kind, place, high, low, table, twist):
    shape = jax.ShapeDtypeStruct((4, 4, 2, ROWS, 128), F32)
    return pl.pallas_call(
        functools.partial(column_kernel, kind),
        in_specs=[IN_SMEM] + [IN_VMEM] * 4,
        out_specs=[IN_VMEM] * 4,
        out_shape=[shape] * 4,
        compiler_params=pltpu.CompilerParams(vmem_limit_bytes=40 * 2**20),
        cost_estimate=pl.CostEstimate(flops=7 * 10**9 // CHUNKS, bytes_accessed=6 * 2**20, transcendentals=0),
    )(place, high, low, table, twist)


def add(a, b):
    return a[0] + b[0], a[1] + b[1]


def sub(a, b):
    return a[0] - b[0], a[1] - b[1]


def turn_back(a):
    return a[1], -a[0]


ROOT = math.sqrt(0.5)


def dft_4(a, b, c, d):
    even, odd = add(a, c), add(b, d)
    less, turned = sub(a, c), turn_back(sub(b, d))
    return add(even, odd), add(less, turned), sub(even, odd), sub(less, turned)


def dft_8(v):
    even = dft_4(v[0], v[2], v[4], v[6])
    odd = dft_4(v[1], v[3], v[5], v[7])
    spun = [
        odd[0],
        ((odd[1][0] + odd[1][1]) * ROOT, (odd[1][1] - odd[1][0]) * ROOT),
        turn_back(odd[2]),
        ((odd[3][1] - odd[3][0]) * ROOT, (odd[3][0] + odd[3][1]) * -ROOT),
    ]
    return [add(e, o) for e, o in zip(even, spun)] + [sub(e, o) for e, o in zip(even, spun)]


def middle_kernel(kind, place, scalars, mine, other, *outs):
    sign = scalars[16]
    at_x, at_zh, at_zl = place[0], place[1], place[3]

    def run(here):
        def step(d_y, carry):
            for zl in range(2):
                for row in range(0, ROWS, 8):
                    at = pl.ds(row, 8)
                    values = []
                    for e in range(8):
                        zh, xl, xh = e >> 2, e >> 1 & 1, e & 1
                        d_x, d_z = (2 * xh + xl) ^ at_x, 2 * (zh ^ at_zh) + (zl ^ at_zl)
                        index = (d_z, d_y, d_x) if kind == "x" else (d_y, d_x, d_z)
                        re = mine[*index, 0, at, :] * sign + other[*index, 0, at, :]
                        im = mine[*index, 1, at, :] * sign + other[*index, 1, at, :]
                        c, s = scalars[2 * e], scalars[2 * e + 1]
                        values.append((re * c - im * s, re * s + im * c))
                    for k, value in enumerate(dft_8(values)):
                        zh, x = k & 1, 2 * (k >> 2) + (k >> 1 & 1)
                        for part in range(2):
                            if kind == "x":
                                outs[x ^ here][zh ^ at_zh, zl, d_y, part, at, :] = value[part]
                            else:
                                outs[zh ^ here][x ^ at_x, zl, d_y, part, at, :] = value[part]
            return carry

        lax.fori_loop(0, 4, step, 0)

    for here in range(4 if kind == "x" else 2):
        pl.when((at_x if kind == "x" else at_zh) == here)(functools.partial(run, here))


def middle(kind, place, scalars, mine, other):
    count = 4 if kind == "x" else 2
    shape = jax.ShapeDtypeStruct((8 // count, 2, 4, 2, ROWS, 128), F32)
    return pl.pallas_call(
        functools.partial(middle_kernel, kind),
        in_specs=[IN_SMEM] * 2 + [IN_VMEM] * 2,
        out_specs=[IN_VMEM] * count,
        out_shape=[shape] * count,
        compiler_params=pltpu.CompilerParams(vmem_limit_bytes=32 * 2**20),
        cost_estimate=pl.CostEstimate(flops=10**7, bytes_accessed=3 * 2**20, transcendentals=0),
    )(place, scalars, mine, other)


def row_kernel(count, *refs):
    pieces, (first, twist, second) = refs[:count], refs[count : count + 3]
    out, turned = refs[-2:]
    for t in range(8):
        high, low = split(jnp.concatenate([piece[:, t, :] for piece in pieces], 0))
        table = first[0]
        step = dot(table, high) + dot(first[1], high) + dot(table, low)
        both = []
        for v in range(2):
            re, im = twist[0, 64 * v : 64 * (v + 1), :], twist[1, 64 * v : 64 * (v + 1), :]
            both.append(jnp.concatenate([step[:64] * re - step[64:] * im, step[:64] * im + step[64:] * re], 1))
        high, low = split(jnp.concatenate(both, 0))
        table = second[0]
        last = dot_nt(table, high) + dot_nt(second[1], high) + dot_nt(table, low)
        turned[pl.ds(t, 128, stride=8), :] = last
    for part in range(2):
        for u in range(64):
            out[part, :, 128 * u : 128 * (u + 1)] = turned[8 * (64 * part + u) : 8 * (64 * part + u) + 8, :]


def row_transform(chunk, result, pieces, first, twist, second):
    count = len(pieces)
    pieces = [piece.reshape(128 // count, ROWS, 128) for piece in pieces]
    whole = lambda shape: pl.BlockSpec(shape, lambda i: (0,) * len(shape))
    kernel = functools.partial(row_kernel, count)
    operands = pieces + [first, twist, second]
    specs = [pl.BlockSpec((128 // count, 8, 128), lambda i: (0, i, 0))] * count
    specs += [whole(first.shape), whole(twist.shape), whole(second.shape)]
    aliases = {}
    if result is not None:
        aliases = {len(operands): 0}
        operands.append(result)
        specs.append(pl.BlockSpec(memory_space=pl.ANY))
    steps = ROWS // 8
    return pl.pallas_call(
        kernel,
        grid=(steps,),
        in_specs=specs,
        out_specs=pl.BlockSpec((2, 8, M), lambda i: (0, chunk * steps + i, 0)),
        out_shape=jax.ShapeDtypeStruct((2, 64, M), F32),
        input_output_aliases=aliases,
        scratch_shapes=[pltpu.VMEM((1024, 128), F32)],
        compiler_params=pltpu.CompilerParams(vmem_limit_bytes=32 * 2**20),
        cost_estimate=pl.CostEstimate(flops=3 * 10**9 // CHUNKS, bytes_accessed=2 * 2**20, transcendentals=0),
    )(*operands)


def swap(value, axis, apart):
    if apart == 0:
        return value
    count = math.prod(SIZES[AXES.index(name)] for name in (axis if isinstance(axis, tuple) else (axis,)))
    return lax.ppermute(value, axis, [(i, i ^ apart) for i in range(count)])


def exchange(pieces, axis):
    return [swap(piece, axis, d) for d, piece in enumerate(pieces)]


def regroup(pieces, count):
    return [jnp.stack([piece[j] for piece in pieces]) for j in range(count)]


Z = ("zh", "zl")


def on_device(noise, eigen):
    place = jnp.stack([lax.axis_index(name) for name in AXES]).astype(jnp.int32)
    x, zh, core = place[0], place[1], place[2]
    xh, xl = x // 2, x % 2
    anchor = 8 * core + 4 * zh + 2 * xl + xh
    rows = jnp.arange(LOCAL, dtype=jnp.int32).reshape(8, CHUNKS, ROWS).transpose(1, 0, 2).reshape(CHUNKS, 8 * ROWS)
    angle = (anchor * rows % N).astype(F32) * (-2.0 * math.pi / N)
    twist = jnp.stack([jnp.cos(angle), jnp.sin(angle)], 1)
    twist = jnp.broadcast_to(twist[..., None], (CHUNKS, 2, 8 * ROWS, 128))
    angle = (core * jnp.arange(8, dtype=jnp.int32)).astype(F32) * (-2.0 * math.pi / 16)
    scalars = jnp.concatenate(
        [jnp.stack([jnp.cos(angle), jnp.sin(angle)], 1).reshape(16), (1 - 2 * core).astype(F32)[None]]
    )
    tables = {kind: row_tables(kind) for kind in sorted(set(KINDS))}
    own = (x * 2 + zh) * 4 + place[4]
    firsts = {
        kind: lax.dynamic_index_in_dim(jnp.asarray(table[0]), own, 0, keepdims=False) for kind, table in tables.items()
    }
    row_twist, second = (jnp.asarray(t) for t in tables[KINDS[0]][1:])
    column_table = column_tables()

    with jax.named_scope("draw"):
        high, low = draw_field(noise, eigen)
    current = []
    for chunk, kind in enumerate(KINDS):
        with jax.named_scope(f"columns_{chunk}"):
            current.append(
                column_transform(kind, place, high, low, jnp.asarray(column_table[:, chunk]), twist[chunk])
            )
    result = None
    for chunk, kind in enumerate(KINDS):
        pieces = current[chunk]
        with jax.named_scope(f"out_{chunk}"):
            if kind == "x":
                pieces = exchange(pieces, "x")
                pieces = [jnp.stack([piece[:, j] for piece in pieces], 1) for j in range(4)]
                pieces = exchange(pieces, "y")
                pieces = exchange(regroup(pieces, 4), Z)
            else:
                pieces = exchange(pieces, Z)
                pieces = exchange(regroup(pieces, 4), "x")
                pieces = [jnp.stack([piece[:, j] for piece in pieces]) for j in range(4)]
                pieces = exchange(pieces, "y")
            mine = jnp.stack(pieces)
            other = swap(mine, "core", 1)
        with jax.named_scope(f"middle_{chunk}"):
            pieces = middle(kind, place, scalars, mine, other)
        with jax.named_scope(f"back_{chunk}"):
            if kind == "x":
                pieces = exchange(pieces, "x")
                pieces = exchange(regroup(pieces, 2), "zh")
            else:
                pieces = exchange(pieces, "zh")
                pieces = exchange(regroup(pieces, 4), "x")
        with jax.named_scope(f"rows_{chunk}"):
            result = row_transform(chunk, result, pieces, firsts[kind], row_twist, second)
    return result


def solution(mesh):
    fine = Mesh(mesh.devices.reshape(SIZES), AXES)
    col, row = AXES[:3], AXES[3:]
    return jax.shard_map(
        on_device,
        mesh=fine,
        in_specs=(P(None, col, row), P(col, row)),
        out_specs=P(None, AXES, None),
        check_vma=False,
    )
```

```python
import functools
import math

import jax
import jax.numpy as jnp
import ml_dtypes
import numpy as np
from jax import lax
from jax.experimental import pallas as pl
from jax.experimental.pallas import tpu as pltpu
from jax.sharding import Mesh, PartitionSpec as P

N = 8192
M = 8192
LOCAL = 512
WIDTH = 1024
BLOCK = 256
STEPS = WIDTH // BLOCK

AXES = ("x", "zh", "core", "zl", "y")
SIZES = (4, 2, 2, 2, 4)

F32 = jnp.float32
BF16 = jnp.bfloat16


def halves(table):
    high = table.astype(np.float32).astype(ml_dtypes.bfloat16)
    low = (table - high.astype(np.float64)).astype(np.float32).astype(ml_dtypes.bfloat16)
    return high, low


def split(value):
    high = value.astype(BF16)
    low = (value - high.astype(F32)).astype(BF16)
    return high, low


def column_table():
    row = 4 * np.arange(128)[None, :, None] + np.arange(4)[:, None, None]
    angle = 2.0 * np.pi * (row * np.arange(128) % LOCAL) / LOCAL
    return np.stack([np.cos(angle), np.sin(angle)]).astype(np.float32)


def row_tables():
    place = 8 * (4 * np.arange(2)[None, None, :] + np.arange(4)[None, :, None]) + np.arange(8)[:, None, None]
    angle = 2.0 * np.pi * (np.arange(64)[:, None] * place.reshape(1, 64) % 64) / 64
    cosine, sine = np.cos(angle), np.sin(angle)
    real_part = np.stack([cosine, sine], -1).reshape(64, 128)
    imag_part = np.stack([-sine, cosine], -1).reshape(64, 128)
    high, low = halves(np.concatenate([real_part, imag_part], 0))
    first = np.concatenate([np.concatenate([high, high], 1), np.concatenate([low, np.zeros_like(low)], 1)], 0)
    angle = 2.0 * np.pi * (np.outer(np.arange(128), np.arange(128)) % M) / M
    twist = np.stack([np.cos(angle), -np.sin(angle)]).astype(np.float32)
    angle = 2.0 * np.pi * (np.outer(np.arange(128), np.arange(64)) % 64) / 64
    cosine, sine = np.cos(angle), np.sin(angle)
    last = np.concatenate([np.concatenate([cosine, -sine], 1), np.concatenate([sine, cosine], 1)], 0)
    return first, twist, np.concatenate(halves(last), 1)


def sine_polynomials():
    nodes = 0.25 * np.cos(np.pi * (np.arange(400) + 0.5) / 800)
    square = np.polynomial.chebyshev.Chebyshev.fit(
        nodes**2, np.sin(2 * np.pi * nodes) / nodes, 4, domain=[0, 1 / 16]
    ).convert(kind=np.polynomial.Polynomial, domain=[-1, 1], window=[-1, 1])
    cosine = np.polynomial.chebyshev.Chebyshev.fit(
        nodes**2, np.cos(2 * np.pi * nodes), 5, domain=[0, 1 / 16]
    ).convert(kind=np.polynomial.Polynomial, domain=[-1, 1], window=[-1, 1])
    return [float(c) for c in square.coef], [float(c) for c in cosine.coef]


SINE, COSINE = sine_polynomials()


def horner(coefficients, value):
    total = jnp.full_like(value, coefficients[-1])
    for coefficient in coefficients[-2::-1]:
        total = total * value + coefficient
    return total


def dot(a, b):
    return jnp.dot(a, b, preferred_element_type=F32)


def draw(bits_0, bits_1, eigen):
    uniform = (bits_0.astype(F32) + 0.5) * 2.0**-12
    radius = jnp.sqrt(jnp.log(uniform) * eigen * (-2.0 / (N * M)))
    past = (bits_1.astype(F32) - 2047.5) * 2.0**-12
    h = jnp.abs(past) - 0.25
    square = h * h
    value_re = radius * (h * horner(SINE, square))
    value_im = jnp.where(past > 0, -radius, radius) * horner(COSINE, square)
    return value_re, value_im


def add(a, b):
    return a[0] + b[0], a[1] + b[1]


def sub(a, b):
    return a[0] - b[0], a[1] - b[1]


def turn_back(a):
    return a[1], -a[0]


def dft_4(a, b, c, d):
    even, odd = add(a, c), add(b, d)
    less, turned = sub(a, c), turn_back(sub(b, d))
    return add(even, odd), add(less, turned), sub(even, odd), sub(less, turned)


def spin(a, step):
    if step == 0:
        return a
    if step == 4:
        return turn_back(a)
    if step % 4 == 2:
        root = math.sqrt(0.5)
        a = ((a[0] + a[1]) * root, (a[1] - a[0]) * root)
        return a if step == 2 else turn_back(a)
    c, s = math.cos(math.pi * step / 8), math.sin(math.pi * step / 8)
    return a[0] * c + a[1] * s, a[1] * c - a[0] * s


def dft_16(v):
    first = [dft_4(v[e], v[4 + e], v[8 + e], v[12 + e]) for e in range(4)]
    second = [dft_4(*(spin(first[e][s], e * s) for e in range(4))) for s in range(4)]
    return [second[k % 4][k // 4] for k in range(16)]


def front_kernel(noise, eigen, base, turn, out, bits, eig, base_in, turn_in, tables, high, low, arrived):
    step = pl.program_id(0)

    def copies():
        for i in range(STEPS):
            columns = slice(BLOCK * i, BLOCK * (i + 1))
            yield pltpu.make_async_copy(noise.at[:, :, columns], bits.at[i], arrived.at[i])
            yield pltpu.make_async_copy(eigen.at[:, columns], eig.at[i], arrived.at[STEPS + i])
        yield pltpu.make_async_copy(base, base_in, arrived.at[2 * STEPS])
        yield pltpu.make_async_copy(turn, turn_in, arrived.at[2 * STEPS + 1])

    moves = list(copies())

    def start():
        for move in moves:
            move.start()

    def prepare():
        moves[-2].wait()
        moves[-1].wait()
        for r in range(4):
            cosine = base_in[0, r] * turn_in[0, r] - base_in[1, r] * turn_in[1, r]
            sine = base_in[1, r] * turn_in[0, r] + base_in[0, r] * turn_in[1, r]
            (cosine, cosine_low), (sine, sine_low) = split(cosine), split(sine)
            for at, c, s in ((0, cosine, sine), (256, cosine_low, sine_low)):
                tables[r, at : at + 128, :128] = c
                tables[r, at : at + 128, 128:] = s
                tables[r, at + 128 : at + 256, :128] = -s
                tables[r, at + 128 : at + 256, 128:] = c

    def wait(i):
        moves[2 * i].wait()
        moves[2 * i + 1].wait()

    def draws():
        parts = [
            draw(bits[step, 0, at, :], bits[step, 1, at, :], eig[step, at, :])
            for at in (slice(128 * j, 128 * (j + 1)) for j in range(4))
        ]
        for r, value in enumerate(dft_4(*parts)):
            for part in range(2):
                at = slice(128 * part, 128 * (part + 1))
                high[r, at, :], low[r, at, :] = split(value[part])

    def multiply():
        for r in range(4):
            both = dot(tables[r], high[r])
            both = both[:256] + both[256:] + dot(tables[r, :256, :], low[r])
            for a in range(BLOCK // 128):
                for row in range(0, 256, 8):
                    part, zl, y, b = row // 128, row // 64 % 2, row // 16 % 4, row // 8 % 2
                    out[a, b, zl, y, part, r] = both[row : row + 8, 128 * a : 128 * (a + 1)]

    @pl.when(step == 0)
    def _():
        start()
        wait(0)
        draws()
        prepare()

    for i in range(1, STEPS):
        pl.when(step == i)(functools.partial(wait, i))

    @pl.when(jnp.logical_and(step > 0, step < STEPS))
    def _():
        multiply()
        draws()

    pl.when(step == STEPS)(multiply)


def front(noise, eigen, turn):
    base = jnp.asarray(column_table())
    in_hbm = pl.BlockSpec(memory_space=pltpu.HBM)
    return pl.pallas_call(
        front_kernel,
        grid=(STEPS + 1,),
        in_specs=[in_hbm] * 4,
        out_specs=pl.BlockSpec(
            (BLOCK // 128, 2, 2, 4, 2, 4, 8, 128), lambda i: (jnp.maximum(i - 1, 0), 0, 0, 0, 0, 0, 0, 0)
        ),
        out_shape=jax.ShapeDtypeStruct((8, 2, 2, 4, 2, 4, 8, 128), F32),
        scratch_shapes=[
            pltpu.VMEM((STEPS, 2, LOCAL, BLOCK), jnp.int32),
            pltpu.VMEM((STEPS, LOCAL, BLOCK), F32),
            pltpu.VMEM((2, 4, 128, 128), F32),
            pltpu.VMEM((2, 4, 128, 128), F32),
            pltpu.VMEM((4, 512, 256), BF16),
            pltpu.VMEM((4, 256, BLOCK), BF16),
            pltpu.VMEM((4, 256, BLOCK), BF16),
            pltpu.SemaphoreType.DMA((2 * STEPS + 2,)),
        ],
        compiler_params=pltpu.CompilerParams(vmem_limit_bytes=40 * 2**20),
        cost_estimate=pl.CostEstimate(flops=2 * 10**9, bytes_accessed=12 * 2**20, transcendentals=0),
    )(noise, eigen, base, turn)


IN_VMEM = pl.BlockSpec(memory_space=pltpu.VMEM)


def middle_kernel(data, out):
    def step(at, carry):
        y, part = at // 4, at % 4
        row = pl.ds(pl.multiple_of(8 * part, 8), 8)
        for zl in range(2):
            values = []
            for e in range(16):
                core, zh, xl, xh = e >> 3, e >> 2 & 1, e >> 1 & 1, e & 1
                index = (2 * xh + xl, zh, core, zl, y)
                values.append((data[*index, 0, row, :], data[*index, 1, row, :]))
            for k, value in enumerate(dft_16(values)):
                core, zh, xl, xh = k & 1, k >> 1 & 1, k >> 2 & 1, k >> 3
                index = (2 * xh + xl, zh, core, y, zl)
                out[*index, 0, row, :], out[*index, 1, row, :] = value
        return carry

    lax.fori_loop(0, 16, step, 0)


def middle(data):
    return pl.pallas_call(
        middle_kernel,
        in_specs=[IN_VMEM],
        out_specs=IN_VMEM,
        out_shape=jax.ShapeDtypeStruct((4, 2, 2, 4, 2, 2, 32, 128), F32),
        compiler_params=pltpu.CompilerParams(vmem_limit_bytes=32 * 2**20),
        cost_estimate=pl.CostEstimate(flops=10**7, bytes_accessed=8 * 2**20, transcendentals=0),
    )(data)


def row_kernel(data, first, twist, last, out):
    step = pl.program_id(0)
    start = 512 * (step // 2) + 4 * (step % 2)

    def piece(t):
        row = start + 8 * (t % 4) + t // 4
        return jnp.concatenate([data[pl.ds(1024 * a + row, 16, stride=32), :] for a in range(8)], 0)

    high, low = split(jnp.concatenate([piece(t) for t in range(16)], 1))
    sums = dot(first[...], jnp.concatenate([high, low], 0))
    sums = sums[:128] + sums[128:]
    for t in range(16):
        re, im = sums[:64, 128 * t : 128 * (t + 1)], sums[64:, 128 * t : 128 * (t + 1)]
        both = []
        for v in range(2):
            c, s = twist[0, 64 * v : 64 * (v + 1), :], twist[1, 64 * v : 64 * (v + 1), :]
            both.append(jnp.concatenate([re * c - im * s, re * s + im * c], 1))
        high, low = split(jnp.concatenate(both, 0))
        whole = dot(high, last[...])
        whole = (whole[:, :128] + whole[:, 128:] + dot(low, last[:, :128])).T
        for part in range(2):
            out[part, t // 8, :, t % 8, :] = whole[64 * part : 64 * (part + 1)]


def row_transform(data):
    tables = [jnp.asarray(table) for table in row_tables()]
    result = pl.pallas_call(
        row_kernel,
        grid=(4,),
        in_specs=[IN_VMEM] * 4,
        out_specs=pl.BlockSpec((2, 2, 64, 8, 128), lambda i: (0, i, 0, 0, 0)),
        out_shape=jax.ShapeDtypeStruct((2, 8, 64, 8, 128), F32),
        compiler_params=pltpu.CompilerParams(vmem_limit_bytes=48 * 2**20),
        cost_estimate=pl.CostEstimate(flops=3 * 10**9, bytes_accessed=9 * 2**20, transcendentals=0),
    )(data.reshape(8192, 128), *tables)
    return result.transpose(0, 1, 3, 2, 4).reshape(2, 64, M)


def on_device(noise, eigen):
    x, zh, core = (lax.axis_index(name) for name in AXES[:3])
    anchor = 8 * core + 4 * zh + 2 * (x % 2) + x // 2
    row = 4 * jnp.arange(128, dtype=jnp.int32)[None, :] + jnp.arange(4, dtype=jnp.int32)[:, None]
    angle = (anchor * row).astype(F32) * (2.0 * math.pi / N)
    turn = jnp.broadcast_to(jnp.stack([jnp.cos(angle), jnp.sin(angle)])[..., None], (2, 4, 128, 128))
    with jax.named_scope("columns"):
        data = front(noise, eigen, turn)
    with jax.named_scope("first_exchange"):
        data = lax.all_to_all(data.reshape(32, 4, 2, 32, 128), ("x", "zh", "core", "zl"), 0, 0, tiled=True)
    with jax.named_scope("middle"):
        data = middle(data.reshape(4, 2, 2, 2, 4, 2, 32, 128))
    with jax.named_scope("second_exchange"):
        data = lax.all_to_all(data.reshape(64, 2, 2, 32, 128), ("x", "zh", "core", "y"), 0, 0, tiled=True)
    with jax.named_scope("rows"):
        return row_transform(data)


def solution(mesh):
    fine = Mesh(mesh.devices.reshape(SIZES), AXES)
    col, row = AXES[:3], AXES[3:]
    return jax.shard_map(
        on_device,
        mesh=fine,
        in_specs=(P(None, col, row), P(col, row)),
        out_specs=P(None, AXES, None),
        check_vma=False,
    )
```

```python
import functools
import math

import jax
import jax.numpy as jnp
import ml_dtypes
import numpy as np
from jax import lax
from jax.experimental import pallas as pl
from jax.experimental.pallas import tpu as pltpu
from jax.sharding import Mesh, PartitionSpec as P

N = 8192
M = 8192
LOCAL = 512
WIDTH = 1024
BLOCK = 256
STEPS = WIDTH // BLOCK

AXES = ("x", "zh", "core", "zl", "y")
SIZES = (4, 2, 2, 2, 4)

F32 = jnp.float32
BF16 = jnp.bfloat16


def halves(table):
    high = table.astype(np.float32).astype(ml_dtypes.bfloat16)
    low = (table - high.astype(np.float64)).astype(np.float32).astype(ml_dtypes.bfloat16)
    return high, low


def split(value):
    high = value.astype(BF16)
    low = (value - high.astype(F32)).astype(BF16)
    return high, low


def column_table():
    row = 4 * np.arange(128)[None, :, None] + np.arange(4)[:, None, None]
    angle = 2.0 * np.pi * (row * np.arange(128) % LOCAL) / LOCAL
    return np.stack([np.cos(angle), np.sin(angle)]).astype(np.float32)


def row_tables():
    place = 8 * (4 * np.arange(2)[None, :, None] + np.arange(4)[None, None, :]) + np.arange(8)[:, None, None]
    angle = 2.0 * np.pi * (np.arange(64)[:, None] * place.reshape(1, 64) % 64) / 64
    cosine, sine = np.cos(angle), np.sin(angle)
    real_part = np.stack([cosine, sine], -1).reshape(64, 128)
    imag_part = np.stack([-sine, cosine], -1).reshape(64, 128)
    high, low = halves(np.concatenate([real_part, imag_part], 0))
    first = np.concatenate([np.concatenate([high, high], 1), np.concatenate([low, np.zeros_like(low)], 1)], 0)
    angle = 2.0 * np.pi * (np.outer(np.arange(128), np.arange(128)) % M) / M
    twist = np.stack([np.cos(angle), -np.sin(angle)]).astype(np.float32)
    angle = 2.0 * np.pi * (np.outer(np.arange(128), np.arange(64)) % 64) / 64
    cosine, sine = np.cos(angle), np.sin(angle)
    last = np.concatenate([np.concatenate([cosine, -sine], 1), np.concatenate([sine, cosine], 1)], 0)
    return first, twist, np.concatenate(halves(last), 1)


def sine_polynomials():
    nodes = 0.25 * np.cos(np.pi * (np.arange(400) + 0.5) / 800)
    square = np.polynomial.chebyshev.Chebyshev.fit(
        nodes**2, np.sin(2 * np.pi * nodes) / nodes, 4, domain=[0, 1 / 16]
    ).convert(kind=np.polynomial.Polynomial, domain=[-1, 1], window=[-1, 1])
    cosine = np.polynomial.chebyshev.Chebyshev.fit(
        nodes**2, np.cos(2 * np.pi * nodes), 4, domain=[0, 1 / 16]
    ).convert(kind=np.polynomial.Polynomial, domain=[-1, 1], window=[-1, 1])
    scale = 2.0**-12
    return (
        [float(c) * scale ** (2 * i + 1) for i, c in enumerate(square.coef)],
        [float(c) * scale ** (2 * i) for i, c in enumerate(cosine.coef)],
    )


SINE, COSINE = sine_polynomials()


def horner(coefficients, value):
    total = jnp.full_like(value, coefficients[-1])
    for coefficient in coefficients[-2::-1]:
        total = total * value + coefficient
    return total


def dot(a, b):
    return jnp.dot(a, b, preferred_element_type=F32)


def draw(bits_0, bits_1, eigen):
    uniform = (bits_0.astype(F32) + 0.5) * 2.0**-12
    square = jnp.log(uniform) * eigen * (-2.0 / (N * M))
    radius = square * lax.rsqrt(square)
    past = bits_1.astype(F32) - 2047.5
    h = jnp.abs(past) - 1024.0
    square = h * h
    value_re = radius * (h * horner(SINE, square))
    value_im = jnp.where(past > 0, -radius, radius) * horner(COSINE, square)
    return value_re, value_im


def add(a, b):
    return a[0] + b[0], a[1] + b[1]


def sub(a, b):
    return a[0] - b[0], a[1] - b[1]


def turn_back(a):
    return a[1], -a[0]


def dft_4(a, b, c, d):
    even, odd = add(a, c), add(b, d)
    less, turned = sub(a, c), turn_back(sub(b, d))
    return add(even, odd), add(less, turned), sub(even, odd), sub(less, turned)


def spin(a, step):
    if step == 0:
        return a
    if step == 4:
        return turn_back(a)
    if step % 4 == 2:
        root = math.sqrt(0.5)
        a = ((a[0] + a[1]) * root, (a[1] - a[0]) * root)
        return a if step == 2 else turn_back(a)
    c, s = math.cos(math.pi * step / 8), math.sin(math.pi * step / 8)
    return a[0] * c + a[1] * s, a[1] * c - a[0] * s


def dft_16(v):
    first = [dft_4(v[e], v[4 + e], v[8 + e], v[12 + e]) for e in range(4)]
    second = [dft_4(*(spin(first[e][s], e * s) for e in range(4))) for s in range(4)]
    return [second[k % 4][k // 4] for k in range(16)]


def front_kernel(noise, eigen, base, turn, out, bits, eig, base_in, tables, values, arrived):
    step = pl.program_id(0)

    def copies():
        for i in range(STEPS):
            columns = slice(BLOCK * i, BLOCK * (i + 1))
            yield pltpu.make_async_copy(noise.at[:, :, columns], bits.at[i], arrived.at[i])
            yield pltpu.make_async_copy(eigen.at[:, columns], eig.at[i], arrived.at[STEPS + i])
        yield pltpu.make_async_copy(base, base_in, arrived.at[2 * STEPS])

    moves = list(copies())

    def start():
        for move in moves:
            move.start()

    def prepare():
        moves[-1].wait()
        for r in range(4):
            cosine = base_in[0, r] * turn[0, r] - base_in[1, r] * turn[1, r]
            sine = base_in[1, r] * turn[0, r] + base_in[0, r] * turn[1, r]
            (cosine, cosine_low), (sine, sine_low) = split(cosine), split(sine)
            for at, c, s in ((0, cosine, sine), (256, cosine, sine), (512, cosine_low, sine_low)):
                tables[r, :128, at : at + 128] = c
                tables[r, :128, at + 128 : at + 256] = s
                tables[r, 128:, at : at + 128] = -s
                tables[r, 128:, at + 128 : at + 256] = c

    def wait(i):
        moves[2 * i].wait()
        moves[2 * i + 1].wait()

    def draws():
        parts = [
            draw(bits[step, 0, at, :], bits[step, 1, at, :], eig[step, at, :])
            for at in (slice(128 * j, 128 * (j + 1)) for j in range(4))
        ]
        for r, value in enumerate(dft_4(*parts)):
            for part in range(2):
                high, low = split(value[part])
                for at, half in ((0, high), (256, low), (512, high)):
                    values[r, at + 128 * part : at + 128 * (part + 1), :] = half

    def multiply():
        for r in range(4):
            both = dot(tables[r], values[r])
            for a in range(BLOCK // 128):
                for row in range(0, 256, 8):
                    part, zl, y, b = row // 128, row // 64 % 2, row // 16 % 4, row // 8 % 2
                    out[a, b, y, zl, part, r] = both[row : row + 8, 128 * a : 128 * (a + 1)]

    @pl.when(step == 0)
    def _():
        start()
        wait(0)
        draws()
        prepare()

    for i in range(1, STEPS):
        pl.when(step == i)(functools.partial(wait, i))

    @pl.when(jnp.logical_and(step > 0, step < STEPS))
    def _():
        multiply()
        draws()

    pl.when(step == STEPS)(multiply)


def front(noise, eigen, turn):
    base = jnp.asarray(column_table())
    in_hbm = pl.BlockSpec(memory_space=pltpu.HBM)
    return pl.pallas_call(
        front_kernel,
        grid=(STEPS + 1,),
        in_specs=[in_hbm] * 3 + [pl.BlockSpec(memory_space=pltpu.VMEM)],
        out_specs=pl.BlockSpec(
            (BLOCK // 128, 2, 4, 2, 2, 4, 8, 128), lambda i: (jnp.maximum(i - 1, 0), 0, 0, 0, 0, 0, 0, 0)
        ),
        out_shape=jax.ShapeDtypeStruct((8, 2, 4, 2, 2, 4, 8, 128), F32),
        scratch_shapes=[
            pltpu.VMEM((STEPS, 2, LOCAL, BLOCK), jnp.int32),
            pltpu.VMEM((STEPS, LOCAL, BLOCK), F32),
            pltpu.VMEM((2, 4, 128, 128), F32),
            pltpu.VMEM((4, 256, 768), BF16),
            pltpu.VMEM((4, 768, BLOCK), BF16),
            pltpu.SemaphoreType.DMA((2 * STEPS + 1,)),
        ],
        compiler_params=pltpu.CompilerParams(vmem_limit_bytes=40 * 2**20),
        cost_estimate=pl.CostEstimate(flops=2 * 10**9, bytes_accessed=12 * 2**20, transcendentals=0),
    )(*(pltpu.with_memory_space_constraint(value, pltpu.HBM) for value in (noise, eigen, base)), turn)


IN_VMEM = pl.BlockSpec(memory_space=pltpu.VMEM)


def middle_kernel(data, out):
    def step(at, carry):
        zl, r = at // 4, at % 4
        for y in range(4):
            values = []
            for e in range(16):
                core, zh, xl, xh = e >> 3, e >> 2 & 1, e >> 1 & 1, e & 1
                index = (2 * xh + xl, zh, core, y, zl)
                values.append((data[*index, 0, r], data[*index, 1, r]))
            for k, value in enumerate(dft_16(values)):
                core, zh, xl, xh = k & 1, k >> 1 & 1, k >> 2 & 1, k >> 3
                place = 4 * (2 * xh + xl) + 2 * zh + core
                row = pl.multiple_of(512 * place + 64 * at, 64)
                for part in range(2):
                    out[pl.ds(row + 2 * y + part, 8, stride=8), :] = value[part]
        return carry

    lax.fori_loop(0, 8, step, 0)


def middle(data):
    return pl.pallas_call(
        middle_kernel,
        in_specs=[IN_VMEM],
        out_specs=IN_VMEM,
        out_shape=jax.ShapeDtypeStruct((8192, 128), F32),
        compiler_params=pltpu.CompilerParams(vmem_limit_bytes=32 * 2**20),
        cost_estimate=pl.CostEstimate(flops=10**7, bytes_accessed=8 * 2**20, transcendentals=0),
    )(data)


def row_kernel(data, first, twist, last, out):
    step = pl.program_id(0)

    def piece(t):
        return data[:, step // 2, :, t % 4, 4 * (step % 2) + t // 4].reshape(128, 128)

    high, low = split(jnp.concatenate([piece(t) for t in range(16)], 1))
    sums = dot(first[...], jnp.concatenate([high, low], 0))
    sums = sums[:128] + sums[128:]
    for t in range(16):
        re, im = sums[:64, 128 * t : 128 * (t + 1)], sums[64:, 128 * t : 128 * (t + 1)]
        both = []
        for v in range(2):
            c, s = twist[0, 64 * v : 64 * (v + 1), :], twist[1, 64 * v : 64 * (v + 1), :]
            both.append(jnp.concatenate([re * c - im * s, re * s + im * c], 1))
        high, low = split(jnp.concatenate(both, 0))
        whole = dot(high, last[...])
        whole = (whole[:, :128] + whole[:, 128:] + dot(low, last[:, :128])).T
        for part in range(2):
            out[part, pl.ds(512 * (t // 8) + t % 8, 64, stride=8), :] = whole[64 * part : 64 * (part + 1)]


def row_transform(data):
    tables = [jnp.asarray(table) for table in row_tables()]
    result = pl.pallas_call(
        row_kernel,
        grid=(4,),
        in_specs=[IN_VMEM] * 4,
        out_specs=pl.BlockSpec((2, 1024, 128), lambda i: (0, i, 0)),
        out_shape=jax.ShapeDtypeStruct((2, 4096, 128), F32),
        compiler_params=pltpu.CompilerParams(vmem_limit_bytes=48 * 2**20),
        cost_estimate=pl.CostEstimate(flops=3 * 10**9, bytes_accessed=9 * 2**20, transcendentals=0),
    )(data.reshape(8, 2, 2, 4, 8, 8, 128), *tables)
    return result.reshape(2, 8, 64, 8, 128).transpose(0, 1, 3, 2, 4).reshape(2, 64, M)


def on_device(noise, eigen):
    x, zh, core = (lax.axis_index(name) for name in AXES[:3])
    anchor = 8 * core + 4 * zh + 2 * (x % 2) + x // 2
    row = 4 * jnp.arange(128, dtype=jnp.int32)[None, :] + jnp.arange(4, dtype=jnp.int32)[:, None]
    angle = (anchor * row).astype(F32) * (2.0 * math.pi / N)
    turn = jnp.broadcast_to(jnp.stack([jnp.cos(angle), jnp.sin(angle)])[..., None], (2, 4, 128, 128))
    with jax.named_scope("columns"):
        data = front(noise, eigen, turn)
    with jax.named_scope("first_exchange"):
        data = lax.all_to_all(data.reshape(64, 2, 2, 32, 128), ("x", "zh", "core", "y"), 0, 0, tiled=True)
    with jax.named_scope("middle"):
        data = middle(data.reshape(4, 2, 2, 4, 2, 2, 4, 8, 128))
    with jax.named_scope("second_exchange"):
        data = lax.all_to_all(data.reshape(32, 256, 128), ("x", "zh", "core", "zl"), 0, 0, tiled=True)
    with jax.named_scope("rows"):
        return row_transform(data)


def solution(mesh):
    fine = Mesh(mesh.devices.reshape(SIZES), AXES)
    col, row = AXES[:3], AXES[3:]
    return jax.shard_map(
        on_device,
        mesh=fine,
        in_specs=(P(None, col, row), P(col, row)),
        out_specs=P(None, AXES, None),
        check_vma=False,
    )
```

```python
import functools
import math

import jax
import jax.numpy as jnp
import ml_dtypes
import numpy as np
from jax import lax
from jax.experimental import pallas as pl
from jax.experimental.pallas import tpu as pltpu
from jax.sharding import Mesh, PartitionSpec as P

N = 8192
M = 8192
LOCAL = 512
WIDTH = 1024
BLOCK = 256
STEPS = WIDTH // BLOCK // 2

AXES = ("x", "zh", "core", "zl", "y")
SIZES = (4, 2, 2, 2, 4)

F32 = jnp.float32
BF16 = jnp.bfloat16


def halves(table):
    high = table.astype(np.float32).astype(ml_dtypes.bfloat16)
    low = (table - high.astype(np.float64)).astype(np.float32).astype(ml_dtypes.bfloat16)
    return high, low


def split(value):
    high = value.astype(BF16)
    low = (value - high.astype(F32)).astype(BF16)
    return high, low


def column_table():
    row = 4 * np.arange(128)[None, :, None] + np.arange(4)[:, None, None]
    angle = 2.0 * np.pi * (row * np.arange(128) % LOCAL) / LOCAL
    return np.stack([np.cos(angle), np.sin(angle)]).astype(np.float32)


def row_tables():
    place = 8 * (4 * np.arange(2)[None, :, None] + np.arange(4)[None, None, :]) + np.arange(8)[:, None, None]
    angle = 2.0 * np.pi * (np.arange(64)[:, None] * place.reshape(1, 64) % 64) / 64
    cosine, sine = np.cos(angle), np.sin(angle)
    real_part = np.stack([cosine, sine], -1).reshape(64, 128)
    imag_part = np.stack([-sine, cosine], -1).reshape(64, 128)
    high, low = halves(np.concatenate([real_part, imag_part], 0))
    first = np.concatenate([np.concatenate([high, high], 1), np.concatenate([low, np.zeros_like(low)], 1)], 0)
    angle = 2.0 * np.pi * (np.outer(np.arange(128), np.arange(128)) % M) / M
    twist = np.stack([np.cos(angle), -np.sin(angle)]).astype(np.float32)
    angle = 2.0 * np.pi * (np.outer(np.arange(128), np.arange(64)) % 64) / 64
    cosine, sine = np.cos(angle), np.sin(angle)
    last = np.concatenate([np.concatenate([cosine, -sine], 1), np.concatenate([sine, cosine], 1)], 0)
    return first, twist, np.concatenate(halves(last), 1)


def sine_polynomials():
    nodes = 0.25 * np.cos(np.pi * (np.arange(400) + 0.5) / 800)
    square = np.polynomial.chebyshev.Chebyshev.fit(
        nodes**2, np.sin(2 * np.pi * nodes) / nodes, 4, domain=[0, 1 / 16]
    ).convert(kind=np.polynomial.Polynomial, domain=[-1, 1], window=[-1, 1])
    cosine = np.polynomial.chebyshev.Chebyshev.fit(
        nodes**2, np.cos(2 * np.pi * nodes), 4, domain=[0, 1 / 16]
    ).convert(kind=np.polynomial.Polynomial, domain=[-1, 1], window=[-1, 1])
    scale = 2.0**-12
    return (
        [float(c) * scale ** (2 * i + 1) for i, c in enumerate(square.coef)],
        [float(c) * scale ** (2 * i) for i, c in enumerate(cosine.coef)],
    )


SINE, COSINE = sine_polynomials()


def horner(coefficients, value):
    total = jnp.full_like(value, coefficients[-1])
    for coefficient in coefficients[-2::-1]:
        total = total * value + coefficient
    return total


def dot(a, b):
    return jnp.dot(a, b, preferred_element_type=F32)


def draw(bits_0, bits_1, eigen):
    uniform = (bits_0.astype(F32) + 0.5) * 2.0**-12
    square = jnp.log(uniform) * eigen * (-2.0 / (N * M))
    radius = square * lax.rsqrt(square)
    past = bits_1.astype(F32) - 2047.5
    h = jnp.abs(past) - 1024.0
    square = h * h
    value_re = radius * (h * horner(SINE, square))
    value_im = jnp.where(past > 0, -radius, radius) * horner(COSINE, square)
    return value_re, value_im


def add(a, b):
    return a[0] + b[0], a[1] + b[1]


def sub(a, b):
    return a[0] - b[0], a[1] - b[1]


def turn_back(a):
    return a[1], -a[0]


def dft_4(a, b, c, d):
    even, odd = add(a, c), add(b, d)
    less, turned = sub(a, c), turn_back(sub(b, d))
    return add(even, odd), add(less, turned), sub(even, odd), sub(less, turned)


ROOT = math.sqrt(0.5)


def dft_8(v):
    even = dft_4(v[0], v[2], v[4], v[6])
    odd = dft_4(v[1], v[3], v[5], v[7])
    spun = [
        odd[0],
        ((odd[1][0] + odd[1][1]) * ROOT, (odd[1][1] - odd[1][0]) * ROOT),
        turn_back(odd[2]),
        ((odd[3][1] - odd[3][0]) * ROOT, (odd[3][0] + odd[3][1]) * -ROOT),
    ]
    return [add(e, o) for e, o in zip(even, spun)] + [sub(e, o) for e, o in zip(even, spun)]


def draws(bits, eig, block, values):
    parts = [
        draw(bits[block, 0, at, :], bits[block, 1, at, :], eig[block, at, :])
        for at in (slice(128 * j, 128 * (j + 1)) for j in range(4))
    ]
    for r, value in enumerate(dft_4(*parts)):
        for part in range(2):
            high, low = split(value[part])
            for at, half in ((0, high), (256, low), (512, high)):
                values[r, at + 128 * part : at + 128 * (part + 1), :] = half


def multiply(tables, values, out):
    for r in range(4):
        both = dot(tables[r], values[r])
        for a in range(BLOCK // 128):
            for row in range(0, 256, 8):
                part, zl, y, t = row // 128, row // 64 % 2, row // 16 % 4, row % 16
                out[a, y, zl, part, r, t : t + 8] = both[row : row + 8, 128 * a : 128 * (a + 1)]


def blocks(step, arrive, bits, eig, tables, values, out):
    @pl.when(step == 0)
    def _():
        arrive(0)
        draws(bits, eig, 0, values)

    for i in range(1, STEPS):
        pl.when(step == i)(functools.partial(arrive, i))

    @pl.when(jnp.logical_and(step > 0, step < STEPS))
    def _():
        multiply(tables, values, out)
        draws(bits, eig, step, values)

    pl.when(step == STEPS)(functools.partial(multiply, tables, values, out))


def first_half_kernel(noise, eigen, base, turn, out, tables, bits_left, eig_left, bits, eig, base_in, values, arrived):
    step = pl.program_id(0)
    moves = []
    for i in range(2 * STEPS):
        columns = slice(BLOCK * i, BLOCK * (i + 1))
        to = (bits.at[i], eig.at[i]) if i < STEPS else (bits_left.at[i - STEPS], eig_left.at[i - STEPS])
        moves.append(pltpu.make_async_copy(noise.at[:, :, columns], to[0], arrived.at[2 * i]))
        moves.append(pltpu.make_async_copy(eigen.at[:, columns], to[1], arrived.at[2 * i + 1]))
    moves.insert(2, pltpu.make_async_copy(base, base_in, arrived.at[4 * STEPS]))

    @pl.when(step == 0)
    def _():
        for move in moves:
            move.start()
        moves[2].wait()
        for r in range(4):
            cosine = base_in[0, r] * turn[0, r] - base_in[1, r] * turn[1, r]
            sine = base_in[1, r] * turn[0, r] + base_in[0, r] * turn[1, r]
            (cosine, cosine_low), (sine, sine_low) = split(cosine), split(sine)
            for at, c, s in ((0, cosine, sine), (256, cosine, sine), (512, cosine_low, sine_low)):
                tables[r, :128, at : at + 128] = c
                tables[r, :128, at + 128 : at + 256] = s
                tables[r, 128:, at : at + 128] = -s
                tables[r, 128:, at + 128 : at + 256] = c

    def arrive(i):
        for move in moves[:2] if i == 0 else moves[2 * i + 1 : 2 * i + 3]:
            move.wait()

    blocks(step, arrive, bits, eig, tables, values, out)

    @pl.when(step == STEPS)
    def _():
        for move in moves[2 * STEPS + 1 :]:
            move.wait()


def second_half_kernel(bits, eig, tables, out, values):
    blocks(pl.program_id(0), lambda i: None, bits, eig, tables, values, out)


IN_VMEM = pl.BlockSpec(memory_space=pltpu.VMEM)
HALF_OUT = pl.BlockSpec((BLOCK // 128, 4, 2, 2, 4, 16, 128), lambda i: (jnp.maximum(i - 1, 0), 0, 0, 0, 0, 0, 0))
HALF_SHAPE = jax.ShapeDtypeStruct((4, 4, 2, 2, 4, 16, 128), F32)
VALUES = pltpu.VMEM((4, 768, BLOCK), BF16)


def first_half(noise, eigen, turn):
    base = jnp.asarray(column_table())
    bits, eig = (STEPS, 2, LOCAL, BLOCK), (STEPS, LOCAL, BLOCK)
    return pl.pallas_call(
        first_half_kernel,
        grid=(STEPS + 1,),
        in_specs=[pl.BlockSpec(memory_space=pltpu.HBM)] * 3 + [IN_VMEM],
        out_specs=[HALF_OUT] + [IN_VMEM] * 3,
        out_shape=[
            HALF_SHAPE,
            jax.ShapeDtypeStruct((4, 256, 768), BF16),
            jax.ShapeDtypeStruct(bits, jnp.int32),
            jax.ShapeDtypeStruct(eig, F32),
        ],
        scratch_shapes=[
            pltpu.VMEM(bits, jnp.int32),
            pltpu.VMEM(eig, F32),
            pltpu.VMEM((2, 4, 128, 128), F32),
            VALUES,
            pltpu.SemaphoreType.DMA((4 * STEPS + 1,)),
        ],
        compiler_params=pltpu.CompilerParams(vmem_limit_bytes=40 * 2**20),
        cost_estimate=pl.CostEstimate(flops=10**9, bytes_accessed=12 * 2**20, transcendentals=0),
    )(*(pltpu.with_memory_space_constraint(value, pltpu.HBM) for value in (noise, eigen, base)), turn)


def second_half(bits, eig, tables):
    return pl.pallas_call(
        second_half_kernel,
        grid=(STEPS + 1,),
        in_specs=[IN_VMEM] * 3,
        out_specs=HALF_OUT,
        out_shape=HALF_SHAPE,
        scratch_shapes=[VALUES],
        compiler_params=pltpu.CompilerParams(vmem_limit_bytes=40 * 2**20),
        cost_estimate=pl.CostEstimate(flops=10**9, bytes_accessed=8 * 2**20, transcendentals=0),
    )(bits, eig, tables)


def middle_kernel(scalars, data, out):
    def step(at, carry):
        zl, r = at // 4, at % 4
        for half in range(2):
            line = slice(8 * half, 8 * half + 8)
            for y in range(4):
                values = []
                for e in range(8):
                    zh, xl, xh = e >> 2, e >> 1 & 1, e & 1
                    index = (2 * xh + xl, zh, y, zl)
                    re, im = data[*index, 0, r, line], data[*index, 1, r, line]
                    c, s = scalars[2 * e], scalars[2 * e + 1]
                    values.append((re * c - im * s, re * s + im * c) if e else (re, im))
                for k, value in enumerate(dft_8(values)):
                    zh, xl, xh = k & 1, k >> 1 & 1, k >> 2
                    place = 2 * (2 * xh + xl) + zh
                    row = pl.multiple_of(1024 * place + 128 * at, 128) + 64 * half
                    for part in range(2):
                        out[pl.ds(row + 2 * y + part, 8, stride=8), :] = value[part]
        return carry

    lax.fori_loop(0, 8, step, 0)


def middle(scalars, data):
    return pl.pallas_call(
        middle_kernel,
        in_specs=[pl.BlockSpec(memory_space=pltpu.SMEM), IN_VMEM],
        out_specs=IN_VMEM,
        out_shape=jax.ShapeDtypeStruct((8192, 128), F32),
        compiler_params=pltpu.CompilerParams(vmem_limit_bytes=32 * 2**20),
        cost_estimate=pl.CostEstimate(flops=10**7, bytes_accessed=8 * 2**20, transcendentals=0),
    )(scalars, data)


def row_kernel(data, first, twist, last, out):
    step = pl.program_id(0)

    def piece(t):
        return data[:, :, t % 4, 4 * step + t // 4].reshape(128, 128)

    high, low = split(jnp.concatenate([piece(t) for t in range(16)], 1))
    sums = dot(first[...], jnp.concatenate([high, low], 0))
    sums = sums[:128] + sums[128:]
    for t in range(16):
        re, im = sums[:64, 128 * t : 128 * (t + 1)], sums[64:, 128 * t : 128 * (t + 1)]
        both = []
        for v in range(2):
            c, s = twist[0, 64 * v : 64 * (v + 1), :], twist[1, 64 * v : 64 * (v + 1), :]
            both.append(jnp.concatenate([re * c - im * s, re * s + im * c], 1))
        high, low = split(jnp.concatenate(both, 0))
        whole = dot(high, last[...])
        whole = (whole[:, :128] + whole[:, 128:] + dot(low, last[:, :128])).T
        for part in range(2):
            out[part, pl.ds(512 * (t // 8) + t % 8, 64, stride=8), :] = whole[64 * part : 64 * (part + 1)]


def row_transform(data):
    tables = [jnp.asarray(table) for table in row_tables()]
    result = pl.pallas_call(
        row_kernel,
        grid=(4,),
        in_specs=[IN_VMEM] * 4,
        out_specs=pl.BlockSpec((2, 1024, 128), lambda i: (0, i, 0)),
        out_shape=jax.ShapeDtypeStruct((2, 4096, 128), F32),
        compiler_params=pltpu.CompilerParams(vmem_limit_bytes=48 * 2**20),
        cost_estimate=pl.CostEstimate(flops=3 * 10**9, bytes_accessed=9 * 2**20, transcendentals=0),
    )(data.reshape(8, 2, 4, 16, 8, 128), *tables)
    return result.reshape(2, 8, 64, 8, 128).transpose(0, 1, 3, 2, 4).reshape(2, 64, M)


def on_device(noise, eigen):
    x, zh, core = (lax.axis_index(name) for name in AXES[:3])
    anchor = 8 * core + 4 * zh + 2 * (x % 2) + x // 2
    row = 4 * jnp.arange(128, dtype=jnp.int32)[None, :] + jnp.arange(4, dtype=jnp.int32)[:, None]
    angle = (anchor * row).astype(F32) * (2.0 * math.pi / N)
    turn = jnp.broadcast_to(jnp.stack([jnp.cos(angle), jnp.sin(angle)])[..., None], (2, 4, 128, 128))
    angle = (core * jnp.arange(8, dtype=jnp.int32)).astype(F32) * (-2.0 * math.pi / 16)
    scalars = jnp.stack([jnp.cos(angle), jnp.sin(angle)], 1).reshape(16)
    sign = (1 - 2 * core).astype(F32)
    swap = lambda value: lax.ppermute(value, "core", [(0, 1), (1, 0)])
    with jax.named_scope("columns"):
        data, tables, bits, eig = first_half(noise, eigen, turn)
        other = swap(data)
        data_2 = second_half(bits, eig, tables)
        other_2 = swap(data_2)
    with jax.named_scope("cores"):
        data = jnp.concatenate([data * sign + other, data_2 * sign + other_2])
    with jax.named_scope("first_exchange"):
        data = lax.all_to_all(data.reshape(32, 256, 128), ("x", "zh", "y"), 0, 0, tiled=True)
    with jax.named_scope("middle"):
        data = middle(scalars, data.reshape(4, 2, 4, 2, 2, 4, 16, 128))
    with jax.named_scope("second_exchange"):
        data = lax.all_to_all(data.reshape(16, 512, 128), ("x", "zh", "zl"), 0, 0, tiled=True)
    with jax.named_scope("rows"):
        return row_transform(data)


def solution(mesh):
    fine = Mesh(mesh.devices.reshape(SIZES), AXES)
    col, row = AXES[:3], AXES[3:]
    return jax.shard_map(
        on_device,
        mesh=fine,
        in_specs=(P(None, col, row), P(col, row)),
        out_specs=P(None, AXES, None),
        check_vma=False,
    )
```

```python
import functools
import math

import jax
import jax.numpy as jnp
import ml_dtypes
import numpy as np
from jax import lax
from jax.experimental import pallas as pl
from jax.experimental.pallas import tpu as pltpu
from jax.sharding import Mesh, PartitionSpec as P

N = 8192
M = 8192
LOCAL = 512
WIDTH = 1024
BLOCK = 256
STEPS = WIDTH // BLOCK // 2

AXES = ("x", "zh", "core", "zl", "y")
SIZES = (4, 2, 2, 2, 4)

F32 = jnp.float32
BF16 = jnp.bfloat16


def halves(table):
    high = table.astype(np.float32).astype(ml_dtypes.bfloat16)
    low = (table - high.astype(np.float64)).astype(np.float32).astype(ml_dtypes.bfloat16)
    return high, low


def split(value):
    high = value.astype(BF16)
    low = (value - high.astype(F32)).astype(BF16)
    return high, low


def column_table():
    row = 4 * np.arange(128)[None, :, None] + np.arange(4)[:, None, None]
    angle = 2.0 * np.pi * (row * np.arange(128) % LOCAL) / LOCAL
    return np.stack([np.cos(angle), np.sin(angle)]).astype(np.float32)


def row_tables():
    place = 8 * (4 * np.arange(2)[None, :, None] + np.arange(4)[None, None, :]) + np.arange(8)[:, None, None]
    angle = 2.0 * np.pi * (np.arange(64)[:, None] * place.reshape(1, 64) % 64) / 64
    cosine, sine = np.cos(angle), np.sin(angle)
    real_part = np.stack([cosine, sine], -1).reshape(64, 128)
    imag_part = np.stack([-sine, cosine], -1).reshape(64, 128)
    high, low = halves(np.concatenate([real_part, imag_part], 0))
    first = np.concatenate([np.concatenate([high, high], 1), np.concatenate([low, np.zeros_like(low)], 1)], 0)
    angle = 2.0 * np.pi * (np.outer(np.arange(128), np.arange(128)) % M) / M
    twist = np.stack([np.cos(angle), -np.sin(angle)]).astype(np.float32)
    angle = 2.0 * np.pi * (np.outer(np.arange(128), np.arange(64)) % 64) / 64
    cosine, sine = np.cos(angle), np.sin(angle)
    last = np.concatenate([np.concatenate([cosine, -sine], 1), np.concatenate([sine, cosine], 1)], 0)
    return first, twist, np.concatenate(halves(last), 1)


def sine_polynomials():
    nodes = 0.25 * np.cos(np.pi * (np.arange(400) + 0.5) / 800)
    square = np.polynomial.chebyshev.Chebyshev.fit(
        nodes**2, np.sin(2 * np.pi * nodes) / nodes, 4, domain=[0, 1 / 16]
    ).convert(kind=np.polynomial.Polynomial, domain=[-1, 1], window=[-1, 1])
    cosine = np.polynomial.chebyshev.Chebyshev.fit(
        nodes**2, np.cos(2 * np.pi * nodes), 4, domain=[0, 1 / 16]
    ).convert(kind=np.polynomial.Polynomial, domain=[-1, 1], window=[-1, 1])
    scale = 2.0**-12
    return (
        [float(c) * scale ** (2 * i + 1) for i, c in enumerate(square.coef)],
        [float(c) * scale ** (2 * i) for i, c in enumerate(cosine.coef)],
    )


SINE, COSINE = sine_polynomials()


def horner(coefficients, value):
    total = jnp.full_like(value, coefficients[-1])
    for coefficient in coefficients[-2::-1]:
        total = total * value + coefficient
    return total


def dot(a, b):
    return jnp.dot(a, b, preferred_element_type=F32)


def draw(bits_0, bits_1, eigen):
    uniform = (bits_0.astype(F32) + 0.5) * 2.0**-12
    square = jnp.log(uniform) * eigen * (-2.0 / (N * M))
    radius = square * lax.rsqrt(square)
    past = bits_1.astype(F32) - 2047.5
    h = jnp.abs(past) - 1024.0
    square = h * h
    value_re = radius * (h * horner(SINE, square))
    value_im = jnp.where(past > 0, -radius, radius) * horner(COSINE, square)
    return value_re, value_im


def add(a, b):
    return a[0] + b[0], a[1] + b[1]


def sub(a, b):
    return a[0] - b[0], a[1] - b[1]


def turn_back(a):
    return a[1], -a[0]


def dft_4(a, b, c, d):
    even, odd = add(a, c), add(b, d)
    less, turned = sub(a, c), turn_back(sub(b, d))
    return add(even, odd), add(less, turned), sub(even, odd), sub(less, turned)


ROOT = math.sqrt(0.5)


def dft_8(v):
    even = dft_4(v[0], v[2], v[4], v[6])
    odd = dft_4(v[1], v[3], v[5], v[7])
    spun = [
        odd[0],
        ((odd[1][0] + odd[1][1]) * ROOT, (odd[1][1] - odd[1][0]) * ROOT),
        turn_back(odd[2]),
        ((odd[3][1] - odd[3][0]) * ROOT, (odd[3][0] + odd[3][1]) * -ROOT),
    ]
    return [add(e, o) for e, o in zip(even, spun)] + [sub(e, o) for e, o in zip(even, spun)]


def draws(bits, eig, block, values):
    parts = [
        draw(bits[block, 0, at, :], bits[block, 1, at, :], eig[block, at, :])
        for at in (slice(128 * j, 128 * (j + 1)) for j in range(4))
    ]
    for r, value in enumerate(dft_4(*parts)):
        for part in range(2):
            high, low = split(value[part])
            for at, half in ((0, high), (256, low), (512, high)):
                values[r, at + 128 * part : at + 128 * (part + 1), :] = half


def multiply(tables, values, out):
    for r in range(4):
        both = dot(tables[r], values[r])
        for a in range(BLOCK // 128):
            for row in range(0, 256, 8):
                part, zl, y, t = row // 128, row // 64 % 2, row // 16 % 4, row % 16
                out[a, y, zl, part, r, t : t + 8] = both[row : row + 8, 128 * a : 128 * (a + 1)]


def blocks(step, arrive, bits, eig, tables, values, out):
    @pl.when(step == 0)
    def _():
        arrive(0)
        draws(bits, eig, 0, values)

    for i in range(1, STEPS):
        pl.when(step == i)(functools.partial(arrive, i))

    @pl.when(jnp.logical_and(step > 0, step < STEPS))
    def _():
        multiply(tables, values, out)
        draws(bits, eig, step, values)

    pl.when(step == STEPS)(functools.partial(multiply, tables, values, out))


def first_half_kernel(noise, eigen, base, turn, out, tables, bits_left, eig_left, bits, eig, base_in, values, arrived):
    step = pl.program_id(0)
    moves = []
    for i in range(2 * STEPS):
        columns = slice(BLOCK * i, BLOCK * (i + 1))
        to = (bits.at[i], eig.at[i]) if i < STEPS else (bits_left.at[i - STEPS], eig_left.at[i - STEPS])
        moves.append(pltpu.make_async_copy(noise.at[:, :, columns], to[0], arrived.at[2 * i]))
        moves.append(pltpu.make_async_copy(eigen.at[:, columns], to[1], arrived.at[2 * i + 1]))
    moves.insert(2, pltpu.make_async_copy(base, base_in, arrived.at[4 * STEPS]))

    @pl.when(step == 0)
    def _():
        for move in moves:
            move.start()
        moves[2].wait()
        for r in range(4):
            cosine = base_in[0, r] * turn[0, r] - base_in[1, r] * turn[1, r]
            sine = base_in[1, r] * turn[0, r] + base_in[0, r] * turn[1, r]
            (cosine, cosine_low), (sine, sine_low) = split(cosine), split(sine)
            for at, c, s in ((0, cosine, sine), (256, cosine, sine), (512, cosine_low, sine_low)):
                tables[r, :128, at : at + 128] = c
                tables[r, :128, at + 128 : at + 256] = s
                tables[r, 128:, at : at + 128] = -s
                tables[r, 128:, at + 128 : at + 256] = c

    def arrive(i):
        for move in moves[:2] if i == 0 else moves[2 * i + 1 : 2 * i + 3]:
            move.wait()

    blocks(step, arrive, bits, eig, tables, values, out)

    @pl.when(step == STEPS)
    def _():
        for move in moves[2 * STEPS + 1 :]:
            move.wait()


def second_half_kernel(bits, eig, tables, out, values):
    blocks(pl.program_id(0), lambda i: None, bits, eig, tables, values, out)


IN_VMEM = pl.BlockSpec(memory_space=pltpu.VMEM)
HALF_OUT = pl.BlockSpec((BLOCK // 128, 4, 2, 2, 4, 16, 128), lambda i: (jnp.maximum(i - 1, 0), 0, 0, 0, 0, 0, 0))
HALF_SHAPE = jax.ShapeDtypeStruct((4, 4, 2, 2, 4, 16, 128), F32)
VALUES = pltpu.VMEM((4, 768, BLOCK), BF16)


def first_half(noise, eigen, turn):
    base = jnp.asarray(column_table())
    bits, eig = (STEPS, 2, LOCAL, BLOCK), (STEPS, LOCAL, BLOCK)
    return pl.pallas_call(
        first_half_kernel,
        grid=(STEPS + 1,),
        in_specs=[pl.BlockSpec(memory_space=pltpu.HBM)] * 3 + [IN_VMEM],
        out_specs=[HALF_OUT] + [IN_VMEM] * 3,
        out_shape=[
            HALF_SHAPE,
            jax.ShapeDtypeStruct((4, 256, 768), BF16),
            jax.ShapeDtypeStruct(bits, jnp.int32),
            jax.ShapeDtypeStruct(eig, F32),
        ],
        scratch_shapes=[
            pltpu.VMEM(bits, jnp.int32),
            pltpu.VMEM(eig, F32),
            pltpu.VMEM((2, 4, 128, 128), F32),
            VALUES,
            pltpu.SemaphoreType.DMA((4 * STEPS + 1,)),
        ],
        compiler_params=pltpu.CompilerParams(vmem_limit_bytes=16 * 2**20),
        cost_estimate=pl.CostEstimate(flops=10**9, bytes_accessed=12 * 2**20, transcendentals=0),
    )(*(pltpu.with_memory_space_constraint(value, pltpu.HBM) for value in (noise, eigen, base)), turn)


def second_half(bits, eig, tables):
    return pl.pallas_call(
        second_half_kernel,
        grid=(STEPS + 1,),
        in_specs=[IN_VMEM] * 3,
        out_specs=HALF_OUT,
        out_shape=HALF_SHAPE,
        scratch_shapes=[VALUES],
        compiler_params=pltpu.CompilerParams(vmem_limit_bytes=10 * 2**20),
        cost_estimate=pl.CostEstimate(flops=2 * 10**10, bytes_accessed=8 * 2**20, transcendentals=0),
    )(bits, eig, tables)


def cores_kernel(half, sign, mine, other, *refs):
    out = refs[-1]

    def step(i, carry):
        at = pl.ds(pl.multiple_of(128 * i, 128), 128)
        out[half, at, :] = mine[at, :] * sign[0] + other[at, :]
        return carry

    lax.fori_loop(0, 32, step, 0)


def add_cores(half, result, sign, mine, other):
    operands = [sign, mine.reshape(4096, 128), other.reshape(4096, 128)]
    return pl.pallas_call(
        functools.partial(cores_kernel, half),
        in_specs=[pl.BlockSpec(memory_space=pltpu.SMEM)] + [IN_VMEM] * (2 + half),
        out_specs=IN_VMEM,
        out_shape=jax.ShapeDtypeStruct((2, 4096, 128), F32),
        input_output_aliases={3: 0} if half else {},
        compiler_params=pltpu.CompilerParams(vmem_limit_bytes=8 * 2**20),
        cost_estimate=pl.CostEstimate(flops=10**6, bytes_accessed=6 * 2**20, transcendentals=0),
    )(*operands, *([result] * half))


def middle_kernel(scalars, data, out):
    def step(at, carry):
        zl, r = at // 4, at % 4
        for half in range(2):
            line = slice(8 * half, 8 * half + 8)
            for y in range(4):
                values = []
                for e in range(8):
                    zh, xl, xh = e >> 2, e >> 1 & 1, e & 1
                    index = (2 * xh + xl, zh, y, zl)
                    re, im = data[*index, 0, r, line], data[*index, 1, r, line]
                    c, s = scalars[2 * e], scalars[2 * e + 1]
                    values.append((re * c - im * s, re * s + im * c) if e else (re, im))
                for k, value in enumerate(dft_8(values)):
                    zh, xl, xh = k & 1, k >> 1 & 1, k >> 2
                    place = 2 * (2 * xh + xl) + zh
                    row = pl.multiple_of(1024 * place + 128 * at, 128) + 64 * half
                    for part in range(2):
                        out[pl.ds(row + 2 * y + part, 8, stride=8), :] = value[part]
        return carry

    lax.fori_loop(0, 8, step, 0)


def middle(scalars, data):
    return pl.pallas_call(
        middle_kernel,
        in_specs=[pl.BlockSpec(memory_space=pltpu.SMEM), IN_VMEM],
        out_specs=IN_VMEM,
        out_shape=jax.ShapeDtypeStruct((8192, 128), F32),
        compiler_params=pltpu.CompilerParams(vmem_limit_bytes=6 * 2**20),
        cost_estimate=pl.CostEstimate(flops=10**7, bytes_accessed=8 * 2**20, transcendentals=0),
    )(scalars, data)


def row_kernel(data, first, twist, last, out):
    step = pl.program_id(0)

    def piece(t):
        return data[:, :, t % 4, 4 * step + t // 4].reshape(128, 128)

    high, low = split(jnp.concatenate([piece(t) for t in range(16)], 1))
    sums = dot(first[...], jnp.concatenate([high, low], 0))
    sums = sums[:128] + sums[128:]
    for t in range(16):
        re, im = sums[:64, 128 * t : 128 * (t + 1)], sums[64:, 128 * t : 128 * (t + 1)]
        both = []
        for v in range(2):
            c, s = twist[0, 64 * v : 64 * (v + 1), :], twist[1, 64 * v : 64 * (v + 1), :]
            both.append(jnp.concatenate([re * c - im * s, re * s + im * c], 1))
        high, low = split(jnp.concatenate(both, 0))
        whole = dot(high, last[...])
        whole = (whole[:, :128] + whole[:, 128:] + dot(low, last[:, :128])).T
        for part in range(2):
            out[part, pl.ds(512 * (t // 8) + t % 8, 64, stride=8), :] = whole[64 * part : 64 * (part + 1)]


def row_transform(data):
    tables = [jnp.asarray(table) for table in row_tables()]
    result = pl.pallas_call(
        row_kernel,
        grid=(4,),
        in_specs=[IN_VMEM] * 4,
        out_specs=pl.BlockSpec((2, 1024, 128), lambda i: (0, i, 0)),
        out_shape=jax.ShapeDtypeStruct((2, 4096, 128), F32),
        compiler_params=pltpu.CompilerParams(vmem_limit_bytes=16 * 2**20),
        cost_estimate=pl.CostEstimate(flops=3 * 10**9, bytes_accessed=9 * 2**20, transcendentals=0),
    )(data.reshape(8, 2, 4, 16, 8, 128), *tables)
    return result.reshape(2, 8, 64, 8, 128).transpose(0, 1, 3, 2, 4).reshape(2, 64, M)


def on_device(noise, eigen):
    x, zh, core = (lax.axis_index(name) for name in AXES[:3])
    anchor = 8 * core + 4 * zh + 2 * (x % 2) + x // 2
    row = 4 * jnp.arange(128, dtype=jnp.int32)[None, :] + jnp.arange(4, dtype=jnp.int32)[:, None]
    angle = (anchor * row).astype(F32) * (2.0 * math.pi / N)
    turn = jnp.broadcast_to(jnp.stack([jnp.cos(angle), jnp.sin(angle)])[..., None], (2, 4, 128, 128))
    angle = (core * jnp.arange(8, dtype=jnp.int32)).astype(F32) * (-2.0 * math.pi / 16)
    scalars = jnp.stack([jnp.cos(angle), jnp.sin(angle)], 1).reshape(16)
    sign = (1 - 2 * core).astype(F32).reshape(1)
    swap = lambda value: lax.ppermute(value, "core", [(0, 1), (1, 0)])
    with jax.named_scope("columns"):
        data, tables, bits, eig = first_half(noise, eigen, turn)
        other = swap(data)
        data_2 = second_half(bits, eig, tables)
        other_2 = swap(data_2)
    with jax.named_scope("cores"):
        data = add_cores(0, None, sign, data, other)
        data = add_cores(1, data, sign, data_2, other_2)
    with jax.named_scope("first_exchange"):
        data, scalars = lax.optimization_barrier((data, scalars))
        data = lax.all_to_all(data.reshape(32, 256, 128), ("x", "zh", "y"), 0, 0, tiled=True)
    with jax.named_scope("middle"):
        data = middle(scalars, data.reshape(4, 2, 4, 2, 2, 4, 16, 128))
    with jax.named_scope("second_exchange"):
        data = lax.all_to_all(data.reshape(16, 512, 128), ("x", "zh", "zl"), 0, 0, tiled=True)
    with jax.named_scope("rows"):
        return row_transform(data)


def solution(mesh):
    fine = Mesh(mesh.devices.reshape(SIZES), AXES)
    col, row = AXES[:3], AXES[3:]
    return jax.shard_map(
        on_device,
        mesh=fine,
        in_specs=(P(None, col, row), P(col, row)),
        out_specs=P(None, AXES, None),
        check_vma=False,
    )
```

```python
import functools
import math

import jax
import jax.numpy as jnp
import ml_dtypes
import numpy as np
from jax import lax
from jax.experimental import pallas as pl
from jax.experimental.pallas import tpu as pltpu
from jax.sharding import Mesh, PartitionSpec as P

N = 8192
M = 8192
LOCAL = 512
WIDTH = 1024
BLOCK = 256
STEPS = WIDTH // BLOCK

AXES = ("x", "zh", "core", "zl", "y")
SIZES = (4, 2, 2, 2, 4)

F32 = jnp.float32
BF16 = jnp.bfloat16


def halves(table):
    high = table.astype(np.float32).astype(ml_dtypes.bfloat16)
    low = (table - high.astype(np.float64)).astype(np.float32).astype(ml_dtypes.bfloat16)
    return high, low


def split(value):
    high = value.astype(BF16)
    low = (value - high.astype(F32)).astype(BF16)
    return high, low


def column_table():
    row = 4 * np.arange(128)[None, :, None] + np.arange(4)[:, None, None]
    angle = 2.0 * np.pi * (row * np.arange(128) % LOCAL) / LOCAL
    return np.stack([np.cos(angle), np.sin(angle)]).astype(np.float32)


def row_tables():
    place = 8 * (4 * np.arange(2)[None, :, None] + np.arange(4)[None, None, :])
    place = place + np.array([0, 2, 4, 6, 1, 3, 5, 7])[:, None, None]
    angle = 2.0 * np.pi * (np.arange(64)[:, None] * place.reshape(1, 64) % 64) / 64
    cosine, sine = np.cos(angle), np.sin(angle)
    real_part = np.stack([cosine, sine], -1).reshape(64, 128)
    imag_part = np.stack([-sine, cosine], -1).reshape(64, 128)
    high, low = halves(np.concatenate([real_part, imag_part], 0))
    first = np.concatenate([np.concatenate([high, high], 1), np.concatenate([low, np.zeros_like(low)], 1)], 0)
    angle = 2.0 * np.pi * (np.outer(np.arange(128), np.arange(128)) % M) / M
    twist = np.stack([np.cos(angle), -np.sin(angle)]).astype(np.float32)
    angle = 2.0 * np.pi * (np.outer(np.arange(128), np.arange(64)) % 64) / 64
    cosine, sine = np.cos(angle), np.sin(angle)
    last = np.concatenate([np.concatenate([cosine, -sine], 1), np.concatenate([sine, cosine], 1)], 0)
    return first, twist, np.concatenate(halves(last), 1)


def sine_polynomials():
    nodes = 0.25 * np.cos(np.pi * (np.arange(400) + 0.5) / 800)
    square = np.polynomial.chebyshev.Chebyshev.fit(
        nodes**2, np.sin(2 * np.pi * nodes) / nodes, 4, domain=[0, 1 / 16]
    ).convert(kind=np.polynomial.Polynomial, domain=[-1, 1], window=[-1, 1])
    cosine = np.polynomial.chebyshev.Chebyshev.fit(
        nodes**2, np.cos(2 * np.pi * nodes), 4, domain=[0, 1 / 16]
    ).convert(kind=np.polynomial.Polynomial, domain=[-1, 1], window=[-1, 1])
    scale = 2.0**-12
    return (
        [float(c) * scale ** (2 * i + 1) for i, c in enumerate(square.coef)],
        [float(c) * scale ** (2 * i) for i, c in enumerate(cosine.coef)],
    )


SINE, COSINE = sine_polynomials()


def horner(coefficients, value):
    total = jnp.full_like(value, coefficients[-1])
    for coefficient in coefficients[-2::-1]:
        total = total * value + coefficient
    return total


def dot(a, b):
    return jnp.dot(a, b, preferred_element_type=F32)


def draw(bits_0, bits_1, eigen):
    uniform = (bits_0.astype(F32) + 0.5) * 2.0**-12
    square = jnp.log(uniform) * eigen * (-2.0 / (N * M))
    radius = square * lax.rsqrt(square)
    past = bits_1.astype(F32) - 2047.5
    h = jnp.abs(past) - 1024.0
    square = h * h
    value_re = radius * (h * horner(SINE, square))
    value_im = jnp.where(past > 0, -radius, radius) * horner(COSINE, square)
    return value_re, value_im


def add(a, b):
    return a[0] + b[0], a[1] + b[1]


def sub(a, b):
    return a[0] - b[0], a[1] - b[1]


def turn_back(a):
    return a[1], -a[0]


def dft_4(a, b, c, d):
    even, odd = add(a, c), add(b, d)
    less, turned = sub(a, c), turn_back(sub(b, d))
    return add(even, odd), add(less, turned), sub(even, odd), sub(less, turned)


def spin(a, step):
    if step == 0:
        return a
    if step == 4:
        return turn_back(a)
    if step % 4 == 2:
        root = math.sqrt(0.5)
        a = ((a[0] + a[1]) * root, (a[1] - a[0]) * root)
        return a if step == 2 else turn_back(a)
    c, s = math.cos(math.pi * step / 8), math.sin(math.pi * step / 8)
    return a[0] * c + a[1] * s, a[1] * c - a[0] * s


def dft_16(v):
    first = [dft_4(v[e], v[4 + e], v[8 + e], v[12 + e]) for e in range(4)]
    second = [dft_4(*(spin(first[e][s], e * s) for e in range(4))) for s in range(4)]
    return [second[k % 4][k // 4] for k in range(16)]


IN_VMEM = pl.BlockSpec(memory_space=pltpu.VMEM)


def front_kernel(noise, eigen, base, turn, out, bits, eig, base_in, drawn, tables, values, arrived):
    moves = [pltpu.make_async_copy(base, base_in, arrived.at[12])]
    for g in range(4):
        rows = slice(128 * g, 128 * (g + 1))
        for part in range(2):
            moves.append(pltpu.make_async_copy(noise.at[part, rows], bits.at[part, rows], arrived.at[3 * g + part]))
        moves.append(pltpu.make_async_copy(eigen.at[rows], eig.at[rows], arrived.at[3 * g + 2]))
    for move in moves:
        move.start()

    moves[0].wait()
    for r in range(4):
        cosine = base_in[0, r] * turn[0, r] - base_in[1, r] * turn[1, r]
        sine = base_in[1, r] * turn[0, r] + base_in[0, r] * turn[1, r]
        (cosine, cosine_low), (sine, sine_low) = split(cosine), split(sine)
        for at, c, s in ((0, cosine, sine), (256, cosine, sine), (512, cosine_low, sine_low)):
            tables[r, :128, at : at + 128] = c
            tables[r, :128, at + 128 : at + 256] = s
            tables[r, 128:, at : at + 128] = -s
            tables[r, 128:, at + 128 : at + 256] = c

    for g in range(3):
        for move in moves[3 * g + 1 : 3 * g + 4]:
            move.wait()

        def draws(i, carry):
            rows = pl.ds(pl.multiple_of(128 * g + 16 * i, 16), 16)
            drawn[0, rows, :], drawn[1, rows, :] = draw(bits[0, rows, :], bits[1, rows, :], eig[rows, :])
            return carry

        lax.fori_loop(0, 8, draws, 0)

    for move in moves[10:]:
        move.wait()
    for i in range(STEPS):
        columns = slice(BLOCK * i, BLOCK * (i + 1))
        parts = [
            (drawn[0, 128 * j : 128 * (j + 1), columns], drawn[1, 128 * j : 128 * (j + 1), columns]) for j in range(3)
        ]
        parts.append(draw(bits[0, 384:, columns], bits[1, 384:, columns], eig[384:, columns]))
        for r, value in enumerate(dft_4(*parts)):
            for part in range(2):
                high, low = split(value[part])
                for at, half in ((0, high), (256, low), (512, high)):
                    values[i, r, at + 128 * part : at + 128 * (part + 1), :] = half
        for r in range(4):
            both = dot(tables[r], values[i, r])
            for a in range(BLOCK // 128):
                for row in range(0, 256, 8):
                    part, zl, y, b = row // 128, row // 64 % 2, row // 16 % 4, row // 8 % 2
                    out[i, b, a, y, zl, part, r] = both[row : row + 8, 128 * a : 128 * (a + 1)]


def front(noise, eigen, turn):
    base = jnp.asarray(column_table())
    return pl.pallas_call(
        front_kernel,
        in_specs=[pl.BlockSpec(memory_space=pltpu.HBM)] * 3 + [IN_VMEM],
        out_specs=IN_VMEM,
        out_shape=jax.ShapeDtypeStruct((4, 2, 2, 4, 2, 2, 4, 8, 128), F32),
        scratch_shapes=[
            pltpu.VMEM((2, LOCAL, WIDTH), jnp.int32),
            pltpu.VMEM((LOCAL, WIDTH), F32),
            pltpu.VMEM((2, 4, 128, 128), F32),
            pltpu.VMEM((2, 384, WIDTH), F32),
            pltpu.VMEM((4, 256, 768), BF16),
            pltpu.VMEM((STEPS, 4, 768, BLOCK), BF16),
            pltpu.SemaphoreType.DMA((13,)),
        ],
        compiler_params=pltpu.CompilerParams(vmem_limit_bytes=32 * 2**20),
        cost_estimate=pl.CostEstimate(flops=2 * 10**9, bytes_accessed=12 * 2**20, transcendentals=0),
    )(*(pltpu.with_memory_space_constraint(value, pltpu.HBM) for value in (noise, eigen, base)), turn)


def middle_kernel(data, out):
    def step(at, carry):
        for y, zl in ((y, zl) for y in range(4) for zl in range(2)):
            r, values = at, []
            for e in range(16):
                core, zh, xl, xh = e >> 3, e >> 2 & 1, e >> 1 & 1, e & 1
                index = (2 * xh + xl, core, zh, y, zl)
                values.append((data[*index, 0, r], data[*index, 1, r]))
            for k, value in enumerate(dft_16(values)):
                core, zh, xl, xh = k & 1, k >> 1 & 1, k >> 2 & 1, k >> 3
                place = 4 * zh + 2 * xh + xl
                row = pl.multiple_of(1024 * place + 512 * zl + 256 * core + 64 * r, 64)
                for part in range(2):
                    out[pl.ds(row + 2 * y + part, 8, stride=8), :] = value[part]
        return carry

    lax.fori_loop(0, 4, step, 0)


def middle(data):
    return pl.pallas_call(
        middle_kernel,
        in_specs=[IN_VMEM],
        out_specs=IN_VMEM,
        out_shape=jax.ShapeDtypeStruct((8192, 128), F32),
        compiler_params=pltpu.CompilerParams(vmem_limit_bytes=32 * 2**20),
        cost_estimate=pl.CostEstimate(flops=10**7, bytes_accessed=8 * 2**20, transcendentals=0),
    )(data)


GROUP = 16


def row_kernel(data, first, twist, last, out):
    step = pl.program_id(0)

    def piece(t):
        return data[:, :, step // 2, t % 4, 4 * (step % 2) + t // 4].reshape(128, 128)

    for group in range(0, 16, GROUP):
        high, low = split(jnp.concatenate([piece(t) for t in range(group, group + GROUP)], 1))
        sums = dot(first[...], jnp.concatenate([high, low], 0))
        sums = sums[:128] + sums[128:]
        for t in range(group, group + GROUP):
            at = slice(128 * (t - group), 128 * (t - group + 1))
            re, im = sums[:64, at], sums[64:, at]
            both = []
            for v in range(2):
                c, s = twist[0, 64 * v : 64 * (v + 1), :], twist[1, 64 * v : 64 * (v + 1), :]
                both.append(jnp.concatenate([re * c - im * s, re * s + im * c], 1))
            high, low = split(jnp.concatenate(both, 0))
            whole = dot(high, last[...])
            whole = (whole[:, :128] + whole[:, 128:] + dot(low, last[:, :128])).T
            for part in range(2):
                out[part, pl.ds(512 * (t // 8) + t % 8, 64, stride=8), :] = whole[64 * part : 64 * (part + 1)]


def row_transform(data):
    tables = [jnp.asarray(table) for table in row_tables()]
    result = pl.pallas_call(
        row_kernel,
        grid=(4,),
        in_specs=[IN_VMEM] * 4,
        out_specs=pl.BlockSpec((2, 1024, 128), lambda i: (0, i, 0)),
        out_shape=jax.ShapeDtypeStruct((2, 4096, 128), F32),
        compiler_params=pltpu.CompilerParams(vmem_limit_bytes=16 * 2**20),
        cost_estimate=pl.CostEstimate(flops=3 * 10**9, bytes_accessed=9 * 2**20, transcendentals=0),
    )(data.reshape(8, 2, 2, 4, 8, 8, 128), *tables)
    return result.reshape(2, 8, 64, 8, 128).transpose(0, 1, 3, 2, 4).reshape(2, 64, M)


def on_device(noise, eigen):
    x, zh, core = (lax.axis_index(name) for name in AXES[:3])
    anchor = 8 * core + 4 * zh + 2 * (x % 2) + x // 2
    row = 4 * jnp.arange(128, dtype=jnp.int32)[None, :] + jnp.arange(4, dtype=jnp.int32)[:, None]
    angle = (anchor * row).astype(F32) * (2.0 * math.pi / N)
    turn = jnp.broadcast_to(jnp.stack([jnp.cos(angle), jnp.sin(angle)])[..., None], (2, 4, 128, 128))
    with jax.named_scope("columns"):
        data = front(noise, eigen, turn)
    with jax.named_scope("first_exchange"):
        data = lax.all_to_all(data.reshape(64, 2, 2, 32, 128), ("x", "core", "zh", "y"), 0, 0, tiled=True)
    with jax.named_scope("middle"):
        data = middle(data.reshape(4, 2, 2, 4, 2, 2, 4, 8, 128))
    with jax.named_scope("second_exchange"):
        data = lax.all_to_all(data.reshape(32, 256, 128), ("zh", "x", "zl", "core"), 0, 0, tiled=True)
    with jax.named_scope("rows"):
        return row_transform(data)


def solution(mesh):
    fine = Mesh(mesh.devices.reshape(SIZES), AXES)
    col, row = AXES[:3], AXES[3:]
    return jax.shard_map(
        on_device,
        mesh=fine,
        in_specs=(P(None, col, row), P(col, row)),
        out_specs=P(None, AXES, None),
        check_vma=False,
    )
```

```python
import functools
import math

import jax
import jax.numpy as jnp
import ml_dtypes
import numpy as np
from jax import lax
from jax.experimental import pallas as pl
from jax.experimental.pallas import tpu as pltpu
from jax.sharding import Mesh, PartitionSpec as P

N = 8192
M = 8192
LOCAL = 512
WIDTH = 1024
BLOCK = 256
STEPS = WIDTH // BLOCK

AXES = ("x", "zh", "core", "zl", "y")
SIZES = (4, 2, 2, 2, 4)

F32 = jnp.float32
BF16 = jnp.bfloat16


def halves(table):
    high = table.astype(np.float32).astype(ml_dtypes.bfloat16)
    low = (table - high.astype(np.float64)).astype(np.float32).astype(ml_dtypes.bfloat16)
    return high, low


def split(value):
    high = value.astype(BF16)
    low = (value - high.astype(F32)).astype(BF16)
    return high, low


def column_tables():
    e, r, m, j = np.ix_(np.arange(16), np.arange(4), np.arange(128), np.arange(128))
    angle = 2.0 * np.pi * ((4 * m + r) * (16 * j + e) % N) / N
    cosine, sine = np.cos(angle), np.sin(angle)
    table = np.concatenate([np.concatenate([cosine, sine], -1), np.concatenate([-sine, cosine], -1)], -2)
    return np.concatenate(halves(table), -1)


def row_tables():
    place = 8 * (4 * np.arange(2)[None, :, None] + np.arange(4)[None, None, :])
    place = place + np.array([0, 2, 4, 6, 1, 3, 5, 7])[:, None, None]
    angle = 2.0 * np.pi * (np.arange(64)[:, None] * place.reshape(1, 64) % 64) / 64
    cosine, sine = np.cos(angle), np.sin(angle)
    real_part = np.stack([cosine, sine], -1).reshape(64, 128)
    imag_part = np.stack([-sine, cosine], -1).reshape(64, 128)
    high, low = halves(np.concatenate([real_part, imag_part], 0))
    first = np.concatenate([np.concatenate([high, high], 1), np.concatenate([low, np.zeros_like(low)], 1)], 0)
    angle = 2.0 * np.pi * (np.outer(np.arange(128), np.arange(128)) % M) / M
    twist = np.stack([np.cos(angle), -np.sin(angle)]).astype(np.float32)
    angle = 2.0 * np.pi * (np.outer(np.arange(128), np.arange(64)) % 64) / 64
    cosine, sine = np.cos(angle), np.sin(angle)
    last = np.concatenate([np.concatenate([cosine, -sine], 1), np.concatenate([sine, cosine], 1)], 0)
    return first, twist, np.concatenate(halves(last), 1)


def sine_polynomials():
    nodes = 0.25 * np.cos(np.pi * (np.arange(400) + 0.5) / 800)
    square = np.polynomial.chebyshev.Chebyshev.fit(
        nodes**2, np.sin(2 * np.pi * nodes) / nodes, 4, domain=[0, 1 / 16]
    ).convert(kind=np.polynomial.Polynomial, domain=[-1, 1], window=[-1, 1])
    cosine = np.polynomial.chebyshev.Chebyshev.fit(
        nodes**2, np.cos(2 * np.pi * nodes), 4, domain=[0, 1 / 16]
    ).convert(kind=np.polynomial.Polynomial, domain=[-1, 1], window=[-1, 1])
    scale = 2.0**-12
    return (
        [float(c) * scale ** (2 * i + 1) for i, c in enumerate(square.coef)],
        [float(c) * scale ** (2 * i) for i, c in enumerate(cosine.coef)],
    )


SINE, COSINE = sine_polynomials()


def horner(coefficients, value):
    total = jnp.full_like(value, coefficients[-1])
    for coefficient in coefficients[-2::-1]:
        total = total * value + coefficient
    return total


def dot(a, b):
    return jnp.dot(a, b, preferred_element_type=F32)


def draw(bits_0, bits_1, eigen):
    uniform = (bits_0.astype(F32) + 0.5) * 2.0**-12
    square = jnp.log(uniform) * eigen * (-2.0 / (N * M))
    radius = square * lax.rsqrt(square)
    past = bits_1.astype(F32) - 2047.5
    h = jnp.abs(past) - 1024.0
    square = h * h
    value_re = radius * (h * horner(SINE, square))
    value_im = jnp.where(past > 0, -radius, radius) * horner(COSINE, square)
    return value_re, value_im


def add(a, b):
    return a[0] + b[0], a[1] + b[1]


def sub(a, b):
    return a[0] - b[0], a[1] - b[1]


def turn_back(a):
    return a[1], -a[0]


def dft_4(a, b, c, d):
    even, odd = add(a, c), add(b, d)
    less, turned = sub(a, c), turn_back(sub(b, d))
    return add(even, odd), add(less, turned), sub(even, odd), sub(less, turned)


def spin(a, step):
    if step == 0:
        return a
    if step == 4:
        return turn_back(a)
    if step % 4 == 2:
        root = math.sqrt(0.5)
        a = ((a[0] + a[1]) * root, (a[1] - a[0]) * root)
        return a if step == 2 else turn_back(a)
    c, s = math.cos(math.pi * step / 8), math.sin(math.pi * step / 8)
    return a[0] * c + a[1] * s, a[1] * c - a[0] * s


def dft_16(v):
    first = [dft_4(v[e], v[4 + e], v[8 + e], v[12 + e]) for e in range(4)]
    second = [dft_4(*(spin(first[e][s], e * s) for e in range(4))) for s in range(4)]
    return [second[k % 4][k // 4] for k in range(16)]


IN_VMEM = pl.BlockSpec(memory_space=pltpu.VMEM)


def front_kernel(noise, eigen, all_tables, out, bits, eig, drawn, tables, values, arrived):
    moves = []
    for g in range(8):
        rows = slice(64 * g, 64 * (g + 1))
        for part in range(2):
            moves.append(pltpu.make_async_copy(noise.at[part, rows], bits.at[part, rows], arrived.at[3 * g + part]))
        moves.append(pltpu.make_async_copy(eigen.at[rows], eig.at[rows], arrived.at[3 * g + 2]))
    x, zh, core = (lax.axis_index(name) for name in AXES[:3])
    digit = 8 * core + 4 * zh + 2 * (x % 2) + x // 2
    moves.append(pltpu.make_async_copy(all_tables.at[digit], tables, arrived.at[24]))
    for move in moves:
        move.start()

    for g in range(4):
        for move in moves[3 * g : 3 * g + 3]:
            move.wait()

        def draws(i, carry):
            rows = pl.ds(pl.multiple_of(64 * g + 32 * i, 32), 32)
            drawn[0, rows, :], drawn[1, rows, :] = draw(bits[0, rows, :], bits[1, rows, :], eig[rows, :])
            return carry

        lax.fori_loop(0, 2, draws, 0)

    for move in moves[12:]:
        move.wait()

    def prepare(i):
        columns = slice(BLOCK * i, BLOCK * (i + 1))
        parts = [
            (drawn[0, 128 * j : 128 * (j + 1), columns], drawn[1, 128 * j : 128 * (j + 1), columns]) for j in range(2)
        ]
        for j in range(2, 4):
            at = slice(128 * j, 128 * (j + 1))
            parts.append(draw(bits[0, at, columns], bits[1, at, columns], eig[at, columns]))
        for r, value in enumerate(dft_4(*parts)):
            for part in range(2):
                high, low = split(value[part])
                for at, half in ((0, high), (256, low)):
                    values[i, r, at + 128 * part : at + 128 * (part + 1), :] = half

    def multiply(i):
        for r in range(4):
            table, value = tables[r, :, :256], values[i, r, :256, :]
            both = dot(table, values[i, r, :256, :]) + dot(table, values[i, r, 256:, :]) + dot(tables[r, :, 256:], value)
            for a in range(BLOCK // 128):
                for row in range(0, 256, 8):
                    part, zl, y, b = row // 128, row // 64 % 2, row // 16 % 4, row // 8 % 2
                    out[i, b, a, y, zl, part, r] = both[row : row + 8, 128 * a : 128 * (a + 1)]

    prepare(0)
    for i in range(STEPS):
        if i + 1 < STEPS:
            prepare(i + 1)
        multiply(i)


def front(noise, eigen):
    operands = (noise, eigen, jnp.asarray(column_tables()))
    return pl.pallas_call(
        front_kernel,
        in_specs=[pl.BlockSpec(memory_space=pltpu.HBM)] * 3,
        out_specs=IN_VMEM,
        out_shape=jax.ShapeDtypeStruct((4, 2, 2, 4, 2, 2, 4, 8, 128), F32),
        scratch_shapes=[
            pltpu.VMEM((2, LOCAL, WIDTH), jnp.int32),
            pltpu.VMEM((LOCAL, WIDTH), F32),
            pltpu.VMEM((2, 256, WIDTH), F32),
            pltpu.VMEM((4, 256, 512), BF16),
            pltpu.VMEM((STEPS, 4, 512, BLOCK), BF16),
            pltpu.SemaphoreType.DMA((25,)),
        ],
        compiler_params=pltpu.CompilerParams(vmem_limit_bytes=32 * 2**20),
        cost_estimate=pl.CostEstimate(flops=2 * 10**9, bytes_accessed=12 * 2**20, transcendentals=0),
    )(*(pltpu.with_memory_space_constraint(value, pltpu.HBM) for value in operands))


def middle_kernel(data, out):
    def step(at, carry):
        for y, zl in ((y, zl) for y in range(4) for zl in range(2)):
            r, values = at, []
            for e in range(16):
                core, zh, xl, xh = e >> 3, e >> 2 & 1, e >> 1 & 1, e & 1
                index = (2 * xh + xl, core, zh, y, zl)
                values.append((data[*index, 0, r], data[*index, 1, r]))
            for k, value in enumerate(dft_16(values)):
                core, zh, xl, xh = k & 1, k >> 1 & 1, k >> 2 & 1, k >> 3
                place = 4 * zh + 2 * xh + xl
                row = pl.multiple_of(1024 * place + 512 * zl + 256 * core + 64 * r, 64)
                for part in range(2):
                    out[pl.ds(row + 2 * y + part, 8, stride=8), :] = value[part]
        return carry

    lax.fori_loop(0, 4, step, 0)


def middle(data):
    return pl.pallas_call(
        middle_kernel,
        in_specs=[IN_VMEM],
        out_specs=IN_VMEM,
        out_shape=jax.ShapeDtypeStruct((8192, 128), F32),
        compiler_params=pltpu.CompilerParams(vmem_limit_bytes=32 * 2**20),
        cost_estimate=pl.CostEstimate(flops=10**7, bytes_accessed=8 * 2**20, transcendentals=0),
    )(data)


GROUP = 16


def row_kernel(data, first, twist, last, out):
    step = pl.program_id(0)

    def piece(t):
        return data[:, :, step // 2, t % 4, 4 * (step % 2) + t // 4].reshape(128, 128)

    for group in range(0, 16, GROUP):
        high, low = split(jnp.concatenate([piece(t) for t in range(group, group + GROUP)], 1))
        sums = dot(first[...], jnp.concatenate([high, low], 0))
        sums = sums[:128] + sums[128:]
        for t in range(group, group + GROUP):
            at = slice(128 * (t - group), 128 * (t - group + 1))
            re, im = sums[:64, at], sums[64:, at]
            both = []
            for v in range(2):
                c, s = twist[0, 64 * v : 64 * (v + 1), :], twist[1, 64 * v : 64 * (v + 1), :]
                both.append(jnp.concatenate([re * c - im * s, re * s + im * c], 1))
            high, low = split(jnp.concatenate(both, 0))
            whole = dot(high, last[...])
            whole = (whole[:, :128] + whole[:, 128:] + dot(low, last[:, :128])).T
            for part in range(2):
                out[part, pl.ds(512 * (t // 8) + t % 8, 64, stride=8), :] = whole[64 * part : 64 * (part + 1)]


def row_transform(data):
    tables = [jnp.asarray(table) for table in row_tables()]
    result = pl.pallas_call(
        row_kernel,
        grid=(4,),
        in_specs=[IN_VMEM] * 4,
        out_specs=pl.BlockSpec((2, 1024, 128), lambda i: (0, i, 0)),
        out_shape=jax.ShapeDtypeStruct((2, 4096, 128), F32),
        compiler_params=pltpu.CompilerParams(vmem_limit_bytes=16 * 2**20),
        cost_estimate=pl.CostEstimate(flops=3 * 10**9, bytes_accessed=9 * 2**20, transcendentals=0),
    )(data.reshape(8, 2, 2, 4, 8, 8, 128), *tables)
    return result.reshape(2, 8, 64, 8, 128).transpose(0, 1, 3, 2, 4).reshape(2, 64, M)


def on_device(noise, eigen):
    with jax.named_scope("columns"):
        data = front(noise, eigen)
    with jax.named_scope("first_exchange"):
        data = lax.all_to_all(data.reshape(64, 2, 2, 32, 128), ("x", "core", "zh", "y"), 0, 0, tiled=True)
    with jax.named_scope("middle"):
        data = middle(data.reshape(4, 2, 2, 4, 2, 2, 4, 8, 128))
    with jax.named_scope("second_exchange"):
        data = lax.all_to_all(data.reshape(32, 256, 128), ("zh", "x", "zl", "core"), 0, 0, tiled=True)
    with jax.named_scope("rows"):
        return row_transform(data)


def solution(mesh):
    fine = Mesh(mesh.devices.reshape(SIZES), AXES)
    col, row = AXES[:3], AXES[3:]
    return jax.shard_map(
        on_device,
        mesh=fine,
        in_specs=(P(None, col, row), P(col, row)),
        out_specs=P(None, AXES, None),
        check_vma=False,
    )
```

```python
import functools
import math

import jax
import jax.numpy as jnp
import ml_dtypes
import numpy as np
from jax import lax
from jax.experimental import pallas as pl
from jax.experimental.pallas import tpu as pltpu
from jax.sharding import Mesh, PartitionSpec as P

N = 8192
M = 8192
LOCAL = 512
WIDTH = 1024
BLOCK = 256
STEPS = WIDTH // BLOCK

AXES = ("x", "zh", "core", "zl", "y")
SIZES = (4, 2, 2, 2, 4)

F32 = jnp.float32
BF16 = jnp.bfloat16


def halves(table):
    high = table.astype(np.float32).astype(ml_dtypes.bfloat16)
    low = (table - high.astype(np.float64)).astype(np.float32).astype(ml_dtypes.bfloat16)
    return high, low


def split(value):
    high = value.astype(BF16)
    low = (value - high.astype(F32)).astype(BF16)
    return high, low


def column_tables():
    e, r, m, j = np.ix_(np.arange(16), np.arange(4), np.arange(128), np.arange(128))
    angle = 2.0 * np.pi * ((4 * m + r) * (16 * j + e) % N) / N
    cosine, sine = np.cos(angle), np.sin(angle)
    table = np.concatenate([np.concatenate([cosine, sine], -1), np.concatenate([-sine, cosine], -1)], -2)
    return np.concatenate(halves(table), -1)


def row_tables():
    place = 8 * (4 * np.arange(2)[None, :, None] + np.arange(4)[None, None, :])
    place = place + np.array([0, 2, 4, 6, 1, 3, 5, 7])[:, None, None]
    angle = 2.0 * np.pi * (np.arange(64)[:, None] * place.reshape(1, 64) % 64) / 64
    cosine, sine = np.cos(angle), np.sin(angle)
    real_part = np.stack([cosine, sine], -1).reshape(64, 128)
    imag_part = np.stack([-sine, cosine], -1).reshape(64, 128)
    high, low = halves(np.concatenate([real_part, imag_part], 0))
    first = np.concatenate([np.concatenate([high, high], 1), np.concatenate([low, np.zeros_like(low)], 1)], 0)
    angle = 2.0 * np.pi * (np.outer(np.arange(128), np.arange(128)) % M) / M
    twist = np.stack([np.cos(angle), -np.sin(angle)]).astype(np.float32)
    angle = 2.0 * np.pi * (np.outer(np.arange(128), np.arange(64)) % 64) / 64
    cosine, sine = np.cos(angle), np.sin(angle)
    last = np.concatenate([np.concatenate([cosine, -sine], 1), np.concatenate([sine, cosine], 1)], 0)
    return first, twist, np.concatenate(halves(last), 1)


def sine_polynomials():
    nodes = 0.25 * np.cos(np.pi * (np.arange(400) + 0.5) / 800)
    square = np.polynomial.chebyshev.Chebyshev.fit(
        nodes**2, np.sin(2 * np.pi * nodes) / nodes, 4, domain=[0, 1 / 16]
    ).convert(kind=np.polynomial.Polynomial, domain=[-1, 1], window=[-1, 1])
    cosine = np.polynomial.chebyshev.Chebyshev.fit(
        nodes**2, np.cos(2 * np.pi * nodes), 4, domain=[0, 1 / 16]
    ).convert(kind=np.polynomial.Polynomial, domain=[-1, 1], window=[-1, 1])
    scale = 2.0**-12
    return (
        [float(c) * scale ** (2 * i + 1) for i, c in enumerate(square.coef)],
        [float(c) * scale ** (2 * i) for i, c in enumerate(cosine.coef)],
    )


SINE, COSINE = sine_polynomials()


def horner(coefficients, value):
    total = jnp.full_like(value, coefficients[-1])
    for coefficient in coefficients[-2::-1]:
        total = total * value + coefficient
    return total


def dot(a, b):
    return jnp.dot(a, b, preferred_element_type=F32)


def draw(bits_0, bits_1, eigen):
    uniform = (bits_0.astype(F32) + 0.5) * 2.0**-12
    square = jnp.log(uniform) * eigen * (-2.0 / (N * M))
    radius = square * lax.rsqrt(square)
    past = bits_1.astype(F32) - 2047.5
    h = jnp.abs(past) - 1024.0
    square = h * h
    value_re = radius * (h * horner(SINE, square))
    value_im = jnp.where(past > 0, -radius, radius) * horner(COSINE, square)
    return value_re, value_im


def add(a, b):
    return a[0] + b[0], a[1] + b[1]


def sub(a, b):
    return a[0] - b[0], a[1] - b[1]


def turn_back(a):
    return a[1], -a[0]


def dft_4(a, b, c, d):
    even, odd = add(a, c), add(b, d)
    less, turned = sub(a, c), turn_back(sub(b, d))
    return add(even, odd), add(less, turned), sub(even, odd), sub(less, turned)


def spin(a, step):
    if step == 0:
        return a
    if step == 4:
        return turn_back(a)
    if step % 4 == 2:
        root = math.sqrt(0.5)
        a = ((a[0] + a[1]) * root, (a[1] - a[0]) * root)
        return a if step == 2 else turn_back(a)
    c, s = math.cos(math.pi * step / 8), math.sin(math.pi * step / 8)
    return a[0] * c + a[1] * s, a[1] * c - a[0] * s


def dft_16(v):
    first = [dft_4(v[e], v[4 + e], v[8 + e], v[12 + e]) for e in range(4)]
    second = [dft_4(*(spin(first[e][s], e * s) for e in range(4))) for s in range(4)]
    return [second[k % 4][k // 4] for k in range(16)]


IN_VMEM = pl.BlockSpec(memory_space=pltpu.VMEM)


def front_kernel(noise, eigen, all_tables, out, bits, eig, drawn, tables, values, arrived):
    moves = []
    for g in range(8):
        rows = slice(64 * g, 64 * (g + 1))
        for part in range(2):
            moves.append(pltpu.make_async_copy(noise.at[part, rows], bits.at[part, rows], arrived.at[3 * g + part]))
        moves.append(pltpu.make_async_copy(eigen.at[rows], eig.at[rows], arrived.at[3 * g + 2]))
    x, zh, core = (lax.axis_index(name) for name in AXES[:3])
    digit = 8 * core + 4 * zh + 2 * (x % 2) + x // 2
    moves.append(pltpu.make_async_copy(all_tables.at[digit], tables, arrived.at[24]))
    for move in moves:
        move.start()

    for g in range(4):
        for move in moves[3 * g : 3 * g + 3]:
            move.wait()

        def draws(i, carry):
            rows = pl.ds(pl.multiple_of(64 * g + 32 * i, 32), 32)
            drawn[0, rows, :], drawn[1, rows, :] = draw(bits[0, rows, :], bits[1, rows, :], eig[rows, :])
            return carry

        lax.fori_loop(0, 2, draws, 0)

    for move in moves[12:]:
        move.wait()

    def prepare(i):
        columns = slice(BLOCK * i, BLOCK * (i + 1))
        parts = [
            (drawn[0, 128 * j : 128 * (j + 1), columns], drawn[1, 128 * j : 128 * (j + 1), columns]) for j in range(2)
        ]
        for j in range(2, 4):
            at = slice(128 * j, 128 * (j + 1))
            parts.append(draw(bits[0, at, columns], bits[1, at, columns], eig[at, columns]))
        for r, value in enumerate(dft_4(*parts)):
            for part in range(2):
                high, low = split(value[part])
                for at, half in ((0, high), (256, low)):
                    values[i, r, at + 128 * part : at + 128 * (part + 1), :] = half

    def multiply(i):
        for r in range(4):
            table, value = tables[r, :, :256], values[i, r, :256, :]
            both = dot(table, values[i, r, :256, :]) + dot(table, values[i, r, 256:, :]) + dot(tables[r, :, 256:], value)
            for a in range(BLOCK // 128):
                for row in range(0, 256, 8):
                    part, zl, y, b = row // 128, row // 64 % 2, row // 16 % 4, row // 8 % 2
                    out[i, b, a, y, zl, part, r] = both[row : row + 8, 128 * a : 128 * (a + 1)]

    prepare(0)
    for i in range(STEPS):
        if i + 1 < STEPS:
            prepare(i + 1)
        multiply(i)


def front(noise, eigen):
    operands = (noise, eigen, jnp.asarray(column_tables()))
    return pl.pallas_call(
        front_kernel,
        in_specs=[pl.BlockSpec(memory_space=pltpu.HBM)] * 3,
        out_specs=IN_VMEM,
        out_shape=jax.ShapeDtypeStruct((4, 2, 2, 4, 2, 2, 4, 8, 128), F32),
        scratch_shapes=[
            pltpu.VMEM((2, LOCAL, WIDTH), jnp.int32),
            pltpu.VMEM((LOCAL, WIDTH), F32),
            pltpu.VMEM((2, 256, WIDTH), F32),
            pltpu.VMEM((4, 256, 512), BF16),
            pltpu.VMEM((STEPS, 4, 512, BLOCK), BF16),
            pltpu.SemaphoreType.DMA((25,)),
        ],
        compiler_params=pltpu.CompilerParams(vmem_limit_bytes=32 * 2**20),
        cost_estimate=pl.CostEstimate(flops=2 * 10**9, bytes_accessed=12 * 2**20, transcendentals=0),
    )(*(pltpu.with_memory_space_constraint(value, pltpu.HBM) for value in operands))


def middle_kernel(data, out):
    def step(at, carry):
        for y, zl in ((y, zl) for y in range(4) for zl in range(2)):
            r, values = at, []
            for e in range(16):
                core, zh, xl, xh = e >> 3, e >> 2 & 1, e >> 1 & 1, e & 1
                index = (2 * xh + xl, core, zh, y, zl)
                values.append((data[*index, 0, r], data[*index, 1, r]))
            for k, value in enumerate(dft_16(values)):
                core, zh, xl, xh = k & 1, k >> 1 & 1, k >> 2 & 1, k >> 3
                place = 4 * zh + 2 * xh + xl
                row = pl.multiple_of(1024 * place + 512 * zl + 256 * core + 64 * r, 64)
                for part in range(2):
                    out[pl.ds(row + 2 * y + part, 8, stride=8), :] = value[part]
        return carry

    lax.fori_loop(0, 4, step, 0)


def middle(data):
    return pl.pallas_call(
        middle_kernel,
        in_specs=[IN_VMEM],
        out_specs=IN_VMEM,
        out_shape=jax.ShapeDtypeStruct((8192, 128), F32),
        compiler_params=pltpu.CompilerParams(vmem_limit_bytes=32 * 2**20),
        cost_estimate=pl.CostEstimate(flops=10**7, bytes_accessed=8 * 2**20, transcendentals=0),
    )(data)


def row_kernel(data, first, twist, last, out, done, sent):
    moves = []
    for step in range(4):
        pieces = []
        for t in range(16):
            pieces.append(data[:, :, step // 2, t % 4, 4 * (step % 2) + t // 4].reshape(128, 128))
        high, low = split(jnp.concatenate(pieces, 1))
        sums = dot(first[...], jnp.concatenate([high, low], 0))
        sums = sums[:128] + sums[128:]
        for t in range(16):
            at = slice(128 * t, 128 * (t + 1))
            re, im = sums[:64, at], sums[64:, at]
            both = []
            for v in range(2):
                c, s = twist[0, 64 * v : 64 * (v + 1), :], twist[1, 64 * v : 64 * (v + 1), :]
                both.append(jnp.concatenate([re * c - im * s, re * s + im * c], 1))
            high, low = split(jnp.concatenate(both, 0))
            whole = dot(high, last[...])
            whole = (whole[:, :128] + whole[:, 128:] + dot(low, last[:, :128])).T
            for part in range(2):
                rows = pl.ds(512 * (t // 8) + t % 8, 64, stride=8)
                done[step, part, rows, :] = whole[64 * part : 64 * (part + 1)]
            if t % 8 == 7:
                tile = t // 8
                for part in range(2):
                    move = pltpu.make_async_copy(
                        done.at[step, part, pl.ds(512 * tile, 512)],
                        out.at[part, pl.ds(1024 * step + 512 * tile, 512)],
                        sent.at[4 * step + 2 * tile + part],
                    )
                    move.start()
                    moves.append(move)
    for move in moves:
        move.wait()


def row_transform(data):
    tables = [jnp.asarray(table) for table in row_tables()]
    result = pl.pallas_call(
        row_kernel,
        in_specs=[IN_VMEM] * 4,
        out_specs=pl.BlockSpec(memory_space=pltpu.HBM),
        out_shape=jax.ShapeDtypeStruct((2, 4096, 128), F32),
        scratch_shapes=[pltpu.VMEM((4, 2, 1024, 128), F32), pltpu.SemaphoreType.DMA((16,))],
        compiler_params=pltpu.CompilerParams(vmem_limit_bytes=20 * 2**20),
        cost_estimate=pl.CostEstimate(flops=3 * 10**9, bytes_accessed=9 * 2**20, transcendentals=0),
    )(data.reshape(8, 2, 2, 4, 8, 8, 128), *tables)
    return result.reshape(2, 8, 64, 8, 128).transpose(0, 1, 3, 2, 4).reshape(2, 64, M)


def on_device(noise, eigen):
    with jax.named_scope("columns"):
        data = front(noise, eigen)
    with jax.named_scope("first_exchange"):
        data = lax.all_to_all(data.reshape(64, 2, 2, 32, 128), ("x", "core", "zh", "y"), 0, 0, tiled=True)
    with jax.named_scope("middle"):
        data = middle(data.reshape(4, 2, 2, 4, 2, 2, 4, 8, 128))
    with jax.named_scope("second_exchange"):
        data = lax.all_to_all(data.reshape(32, 256, 128), ("zh", "x", "zl", "core"), 0, 0, tiled=True)
    with jax.named_scope("rows"):
        return row_transform(data)


def solution(mesh):
    fine = Mesh(mesh.devices.reshape(SIZES), AXES)
    col, row = AXES[:3], AXES[3:]
    return jax.shard_map(
        on_device,
        mesh=fine,
        in_specs=(P(None, col, row), P(col, row)),
        out_specs=P(None, AXES, None),
        check_vma=False,
    )
```

```python
import functools
import math

import jax
import jax.numpy as jnp
import ml_dtypes
import numpy as np
from jax import lax
from jax.experimental import pallas as pl
from jax.experimental.pallas import tpu as pltpu
from jax.sharding import Mesh, PartitionSpec as P

N = 8192
M = 8192
LOCAL = 512
WIDTH = 1024
BLOCK = 256
STEPS = WIDTH // BLOCK
PIECES = (32, 32, 64, 64, 64, 64, 64, 64, 64)
EARLY = 448

AXES = ("x", "zh", "core", "zl", "y")
SIZES = (4, 2, 2, 2, 4)

F32 = jnp.float32
BF16 = jnp.bfloat16


def halves(table):
    high = table.astype(np.float32).astype(ml_dtypes.bfloat16)
    low = (table - high.astype(np.float64)).astype(np.float32).astype(ml_dtypes.bfloat16)
    return high, low


def split(value):
    high = value.astype(BF16)
    low = (value - high.astype(F32)).astype(BF16)
    return high, low


def column_tables():
    e, r, m, j = np.ix_(np.arange(16), np.arange(4), np.arange(128), np.arange(128))
    angle = 2.0 * np.pi * ((4 * m + r) * (16 * j + e) % N) / N
    cosine, sine = np.cos(angle), np.sin(angle)
    table = np.concatenate([np.concatenate([cosine, sine], -1), np.concatenate([-sine, cosine], -1)], -2)
    return np.concatenate(halves(table), -1)


def row_tables():
    place = 8 * (4 * np.arange(2)[None, :, None] + np.arange(4)[None, None, :])
    place = place + np.array([0, 2, 4, 6, 1, 3, 5, 7])[:, None, None]
    angle = 2.0 * np.pi * (np.arange(64)[:, None] * place.reshape(1, 64) % 64) / 64
    cosine, sine = np.cos(angle), np.sin(angle)
    real_part = np.stack([cosine, sine], -1).reshape(64, 128)
    imag_part = np.stack([-sine, cosine], -1).reshape(64, 128)
    high, low = halves(np.concatenate([real_part, imag_part], 0))
    first = np.concatenate([np.concatenate([high, high], 1), np.concatenate([low, np.zeros_like(low)], 1)], 0)
    angle = 2.0 * np.pi * (np.outer(np.arange(128), np.arange(128)) % M) / M
    twist = np.stack([np.cos(angle), -np.sin(angle)]).astype(np.float32)
    angle = 2.0 * np.pi * (np.outer(np.arange(128), np.arange(64)) % 64) / 64
    cosine, sine = np.cos(angle), np.sin(angle)
    last = np.concatenate([np.concatenate([cosine, -sine], 1), np.concatenate([sine, cosine], 1)], 0)
    return first, twist, np.concatenate(halves(last), 1)


def sine_polynomials():
    nodes = 0.25 * np.cos(np.pi * (np.arange(400) + 0.5) / 800)
    square = np.polynomial.chebyshev.Chebyshev.fit(
        nodes**2, np.sin(2 * np.pi * nodes) / nodes, 4, domain=[0, 1 / 16]
    ).convert(kind=np.polynomial.Polynomial, domain=[-1, 1], window=[-1, 1])
    cosine = np.polynomial.chebyshev.Chebyshev.fit(
        nodes**2, np.cos(2 * np.pi * nodes), 4, domain=[0, 1 / 16]
    ).convert(kind=np.polynomial.Polynomial, domain=[-1, 1], window=[-1, 1])
    scale = 2.0**-12
    return (
        [float(c) * scale ** (2 * i + 1) for i, c in enumerate(square.coef)],
        [float(c) * scale ** (2 * i) for i, c in enumerate(cosine.coef)],
    )


SINE, COSINE = sine_polynomials()


def horner(coefficients, value):
    total = jnp.full_like(value, coefficients[-1])
    for coefficient in coefficients[-2::-1]:
        total = total * value + coefficient
    return total


def dot(a, b):
    return jnp.dot(a, b, preferred_element_type=F32)


def draw(bits_0, bits_1, eigen):
    uniform = (bits_0.astype(F32) + 0.5) * 2.0**-12
    square = jnp.log(uniform) * eigen * (-2.0 / (N * M))
    radius = square * lax.rsqrt(square)
    past = bits_1.astype(F32) - 2047.5
    h = jnp.abs(past) - 1024.0
    square = h * h
    value_re = radius * (h * horner(SINE, square))
    value_im = jnp.where(past > 0, -radius, radius) * horner(COSINE, square)
    return value_re, value_im


def add(a, b):
    return a[0] + b[0], a[1] + b[1]


def sub(a, b):
    return a[0] - b[0], a[1] - b[1]


def turn_back(a):
    return a[1], -a[0]


def dft_4(a, b, c, d):
    even, odd = add(a, c), add(b, d)
    less, turned = sub(a, c), turn_back(sub(b, d))
    return add(even, odd), add(less, turned), sub(even, odd), sub(less, turned)


def spin(a, step):
    if step == 0:
        return a
    if step == 4:
        return turn_back(a)
    if step % 4 == 2:
        root = math.sqrt(0.5)
        a = ((a[0] + a[1]) * root, (a[1] - a[0]) * root)
        return a if step == 2 else turn_back(a)
    c, s = math.cos(math.pi * step / 8), math.sin(math.pi * step / 8)
    return a[0] * c + a[1] * s, a[1] * c - a[0] * s


def dft_16(v):
    first = [dft_4(v[e], v[4 + e], v[8 + e], v[12 + e]) for e in range(4)]
    second = [dft_4(*(spin(first[e][s], e * s) for e in range(4))) for s in range(4)]
    return [second[k % 4][k // 4] for k in range(16)]


IN_VMEM = pl.BlockSpec(memory_space=pltpu.VMEM)


def front_kernel(noise, eigen, all_tables, out, bits, eig, drawn, tables, values, arrived):
    moves, first = [], 0
    for g, count in enumerate(PIECES):
        rows = slice(first, first + count)
        for part in range(2):
            moves.append(pltpu.make_async_copy(noise.at[part, rows], bits.at[part, rows], arrived.at[3 * g + part]))
        moves.append(pltpu.make_async_copy(eigen.at[rows], eig.at[rows], arrived.at[3 * g + 2]))
        first += count
    x, zh, core = (lax.axis_index(name) for name in AXES[:3])
    digit = 8 * core + 4 * zh + 2 * (x % 2) + x // 2
    moves.append(pltpu.make_async_copy(all_tables.at[digit], tables, arrived.at[3 * len(PIECES)]))
    for move in moves:
        move.start()

    first = 0
    for g, count in enumerate(PIECES):
        for move in moves[3 * g : 3 * g + 3]:
            move.wait()
        if first < EARLY:

            def draws(i, carry, first=first):
                rows = pl.ds(pl.multiple_of(first + 32 * i, 32), 32)
                drawn[0, rows, :], drawn[1, rows, :] = draw(bits[0, rows, :], bits[1, rows, :], eig[rows, :])
                return carry

            lax.fori_loop(0, count // 32, draws, 0)
        first += count
    moves[-1].wait()

    def prepare(i):
        columns = slice(BLOCK * i, BLOCK * (i + 1))
        parts = []
        for j in range(4):
            known = min(max(EARLY - 128 * j, 0), 128)
            old, new = slice(128 * j, 128 * j + known), slice(128 * j + known, 128 * (j + 1))
            part = [(drawn[0, old, columns], drawn[1, old, columns])] if known else []
            if known < 128:
                part.append(draw(bits[0, new, columns], bits[1, new, columns], eig[new, columns]))
            parts.append(part[0] if len(part) == 1 else tuple(jnp.concatenate(both, 0) for both in zip(*part)))
        for r, value in enumerate(dft_4(*parts)):
            for part in range(2):
                high, low = split(value[part])
                for at, half in ((0, high), (256, low)):
                    values[i, r, at + 128 * part : at + 128 * (part + 1), :] = half

    def multiply(i):
        for r in range(4):
            table, value = tables[r, :, :256], values[i, r, :256, :]
            both = dot(table, values[i, r, :256, :]) + dot(table, values[i, r, 256:, :]) + dot(tables[r, :, 256:], value)
            for a in range(BLOCK // 128):
                for row in range(0, 256, 8):
                    part, zl, y, b = row // 128, row // 64 % 2, row // 16 % 4, row // 8 % 2
                    out[i, b, a, y, zl, part, r] = both[row : row + 8, 128 * a : 128 * (a + 1)]

    prepare(0)
    for i in range(STEPS):
        if i + 1 < STEPS:
            prepare(i + 1)
        multiply(i)


def front(noise, eigen):
    operands = (noise, eigen, jnp.asarray(column_tables()))
    return pl.pallas_call(
        front_kernel,
        in_specs=[pl.BlockSpec(memory_space=pltpu.HBM)] * 3,
        out_specs=IN_VMEM,
        out_shape=jax.ShapeDtypeStruct((4, 2, 2, 4, 2, 2, 4, 8, 128), F32),
        scratch_shapes=[
            pltpu.VMEM((2, LOCAL, WIDTH), jnp.int32),
            pltpu.VMEM((LOCAL, WIDTH), F32),
            pltpu.VMEM((2, EARLY, WIDTH), F32),
            pltpu.VMEM((4, 256, 512), BF16),
            pltpu.VMEM((STEPS, 4, 512, BLOCK), BF16),
            pltpu.SemaphoreType.DMA((3 * len(PIECES) + 1,)),
        ],
        compiler_params=pltpu.CompilerParams(vmem_limit_bytes=32 * 2**20),
        cost_estimate=pl.CostEstimate(flops=2 * 10**9, bytes_accessed=12 * 2**20, transcendentals=0),
    )(*(pltpu.with_memory_space_constraint(value, pltpu.HBM) for value in operands))


def middle_kernel(data, out):
    def step(at, carry):
        for y, zl in ((y, zl) for y in range(4) for zl in range(2)):
            r, values = at, []
            for e in range(16):
                core, zh, xl, xh = e >> 3, e >> 2 & 1, e >> 1 & 1, e & 1
                index = (2 * xh + xl, core, zh, y, zl)
                values.append((data[*index, 0, r], data[*index, 1, r]))
            for k, value in enumerate(dft_16(values)):
                core, zh, xl, xh = k & 1, k >> 1 & 1, k >> 2 & 1, k >> 3
                place = 4 * zh + 2 * xh + xl
                row = pl.multiple_of(1024 * place + 512 * zl + 256 * core + 64 * r, 64)
                for part in range(2):
                    out[pl.ds(row + 2 * y + part, 8, stride=8), :] = value[part]
        return carry

    lax.fori_loop(0, 4, step, 0)


def middle(data):
    return pl.pallas_call(
        middle_kernel,
        in_specs=[IN_VMEM],
        out_specs=IN_VMEM,
        out_shape=jax.ShapeDtypeStruct((8192, 128), F32),
        compiler_params=pltpu.CompilerParams(vmem_limit_bytes=32 * 2**20),
        cost_estimate=pl.CostEstimate(flops=10**7, bytes_accessed=8 * 2**20, transcendentals=0),
    )(data)


def row_kernel(data, first, twist, last, out, done, sent):
    moves = []
    for step in range(4):
        pieces = []
        for t in range(16):
            pieces.append(data[:, :, step // 2, t % 4, 4 * (step % 2) + t // 4].reshape(128, 128))
        high, low = split(jnp.concatenate(pieces, 1))
        sums = dot(first[...], jnp.concatenate([high, low], 0))
        sums = sums[:128] + sums[128:]
        for t in range(16):
            at = slice(128 * t, 128 * (t + 1))
            re, im = sums[:64, at], sums[64:, at]
            both = []
            for v in range(2):
                c, s = twist[0, 64 * v : 64 * (v + 1), :], twist[1, 64 * v : 64 * (v + 1), :]
                both.append(jnp.concatenate([re * c - im * s, re * s + im * c], 1))
            high, low = split(jnp.concatenate(both, 0))
            whole = dot(high, last[...])
            whole = (whole[:, :128] + whole[:, 128:] + dot(low, last[:, :128])).T
            for part in range(2):
                rows = pl.ds(512 * (t // 8) + t % 8, 64, stride=8)
                done[step, part, rows, :] = whole[64 * part : 64 * (part + 1)]
            if t % 8 == 7:
                tile = t // 8
                for part in range(2):
                    move = pltpu.make_async_copy(
                        done.at[step, part, pl.ds(512 * tile, 512)],
                        out.at[part, pl.ds(1024 * step + 512 * tile, 512)],
                        sent.at[4 * step + 2 * tile + part],
                    )
                    move.start()
                    moves.append(move)
    for move in moves:
        move.wait()


def row_transform(data):
    tables = [jnp.asarray(table) for table in row_tables()]
    result = pl.pallas_call(
        row_kernel,
        in_specs=[IN_VMEM] * 4,
        out_specs=pl.BlockSpec(memory_space=pltpu.HBM),
        out_shape=jax.ShapeDtypeStruct((2, 4096, 128), F32),
        scratch_shapes=[pltpu.VMEM((4, 2, 1024, 128), F32), pltpu.SemaphoreType.DMA((16,))],
        compiler_params=pltpu.CompilerParams(vmem_limit_bytes=20 * 2**20),
        cost_estimate=pl.CostEstimate(flops=3 * 10**9, bytes_accessed=9 * 2**20, transcendentals=0),
    )(data.reshape(8, 2, 2, 4, 8, 8, 128), *tables)
    return result.reshape(2, 8, 64, 8, 128).transpose(0, 1, 3, 2, 4).reshape(2, 64, M)


def on_device(noise, eigen):
    with jax.named_scope("columns"):
        data = front(noise, eigen)
    with jax.named_scope("first_exchange"):
        data = lax.all_to_all(data.reshape(64, 2, 2, 32, 128), ("x", "core", "zh", "y"), 0, 0, tiled=True)
    with jax.named_scope("middle"):
        data = middle(data.reshape(4, 2, 2, 4, 2, 2, 4, 8, 128))
    with jax.named_scope("second_exchange"):
        data = lax.all_to_all(data.reshape(32, 256, 128), ("zh", "x", "zl", "core"), 0, 0, tiled=True)
    with jax.named_scope("rows"):
        return row_transform(data)


def solution(mesh):
    fine = Mesh(mesh.devices.reshape(SIZES), AXES)
    col, row = AXES[:3], AXES[3:]
    return jax.shard_map(
        on_device,
        mesh=fine,
        in_specs=(P(None, col, row), P(col, row)),
        out_specs=P(None, AXES, None),
        check_vma=False,
    )
```

```python
import functools
import math

import jax
import jax.numpy as jnp
import ml_dtypes
import numpy as np
from jax import lax
from jax.experimental import pallas as pl
from jax.experimental.pallas import tpu as pltpu
from jax.sharding import Mesh, PartitionSpec as P

N = 8192
M = 8192
LOCAL = 512
WIDTH = 1024
BLOCK = 256
STEPS = WIDTH // BLOCK
PIECES = (32, 32, 64, 64, 64, 64, 64, 64, 64)
EARLY = 448

AXES = ("x", "zh", "core", "zl", "y")
SIZES = (4, 2, 2, 2, 4)

F32 = jnp.float32
BF16 = jnp.bfloat16


def halves(table):
    high = table.astype(np.float32).astype(ml_dtypes.bfloat16)
    low = (table - high.astype(np.float64)).astype(np.float32).astype(ml_dtypes.bfloat16)
    return high, low


def split(value):
    high = value.astype(BF16)
    low = (value - high.astype(F32)).astype(BF16)
    return high, low


def column_tables():
    e, r, m, j = np.ix_(np.arange(16), np.arange(4), np.arange(128), np.arange(128))
    angle = 2.0 * np.pi * ((4 * m + r) * (16 * j + e) % N) / N
    cosine, sine = np.cos(angle), np.sin(angle)
    table = np.concatenate([np.concatenate([cosine, sine], -1), np.concatenate([-sine, cosine], -1)], -2)
    return np.concatenate(halves(table), -1)


def row_tables():
    place = 8 * (4 * np.arange(2)[None, :, None] + np.arange(4)[None, None, :])
    place = place + np.array([0, 2, 4, 6, 1, 3, 5, 7])[:, None, None]
    angle = 2.0 * np.pi * (np.arange(64)[:, None] * place.reshape(1, 64) % 64) / 64
    cosine, sine = np.cos(angle), np.sin(angle)
    real_part = np.stack([cosine, sine], -1).reshape(64, 128)
    imag_part = np.stack([-sine, cosine], -1).reshape(64, 128)
    high, low = halves(np.concatenate([real_part, imag_part], 0))
    first = np.concatenate([np.concatenate([high, high], 1), np.concatenate([low, np.zeros_like(low)], 1)], 0)
    angle = 2.0 * np.pi * np.outer(np.arange(64), np.arange(128)) / M
    twist = np.stack([np.cos(angle), -np.sin(angle)]).astype(np.float32)
    last = []
    for order in ([0, 1], [1, 0]):
        k = 2 * np.arange(64)[None, :] + np.array(order)[:, None]
        angle = 2.0 * np.pi * (np.outer(np.arange(128), k.reshape(128)) % 128) / 128
        cosine, sine = np.cos(angle), np.sin(angle)
        table = np.concatenate([np.concatenate([cosine, -sine], 1), np.concatenate([sine, cosine], 1)], 0)
        last.append(np.stack(halves(table)))
    return first, twist, np.stack(last)


def sine_polynomials():
    nodes = 0.25 * np.cos(np.pi * (np.arange(400) + 0.5) / 800)
    square = np.polynomial.chebyshev.Chebyshev.fit(
        nodes**2, np.sin(2 * np.pi * nodes) / nodes, 4, domain=[0, 1 / 16]
    ).convert(kind=np.polynomial.Polynomial, domain=[-1, 1], window=[-1, 1])
    cosine = np.polynomial.chebyshev.Chebyshev.fit(
        nodes**2, np.cos(2 * np.pi * nodes), 4, domain=[0, 1 / 16]
    ).convert(kind=np.polynomial.Polynomial, domain=[-1, 1], window=[-1, 1])
    scale = 2.0**-12
    return (
        [float(c) * scale ** (2 * i + 1) for i, c in enumerate(square.coef)],
        [float(c) * scale ** (2 * i) for i, c in enumerate(cosine.coef)],
    )


SINE, COSINE = sine_polynomials()


def horner(coefficients, value):
    total = jnp.full_like(value, coefficients[-1])
    for coefficient in coefficients[-2::-1]:
        total = total * value + coefficient
    return total


def dot(a, b):
    return jnp.dot(a, b, preferred_element_type=F32)


def draw(bits_0, bits_1, eigen):
    uniform = (bits_0.astype(F32) + 0.5) * 2.0**-12
    square = jnp.log(uniform) * eigen * (-2.0 / (N * M))
    radius = square * lax.rsqrt(square)
    past = bits_1.astype(F32) - 2047.5
    h = jnp.abs(past) - 1024.0
    square = h * h
    value_re = radius * (h * horner(SINE, square))
    value_im = jnp.where(past > 0, -radius, radius) * horner(COSINE, square)
    return value_re, value_im


def add(a, b):
    return a[0] + b[0], a[1] + b[1]


def sub(a, b):
    return a[0] - b[0], a[1] - b[1]


def turn_back(a):
    return a[1], -a[0]


def dft_4(a, b, c, d):
    even, odd = add(a, c), add(b, d)
    less, turned = sub(a, c), turn_back(sub(b, d))
    return add(even, odd), add(less, turned), sub(even, odd), sub(less, turned)


def spin(a, step):
    if step == 0:
        return a
    if step == 4:
        return turn_back(a)
    if step % 4 == 2:
        root = math.sqrt(0.5)
        a = ((a[0] + a[1]) * root, (a[1] - a[0]) * root)
        return a if step == 2 else turn_back(a)
    c, s = math.cos(math.pi * step / 8), math.sin(math.pi * step / 8)
    return a[0] * c + a[1] * s, a[1] * c - a[0] * s


def dft_16(v):
    first = [dft_4(v[e], v[4 + e], v[8 + e], v[12 + e]) for e in range(4)]
    second = [dft_4(*(spin(first[e][s], e * s) for e in range(4))) for s in range(4)]
    return [second[k % 4][k // 4] for k in range(16)]


IN_VMEM = pl.BlockSpec(memory_space=pltpu.VMEM)


def front_kernel(noise, eigen, all_tables, out, bits, eig, drawn, tables, values, arrived):
    moves, first = [], 0
    for g, count in enumerate(PIECES):
        rows = slice(first, first + count)
        for part in range(2):
            moves.append(pltpu.make_async_copy(noise.at[part, rows], bits.at[part, rows], arrived.at[3 * g + part]))
        moves.append(pltpu.make_async_copy(eigen.at[rows], eig.at[rows], arrived.at[3 * g + 2]))
        first += count
    x, zh, core = (lax.axis_index(name) for name in AXES[:3])
    digit = 8 * core + 4 * zh + 2 * (x % 2) + x // 2
    moves.append(pltpu.make_async_copy(all_tables.at[digit], tables, arrived.at[3 * len(PIECES)]))
    for move in moves:
        move.start()

    first = 0
    for g, count in enumerate(PIECES):
        for move in moves[3 * g : 3 * g + 3]:
            move.wait()
        if first < EARLY:

            def draws(i, carry, first=first):
                rows = pl.ds(pl.multiple_of(first + 32 * i, 32), 32)
                drawn[0, rows, :], drawn[1, rows, :] = draw(bits[0, rows, :], bits[1, rows, :], eig[rows, :])
                return carry

            lax.fori_loop(0, count // 32, draws, 0)
        first += count
    moves[-1].wait()

    def prepare(i):
        columns = slice(BLOCK * i, BLOCK * (i + 1))
        parts = []
        for j in range(4):
            known = min(max(EARLY - 128 * j, 0), 128)
            old, new = slice(128 * j, 128 * j + known), slice(128 * j + known, 128 * (j + 1))
            part = [(drawn[0, old, columns], drawn[1, old, columns])] if known else []
            if known < 128:
                part.append(draw(bits[0, new, columns], bits[1, new, columns], eig[new, columns]))
            parts.append(part[0] if len(part) == 1 else tuple(jnp.concatenate(both, 0) for both in zip(*part)))
        for r, value in enumerate(dft_4(*parts)):
            for part in range(2):
                high, low = split(value[part])
                for at, half in ((0, high), (256, low)):
                    values[i, r, at + 128 * part : at + 128 * (part + 1), :] = half

    def multiply(i):
        for r in range(4):
            table, value = tables[r, :, :256], values[i, r, :256, :]
            both = dot(table, values[i, r, :256, :]) + dot(table, values[i, r, 256:, :]) + dot(tables[r, :, 256:], value)
            for a in range(BLOCK // 128):
                for row in range(0, 256, 8):
                    part, zl, y, b = row // 128, row // 64 % 2, row // 16 % 4, row // 8 % 2
                    out[i, b, a, y, zl, part, r] = both[row : row + 8, 128 * a : 128 * (a + 1)]

    prepare(0)
    for i in range(STEPS):
        if i + 1 < STEPS:
            prepare(i + 1)
        multiply(i)


def front(noise, eigen):
    operands = (noise, eigen, jnp.asarray(column_tables()))
    return pl.pallas_call(
        front_kernel,
        in_specs=[pl.BlockSpec(memory_space=pltpu.HBM)] * 3,
        out_specs=IN_VMEM,
        out_shape=jax.ShapeDtypeStruct((4, 2, 2, 4, 2, 2, 4, 8, 128), F32),
        scratch_shapes=[
            pltpu.VMEM((2, LOCAL, WIDTH), jnp.int32),
            pltpu.VMEM((LOCAL, WIDTH), F32),
            pltpu.VMEM((2, EARLY, WIDTH), F32),
            pltpu.VMEM((4, 256, 512), BF16),
            pltpu.VMEM((STEPS, 4, 512, BLOCK), BF16),
            pltpu.SemaphoreType.DMA((3 * len(PIECES) + 1,)),
        ],
        compiler_params=pltpu.CompilerParams(vmem_limit_bytes=32 * 2**20),
        cost_estimate=pl.CostEstimate(flops=2 * 10**9, bytes_accessed=12 * 2**20, transcendentals=0),
    )(*(pltpu.with_memory_space_constraint(value, pltpu.HBM) for value in operands))


def middle_kernel(data, out):
    def step(at, carry):
        for y, zl in ((y, zl) for y in range(4) for zl in range(2)):
            r, values = at, []
            for e in range(16):
                core, zh, xl, xh = e >> 3, e >> 2 & 1, e >> 1 & 1, e & 1
                index = (2 * xh + xl, core, zh, y, zl)
                values.append((data[*index, 0, r], data[*index, 1, r]))
            for k, value in enumerate(dft_16(values)):
                core, zh, xl, xh = k & 1, k >> 1 & 1, k >> 2 & 1, k >> 3
                place = 4 * zh + 2 * xh + xl
                row = pl.multiple_of(1024 * place + 512 * zl + 256 * core + 64 * r, 64)
                for part in range(2):
                    out[pl.ds(row + 2 * y + part, 8, stride=8), :] = value[part]
        return carry

    lax.fori_loop(0, 4, step, 0)


def middle(data):
    return pl.pallas_call(
        middle_kernel,
        in_specs=[IN_VMEM],
        out_specs=IN_VMEM,
        out_shape=jax.ShapeDtypeStruct((8192, 128), F32),
        compiler_params=pltpu.CompilerParams(vmem_limit_bytes=32 * 2**20),
        cost_estimate=pl.CostEstimate(flops=10**7, bytes_accessed=8 * 2**20, transcendentals=0),
    )(data)


ROWS = 32
TOGETHER = 8


def row_kernel(data, first, twist, last, out, done, sent):
    def move(step, tile, part):
        row = pl.multiple_of(64 * ROWS * step + 512 * tile, 512)
        return pltpu.make_async_copy(
            done.at[part, pl.ds(row, 512)], out.at[part, pl.ds(row, 512)], sent.at[ROWS // 4 * step + 2 * tile + part]
        )

    left = lax.broadcasted_iota(jnp.int32, (64, 128), 1) < 64

    def run(step, carry):
        pieces = []
        for t in range(ROWS):
            pieces.append(data[:, :, ROWS * step // 32, t % 4, ROWS * step % 32 // 4 + t // 4].reshape(128, 128))
        high, low = split(jnp.concatenate(pieces, 1))
        sums = dot(first[...], jnp.concatenate([high, low], 0))
        sums = sums[:128] + sums[128:]
        for group in range(0, ROWS, TOGETHER):
            sides = []
            for side in range(2):
                turned = []
                for t in range(group + side, group + TOGETHER, 2):
                    at = slice(128 * t, 128 * (t + 1))
                    re, im = sums[:64, at], sums[64:, at]
                    turned.append(jnp.concatenate([re * twist[0] - im * twist[1], re * twist[1] + im * twist[0]], 1))
                high, low = split(jnp.concatenate(turned, 0))
                table = last[side, 0]
                sides.append(dot(high, table) + dot(low, table) + dot(high, last[side, 1]))
            for t in range(group, group + TOGETHER, 2):
                at = slice(32 * (t - group), 32 * (t - group) + 64)
                for part in range(2):
                    lanes = slice(128 * part, 128 * (part + 1))
                    even, odd = sides[0][at, lanes], sides[1][at, lanes]
                    whole = jnp.concatenate([jnp.where(left, even, odd), jnp.where(left, odd, even)], 0).T
                    row = pl.multiple_of(64 * ROWS * step, 64 * ROWS) + 512 * (t // 8) + t % 8
                    done[part, pl.ds(row, 64, stride=8), :] = jnp.where(left, whole[:64], whole[64:])
                    done[part, pl.ds(row + 1, 64, stride=8), :] = jnp.where(left, whole[64:], whole[:64])
                if t % 8 == 6:
                    for part in range(2):
                        move(step, t // 8, part).start()
        return carry

    lax.fori_loop(0, 64 // ROWS, run, 0)
    for step in range(64 // ROWS):
        for tile in range(ROWS // 8):
            for part in range(2):
                move(step, tile, part).wait()


def row_transform(data):
    tables = [jnp.asarray(table) for table in row_tables()]
    result = pl.pallas_call(
        row_kernel,
        in_specs=[IN_VMEM] * 4,
        out_specs=pl.BlockSpec(memory_space=pltpu.HBM),
        out_shape=jax.ShapeDtypeStruct((2, 4096, 128), F32),
        scratch_shapes=[pltpu.VMEM((2, 4096, 128), F32), pltpu.SemaphoreType.DMA((16,))],
        compiler_params=pltpu.CompilerParams(vmem_limit_bytes=20 * 2**20),
        cost_estimate=pl.CostEstimate(flops=3 * 10**9, bytes_accessed=9 * 2**20, transcendentals=0),
    )(data.reshape(8, 2, 2, 4, 8, 8, 128), *tables)
    return result.reshape(2, 8, 64, 8, 128).transpose(0, 1, 3, 2, 4).reshape(2, 64, M)


def on_device(noise, eigen):
    with jax.named_scope("columns"):
        data = front(noise, eigen)
    with jax.named_scope("first_exchange"):
        data = lax.all_to_all(data.reshape(64, 2, 2, 32, 128), ("x", "core", "zh", "y"), 0, 0, tiled=True)
    with jax.named_scope("middle"):
        data = middle(data.reshape(4, 2, 2, 4, 2, 2, 4, 8, 128))
    with jax.named_scope("second_exchange"):
        data = lax.all_to_all(data.reshape(32, 256, 128), ("zh", "x", "zl", "core"), 0, 0, tiled=True)
    with jax.named_scope("rows"):
        return row_transform(data)


def solution(mesh):
    fine = Mesh(mesh.devices.reshape(SIZES), AXES)
    col, row = AXES[:3], AXES[3:]
    return jax.shard_map(
        on_device,
        mesh=fine,
        in_specs=(P(None, col, row), P(col, row)),
        out_specs=P(None, AXES, None),
        check_vma=False,
    )
```

```python
import functools
import math

import jax
import jax.numpy as jnp
import ml_dtypes
import numpy as np
from jax import lax
from jax.experimental import pallas as pl
from jax.experimental.pallas import tpu as pltpu
from jax.sharding import Mesh, PartitionSpec as P

N = 8192
M = 8192
LOCAL = 512
WIDTH = 1024
BLOCK = 256
STEPS = WIDTH // BLOCK
PIECES = (32, 32, 64, 64, 64, 64, 64, 64, 64)
EARLY = 448

AXES = ("x", "zh", "core", "zl", "y")
SIZES = (4, 2, 2, 2, 4)

F32 = jnp.float32
BF16 = jnp.bfloat16


def halves(table):
    high = table.astype(np.float32).astype(ml_dtypes.bfloat16)
    low = (table - high.astype(np.float64)).astype(np.float32).astype(ml_dtypes.bfloat16)
    return high, low


def split(value):
    high = value.astype(BF16)
    low = (value - high.astype(F32)).astype(BF16)
    return high, low


def column_tables():
    e, r, m, j = np.ix_(np.arange(16), np.arange(4), np.arange(128), np.arange(128))
    angle = 2.0 * np.pi * ((4 * m + r) * (16 * j + e) % N) / N
    cosine, sine = np.cos(angle), np.sin(angle)
    table = np.concatenate([np.concatenate([cosine, sine], -1), np.concatenate([-sine, cosine], -1)], -2)
    return np.concatenate(halves(table), -1)


def row_tables():
    place = 8 * (4 * np.arange(2)[None, :, None] + np.arange(4)[None, None, :])
    place = place + np.array([0, 2, 4, 6, 1, 3, 5, 7])[:, None, None]
    angle = 2.0 * np.pi * (np.arange(64)[:, None] * place.reshape(1, 64) % 64) / 64
    cosine, sine = np.cos(angle), np.sin(angle)
    real_part = np.stack([cosine, sine], -1).reshape(64, 128)
    imag_part = np.stack([-sine, cosine], -1).reshape(64, 128)
    high, low = halves(np.concatenate([real_part, imag_part], 0))
    first = np.concatenate([np.concatenate([high, high], 1), np.concatenate([low, np.zeros_like(low)], 1)], 0)
    angle = 2.0 * np.pi * np.outer(np.arange(64), np.arange(128)) / M
    twist = np.stack([np.cos(angle), -np.sin(angle)]).astype(np.float32)
    last = []
    for order in ([0, 1], [1, 0]):
        k = 2 * np.arange(64)[None, :] + np.array(order)[:, None]
        angle = 2.0 * np.pi * (np.outer(np.arange(128), k.reshape(128)) % 128) / 128
        cosine, sine = np.cos(angle), np.sin(angle)
        table = np.concatenate([np.concatenate([cosine, -sine], 1), np.concatenate([sine, cosine], 1)], 0)
        last.append(np.stack(halves(table)))
    return first, twist, np.stack(last)


def sine_polynomials():
    nodes = 0.25 * np.cos(np.pi * (np.arange(400) + 0.5) / 800)
    square = np.polynomial.chebyshev.Chebyshev.fit(
        nodes**2, np.sin(2 * np.pi * nodes) / nodes, 4, domain=[0, 1 / 16]
    ).convert(kind=np.polynomial.Polynomial, domain=[-1, 1], window=[-1, 1])
    cosine = np.polynomial.chebyshev.Chebyshev.fit(
        nodes**2, np.cos(2 * np.pi * nodes), 4, domain=[0, 1 / 16]
    ).convert(kind=np.polynomial.Polynomial, domain=[-1, 1], window=[-1, 1])
    scale = 2.0**-12
    return (
        [float(c) * scale ** (2 * i + 1) for i, c in enumerate(square.coef)],
        [float(c) * scale ** (2 * i) for i, c in enumerate(cosine.coef)],
    )


SINE, COSINE = sine_polynomials()


def horner(coefficients, value):
    total = jnp.full_like(value, coefficients[-1])
    for coefficient in coefficients[-2::-1]:
        total = total * value + coefficient
    return total


def dot(a, b):
    return jnp.dot(a, b, preferred_element_type=F32)


def draw(bits_0, bits_1, eigen):
    uniform = (bits_0.astype(F32) + 0.5) * 2.0**-12
    square = jnp.log(uniform) * eigen * (-2.0 / (N * M))
    radius = square * lax.rsqrt(square)
    past = bits_1.astype(F32) - 2047.5
    h = jnp.abs(past) - 1024.0
    square = h * h
    value_re = radius * (h * horner(SINE, square))
    value_im = jnp.where(past > 0, -radius, radius) * horner(COSINE, square)
    return value_re, value_im


def add(a, b):
    return a[0] + b[0], a[1] + b[1]


def sub(a, b):
    return a[0] - b[0], a[1] - b[1]


def turn_back(a):
    return a[1], -a[0]


def dft_4(a, b, c, d):
    even, odd = add(a, c), add(b, d)
    less, turned = sub(a, c), turn_back(sub(b, d))
    return add(even, odd), add(less, turned), sub(even, odd), sub(less, turned)


def spin(a, step):
    if step == 0:
        return a
    if step == 4:
        return turn_back(a)
    if step % 4 == 2:
        root = math.sqrt(0.5)
        a = ((a[0] + a[1]) * root, (a[1] - a[0]) * root)
        return a if step == 2 else turn_back(a)
    c, s = math.cos(math.pi * step / 8), math.sin(math.pi * step / 8)
    return a[0] * c + a[1] * s, a[1] * c - a[0] * s


def dft_16(v):
    first = [dft_4(v[e], v[4 + e], v[8 + e], v[12 + e]) for e in range(4)]
    second = [dft_4(*(spin(first[e][s], e * s) for e in range(4))) for s in range(4)]
    return [second[k % 4][k // 4] for k in range(16)]


IN_VMEM = pl.BlockSpec(memory_space=pltpu.VMEM)


def front_kernel(noise, eigen, all_tables, out, bits, eig, drawn, tables, values, arrived):
    moves, first = [], 0
    for g, count in enumerate(PIECES):
        rows = slice(first, first + count)
        for part in range(2):
            moves.append(pltpu.make_async_copy(noise.at[part, rows], bits.at[part, rows], arrived.at[3 * g + part]))
        moves.append(pltpu.make_async_copy(eigen.at[rows], eig.at[rows], arrived.at[3 * g + 2]))
        first += count
    x, zh, core = (lax.axis_index(name) for name in AXES[:3])
    digit = 8 * core + 4 * zh + 2 * (x % 2) + x // 2
    moves.append(pltpu.make_async_copy(all_tables.at[digit], tables, arrived.at[3 * len(PIECES)]))
    for move in moves:
        move.start()

    first = 0
    for g, count in enumerate(PIECES):
        for move in moves[3 * g : 3 * g + 3]:
            move.wait()
        if first < EARLY:

            def draws(i, carry, first=first):
                rows = pl.ds(pl.multiple_of(first + 32 * i, 32), 32)
                drawn[0, rows, :], drawn[1, rows, :] = draw(bits[0, rows, :], bits[1, rows, :], eig[rows, :])
                return carry

            lax.fori_loop(0, count // 32, draws, 0)
        first += count
    moves[-1].wait()

    def prepare(i):
        columns = slice(BLOCK * i, BLOCK * (i + 1))
        parts = []
        for j in range(4):
            known = min(max(EARLY - 128 * j, 0), 128)
            old, new = slice(128 * j, 128 * j + known), slice(128 * j + known, 128 * (j + 1))
            part = [(drawn[0, old, columns], drawn[1, old, columns])] if known else []
            if known < 128:
                part.append(draw(bits[0, new, columns], bits[1, new, columns], eig[new, columns]))
            parts.append(part[0] if len(part) == 1 else tuple(jnp.concatenate(both, 0) for both in zip(*part)))
        for r, value in enumerate(dft_4(*parts)):
            for part in range(2):
                high, low = split(value[part])
                for at, half in ((0, high), (256, low)):
                    values[i, r, at + 128 * part : at + 128 * (part + 1), :] = half

    def multiply(i):
        for r in range(4):
            table = jnp.concatenate([tables[r, :, :256], tables[r, :, 256:]], 0)
            both = dot(table, values[i, r, :256, :])
            both = both[:256] + both[256:] + dot(tables[r, :, :256], values[i, r, 256:, :])
            for a in range(BLOCK // 128):
                for row in range(0, 256, 8):
                    part, zl, y, b = row // 128, row // 64 % 2, row // 16 % 4, row // 8 % 2
                    out[i, b, a, y, zl, part, r] = both[row : row + 8, 128 * a : 128 * (a + 1)]

    prepare(0)
    for i in range(STEPS):
        if i + 1 < STEPS:
            prepare(i + 1)
        multiply(i)


def front(noise, eigen):
    operands = (noise, eigen, jnp.asarray(column_tables()))
    return pl.pallas_call(
        front_kernel,
        in_specs=[pl.BlockSpec(memory_space=pltpu.HBM)] * 3,
        out_specs=IN_VMEM,
        out_shape=jax.ShapeDtypeStruct((4, 2, 2, 4, 2, 2, 4, 8, 128), F32),
        scratch_shapes=[
            pltpu.VMEM((2, LOCAL, WIDTH), jnp.int32),
            pltpu.VMEM((LOCAL, WIDTH), F32),
            pltpu.VMEM((2, EARLY, WIDTH), F32),
            pltpu.VMEM((4, 256, 512), BF16),
            pltpu.VMEM((STEPS, 4, 512, BLOCK), BF16),
            pltpu.SemaphoreType.DMA((3 * len(PIECES) + 1,)),
        ],
        compiler_params=pltpu.CompilerParams(vmem_limit_bytes=32 * 2**20),
        cost_estimate=pl.CostEstimate(flops=2 * 10**9, bytes_accessed=12 * 2**20, transcendentals=0),
    )(*(pltpu.with_memory_space_constraint(value, pltpu.HBM) for value in operands))


def middle_kernel(data, out):
    def step(at, carry):
        for y, zl in ((y, zl) for y in range(4) for zl in range(2)):
            r, values = at, []
            for e in range(16):
                core, zh, xl, xh = e >> 3, e >> 2 & 1, e >> 1 & 1, e & 1
                index = (2 * xh + xl, core, zh, y, zl)
                values.append((data[*index, 0, r], data[*index, 1, r]))
            for k, value in enumerate(dft_16(values)):
                core, zh, xl, xh = k & 1, k >> 1 & 1, k >> 2 & 1, k >> 3
                place = 4 * zh + 2 * xh + xl
                row = pl.multiple_of(1024 * place + 512 * zl + 256 * core + 64 * r, 64)
                for part in range(2):
                    out[pl.ds(row + 2 * y + part, 8, stride=8), :] = value[part]
        return carry

    lax.fori_loop(0, 4, step, 0)


def middle(data):
    return pl.pallas_call(
        middle_kernel,
        in_specs=[IN_VMEM],
        out_specs=IN_VMEM,
        out_shape=jax.ShapeDtypeStruct((8192, 128), F32),
        compiler_params=pltpu.CompilerParams(vmem_limit_bytes=32 * 2**20),
        cost_estimate=pl.CostEstimate(flops=10**7, bytes_accessed=8 * 2**20, transcendentals=0),
    )(data)


ROWS = 32
TOGETHER = 8


def row_kernel(data, first, twist, last, out, done, sent):
    def move(step, tile, part):
        row = pl.multiple_of(64 * ROWS * step + 512 * tile, 512)
        return pltpu.make_async_copy(
            done.at[part, pl.ds(row, 512)], out.at[part, pl.ds(row, 512)], sent.at[ROWS // 4 * step + 2 * tile + part]
        )

    left = lax.broadcasted_iota(jnp.int32, (64, 128), 1) < 64

    def run(step, carry):
        pieces = []
        for t in range(ROWS):
            pieces.append(data[:, :, ROWS * step // 32, t % 4, ROWS * step % 32 // 4 + t // 4].reshape(128, 128))
        high, low = split(jnp.concatenate(pieces, 1))
        sums = dot(first[...], jnp.concatenate([high, low], 0))
        sums = sums[:128] + sums[128:]
        for group in range(0, ROWS, TOGETHER):
            sides = []
            for side in range(2):
                turned = []
                for t in range(group + side, group + TOGETHER, 2):
                    at = slice(128 * t, 128 * (t + 1))
                    re, im = sums[:64, at], sums[64:, at]
                    turned.append(jnp.concatenate([re * twist[0] - im * twist[1], re * twist[1] + im * twist[0]], 1))
                high, low = split(jnp.concatenate(turned, 0))
                table = last[side, 0]
                sides.append(dot(high, table) + dot(low, table) + dot(high, last[side, 1]))
            for t in range(group, group + TOGETHER, 2):
                at = slice(32 * (t - group), 32 * (t - group) + 64)
                for part in range(2):
                    lanes = slice(128 * part, 128 * (part + 1))
                    even, odd = sides[0][at, lanes], sides[1][at, lanes]
                    whole = jnp.concatenate([jnp.where(left, even, odd), jnp.where(left, odd, even)], 0).T
                    row = pl.multiple_of(64 * ROWS * step, 64 * ROWS) + 512 * (t // 8) + t % 8
                    done[part, pl.ds(row, 64, stride=8), :] = jnp.where(left, whole[:64], whole[64:])
                    done[part, pl.ds(row + 1, 64, stride=8), :] = jnp.where(left, whole[64:], whole[:64])
                if t % 8 == 6:
                    for part in range(2):
                        move(step, t // 8, part).start()
        return carry

    lax.fori_loop(0, 64 // ROWS, run, 0)
    for step in range(64 // ROWS):
        for tile in range(ROWS // 8):
            for part in range(2):
                move(step, tile, part).wait()


def row_transform(data):
    tables = [jnp.asarray(table) for table in row_tables()]
    result = pl.pallas_call(
        row_kernel,
        in_specs=[IN_VMEM] * 4,
        out_specs=pl.BlockSpec(memory_space=pltpu.HBM),
        out_shape=jax.ShapeDtypeStruct((2, 4096, 128), F32),
        scratch_shapes=[pltpu.VMEM((2, 4096, 128), F32), pltpu.SemaphoreType.DMA((16,))],
        compiler_params=pltpu.CompilerParams(vmem_limit_bytes=20 * 2**20),
        cost_estimate=pl.CostEstimate(flops=3 * 10**9, bytes_accessed=9 * 2**20, transcendentals=0),
    )(data.reshape(8, 2, 2, 4, 8, 8, 128), *tables)
    return result.reshape(2, 8, 64, 8, 128).transpose(0, 1, 3, 2, 4).reshape(2, 64, M)


def on_device(noise, eigen):
    with jax.named_scope("columns"):
        data = front(noise, eigen)
    with jax.named_scope("first_exchange"):
        data = lax.all_to_all(data.reshape(64, 2, 2, 32, 128), ("x", "core", "zh", "y"), 0, 0, tiled=True)
    with jax.named_scope("middle"):
        data = middle(data.reshape(4, 2, 2, 4, 2, 2, 4, 8, 128))
    with jax.named_scope("second_exchange"):
        data = lax.all_to_all(data.reshape(32, 256, 128), ("zh", "x", "zl", "core"), 0, 0, tiled=True)
    with jax.named_scope("rows"):
        return row_transform(data)


def solution(mesh):
    fine = Mesh(mesh.devices.reshape(SIZES), AXES)
    col, row = AXES[:3], AXES[3:]
    return jax.shard_map(
        on_device,
        mesh=fine,
        in_specs=(P(None, col, row), P(col, row)),
        out_specs=P(None, AXES, None),
        check_vma=False,
    )
```

```python
import functools
import math

import jax
import jax.numpy as jnp
import ml_dtypes
import numpy as np
from jax import lax
from jax.experimental import pallas as pl
from jax.experimental.pallas import tpu as pltpu
from jax.sharding import Mesh, PartitionSpec as P

N = 8192
M = 8192
LOCAL = 512
WIDTH = 1024
BLOCK = 256
STEPS = WIDTH // BLOCK
PIECES = (32, 32, 64, 64, 64, 64, 64, 64, 64)
EARLY = 448

AXES = ("x", "zh", "core", "zl", "y")
SIZES = (4, 2, 2, 2, 4)

F32 = jnp.float32
BF16 = jnp.bfloat16


def halves(table):
    high = table.astype(np.float32).astype(ml_dtypes.bfloat16)
    low = (table - high.astype(np.float64)).astype(np.float32).astype(ml_dtypes.bfloat16)
    return high, low


def split(value):
    high = value.astype(BF16)
    low = (value - high.astype(F32)).astype(BF16)
    return high, low


def column_tables():
    e, r, m, j = np.ix_(np.arange(16), np.arange(4), np.arange(128), np.arange(128))
    angle = 2.0 * np.pi * ((4 * m + r) * (16 * j + e) % N) / N
    cosine, sine = np.cos(angle), np.sin(angle)
    table = np.concatenate([np.concatenate([cosine, sine], -1), np.concatenate([-sine, cosine], -1)], -2)
    return np.concatenate(halves(table), -1)


def row_tables():
    zh, zl, x, y = np.ix_(np.arange(2), np.arange(2), np.arange(4), np.arange(4))
    place = 8 * (4 * zl + y) + 2 * x + zh
    angle = 2.0 * np.pi * (np.arange(64)[:, None] * place.reshape(1, 64) % 64) / 64
    cosine, sine = np.cos(angle), np.sin(angle)
    real_part = np.stack([cosine, sine], -1).reshape(64, 128)
    imag_part = np.stack([-sine, cosine], -1).reshape(64, 128)
    high, low = halves(np.concatenate([real_part, imag_part], 0))
    first = np.concatenate([np.concatenate([high, high], 1), np.concatenate([low, np.zeros_like(low)], 1)], 0)
    angle = 2.0 * np.pi * np.outer(np.arange(64), np.arange(128)) / M
    twist = np.stack([np.cos(angle), -np.sin(angle)]).astype(np.float32)
    last = []
    for order in ([0, 1], [1, 0]):
        k = 2 * np.arange(64)[None, :] + np.array(order)[:, None]
        angle = 2.0 * np.pi * (np.outer(np.arange(128), k.reshape(128)) % 128) / 128
        cosine, sine = np.cos(angle), np.sin(angle)
        table = np.concatenate([np.concatenate([cosine, -sine], 1), np.concatenate([sine, cosine], 1)], 0)
        last.append(np.stack(halves(table)))
    return first, twist, np.stack(last)


def sine_polynomials():
    nodes = 0.25 * np.cos(np.pi * (np.arange(400) + 0.5) / 800)
    square = np.polynomial.chebyshev.Chebyshev.fit(
        nodes**2, np.sin(2 * np.pi * nodes) / nodes, 4, domain=[0, 1 / 16]
    ).convert(kind=np.polynomial.Polynomial, domain=[-1, 1], window=[-1, 1])
    cosine = np.polynomial.chebyshev.Chebyshev.fit(
        nodes**2, np.cos(2 * np.pi * nodes), 4, domain=[0, 1 / 16]
    ).convert(kind=np.polynomial.Polynomial, domain=[-1, 1], window=[-1, 1])
    scale = 2.0**-12
    return (
        [float(c) * scale ** (2 * i + 1) for i, c in enumerate(square.coef)],
        [float(c) * scale ** (2 * i) for i, c in enumerate(cosine.coef)],
    )


SINE, COSINE = sine_polynomials()


def horner(coefficients, value):
    total = jnp.full_like(value, coefficients[-1])
    for coefficient in coefficients[-2::-1]:
        total = total * value + coefficient
    return total


def dot(a, b):
    return jnp.dot(a, b, preferred_element_type=F32)


def draw(bits_0, bits_1, eigen):
    uniform = (bits_0.astype(F32) + 0.5) * 2.0**-12
    square = jnp.log(uniform) * eigen * (-2.0 / (N * M))
    radius = square * lax.rsqrt(square)
    past = bits_1.astype(F32) - 2047.5
    h = jnp.abs(past) - 1024.0
    square = h * h
    value_re = radius * (h * horner(SINE, square))
    value_im = jnp.where(past > 0, -radius, radius) * horner(COSINE, square)
    return value_re, value_im


def add(a, b):
    return a[0] + b[0], a[1] + b[1]


def sub(a, b):
    return a[0] - b[0], a[1] - b[1]


def turn_back(a):
    return a[1], -a[0]


def dft_4(a, b, c, d):
    even, odd = add(a, c), add(b, d)
    less, turned = sub(a, c), turn_back(sub(b, d))
    return add(even, odd), add(less, turned), sub(even, odd), sub(less, turned)


def spin(a, step):
    if step == 0:
        return a
    if step == 4:
        return turn_back(a)
    if step % 4 == 2:
        root = math.sqrt(0.5)
        a = ((a[0] + a[1]) * root, (a[1] - a[0]) * root)
        return a if step == 2 else turn_back(a)
    c, s = math.cos(math.pi * step / 8), math.sin(math.pi * step / 8)
    return a[0] * c + a[1] * s, a[1] * c - a[0] * s


def dft_16(v):
    first = [dft_4(v[e], v[4 + e], v[8 + e], v[12 + e]) for e in range(4)]
    second = [dft_4(*(spin(first[e][s], e * s) for e in range(4))) for s in range(4)]
    return [second[k % 4][k // 4] for k in range(16)]


IN_VMEM = pl.BlockSpec(memory_space=pltpu.VMEM)


def front_kernel(noise, eigen, all_tables, out, bits, eig, drawn, tables, values, arrived):
    moves, first = [], 0
    for g, count in enumerate(PIECES):
        rows = slice(first, first + count)
        for part in range(2):
            moves.append(pltpu.make_async_copy(noise.at[part, rows], bits.at[part, rows], arrived.at[3 * g + part]))
        moves.append(pltpu.make_async_copy(eigen.at[rows], eig.at[rows], arrived.at[3 * g + 2]))
        first += count
    x, zh, core = (lax.axis_index(name) for name in AXES[:3])
    digit = 8 * core + 4 * zh + 2 * (x % 2) + x // 2
    moves.append(pltpu.make_async_copy(all_tables.at[digit], tables, arrived.at[3 * len(PIECES)]))
    for move in moves:
        move.start()

    first = 0
    for g, count in enumerate(PIECES):
        for move in moves[3 * g : 3 * g + 3]:
            move.wait()
        if first < EARLY:

            def draws(i, carry, first=first):
                rows = pl.ds(pl.multiple_of(first + 32 * i, 32), 32)
                drawn[0, rows, :], drawn[1, rows, :] = draw(bits[0, rows, :], bits[1, rows, :], eig[rows, :])
                return carry

            lax.fori_loop(0, count // 32, draws, 0)
        first += count
    moves[-1].wait()

    def prepare(i):
        columns = slice(BLOCK * i, BLOCK * (i + 1))
        parts = []
        for j in range(4):
            known = min(max(EARLY - 128 * j, 0), 128)
            old, new = slice(128 * j, 128 * j + known), slice(128 * j + known, 128 * (j + 1))
            part = [(drawn[0, old, columns], drawn[1, old, columns])] if known else []
            if known < 128:
                part.append(draw(bits[0, new, columns], bits[1, new, columns], eig[new, columns]))
            parts.append(part[0] if len(part) == 1 else tuple(jnp.concatenate(both, 0) for both in zip(*part)))
        for r, value in enumerate(dft_4(*parts)):
            for part in range(2):
                high, low = split(value[part])
                for at, half in ((0, high), (256, low)):
                    values[i, r, at + 128 * part : at + 128 * (part + 1), :] = half

    def multiply(i):
        for r in range(4):
            table = jnp.concatenate([tables[r, :, :256], tables[r, :, 256:]], 0)
            both = dot(table, values[i, r, :256, :])
            both = both[:256] + both[256:] + dot(tables[r, :, :256], values[i, r, 256:, :])
            for a in range(BLOCK // 128):
                for row in range(0, 256, 8):
                    part, zl, y, b = row // 128, row // 64 % 2, row // 16 % 4, row // 8 % 2
                    out[i, b, a, y, zl, part, r] = both[row : row + 8, 128 * a : 128 * (a + 1)]

    prepare(0)
    for i in range(STEPS):
        if i + 1 < STEPS:
            prepare(i + 1)
        multiply(i)


def front(noise, eigen):
    operands = (noise, eigen, jnp.asarray(column_tables()))
    return pl.pallas_call(
        front_kernel,
        in_specs=[pl.BlockSpec(memory_space=pltpu.HBM)] * 3,
        out_specs=IN_VMEM,
        out_shape=jax.ShapeDtypeStruct((4, 2, 2, 4, 2, 2, 4, 8, 128), F32),
        scratch_shapes=[
            pltpu.VMEM((2, LOCAL, WIDTH), jnp.int32),
            pltpu.VMEM((LOCAL, WIDTH), F32),
            pltpu.VMEM((2, EARLY, WIDTH), F32),
            pltpu.VMEM((4, 256, 512), BF16),
            pltpu.VMEM((STEPS, 4, 512, BLOCK), BF16),
            pltpu.SemaphoreType.DMA((3 * len(PIECES) + 1,)),
        ],
        compiler_params=pltpu.CompilerParams(vmem_limit_bytes=32 * 2**20),
        cost_estimate=pl.CostEstimate(flops=2 * 10**9, bytes_accessed=12 * 2**20, transcendentals=0),
    )(*(pltpu.with_memory_space_constraint(value, pltpu.HBM) for value in operands))


def middle_kernel(data, out):
    def step(at, carry):
        for y, zl in ((y, zl) for y in range(4) for zl in range(2)):
            r, values = at, []
            for e in range(16):
                core, zh, xl, xh = e >> 3, e >> 2 & 1, e >> 1 & 1, e & 1
                index = (2 * xh + xl, core, zh, y, zl)
                values.append((data[*index, 0, r], data[*index, 1, r]))
            for k, value in enumerate(dft_16(values)):
                core, zh, xl, xh = k & 1, k >> 1 & 1, k >> 2 & 1, k >> 3
                place = 8 * zh + 4 * zl + 2 * xh + xl
                row = pl.multiple_of(512 * place + 256 * core + 64 * r, 64)
                for part in range(2):
                    out[pl.ds(row + 2 * y + part, 8, stride=8), :] = value[part]
        return carry

    lax.fori_loop(0, 4, step, 0)


def middle(data):
    return pl.pallas_call(
        middle_kernel,
        in_specs=[IN_VMEM],
        out_specs=IN_VMEM,
        out_shape=jax.ShapeDtypeStruct((8192, 128), F32),
        compiler_params=pltpu.CompilerParams(vmem_limit_bytes=32 * 2**20),
        cost_estimate=pl.CostEstimate(flops=10**7, bytes_accessed=8 * 2**20, transcendentals=0),
    )(data)


ROWS = 32
TOGETHER = 8


def row_kernel(data, first, twist, last, out, done, sent):
    def move(step, tile, part):
        row = pl.multiple_of(64 * ROWS * step + 512 * tile, 512)
        return pltpu.make_async_copy(
            done.at[part, pl.ds(row, 512)], out.at[part, pl.ds(row, 512)], sent.at[ROWS // 4 * step + 2 * tile + part]
        )

    left = lax.broadcasted_iota(jnp.int32, (64, 128), 1) < 64

    def run(step, carry):
        pieces = []
        for t in range(ROWS):
            pieces.append(data[:, ROWS * step // 32, t % 4, ROWS * step % 32 // 4 + t // 4].reshape(128, 128))
        high, low = split(jnp.concatenate(pieces, 1))
        sums = dot(first[...], jnp.concatenate([high, low], 0))
        sums = sums[:128] + sums[128:]
        for group in range(0, ROWS, TOGETHER):
            sides = []
            for side in range(2):
                turned = []
                for t in range(group + side, group + TOGETHER, 2):
                    at = slice(128 * t, 128 * (t + 1))
                    re, im = sums[:64, at], sums[64:, at]
                    turned.append(jnp.concatenate([re * twist[0] - im * twist[1], re * twist[1] + im * twist[0]], 1))
                high, low = split(jnp.concatenate(turned, 0))
                table = last[side, 0]
                sides.append(dot(high, table) + dot(low, table) + dot(high, last[side, 1]))
            for t in range(group, group + TOGETHER, 2):
                at = slice(32 * (t - group), 32 * (t - group) + 64)
                for part in range(2):
                    lanes = slice(128 * part, 128 * (part + 1))
                    even, odd = sides[0][at, lanes], sides[1][at, lanes]
                    whole = jnp.concatenate([jnp.where(left, even, odd), jnp.where(left, odd, even)], 0).T
                    row = pl.multiple_of(64 * ROWS * step, 64 * ROWS) + 512 * (t // 8) + t % 8
                    done[part, pl.ds(row, 64, stride=8), :] = jnp.where(left, whole[:64], whole[64:])
                    done[part, pl.ds(row + 1, 64, stride=8), :] = jnp.where(left, whole[64:], whole[:64])
                if t % 8 == 6:
                    for part in range(2):
                        move(step, t // 8, part).start()
        return carry

    lax.fori_loop(0, 64 // ROWS, run, 0)
    for step in range(64 // ROWS):
        for tile in range(ROWS // 8):
            for part in range(2):
                move(step, tile, part).wait()


def row_transform(data):
    tables = [jnp.asarray(table) for table in row_tables()]
    result = pl.pallas_call(
        row_kernel,
        in_specs=[IN_VMEM] * 4,
        out_specs=pl.BlockSpec(memory_space=pltpu.HBM),
        out_shape=jax.ShapeDtypeStruct((2, 4096, 128), F32),
        scratch_shapes=[pltpu.VMEM((2, 4096, 128), F32), pltpu.SemaphoreType.DMA((16,))],
        compiler_params=pltpu.CompilerParams(vmem_limit_bytes=20 * 2**20),
        cost_estimate=pl.CostEstimate(flops=3 * 10**9, bytes_accessed=9 * 2**20, transcendentals=0),
    )(data.reshape(16, 2, 4, 8, 8, 128), *tables)
    return result.reshape(2, 8, 64, 8, 128).transpose(0, 1, 3, 2, 4).reshape(2, 64, M)


def on_device(noise, eigen):
    with jax.named_scope("columns"):
        data = front(noise, eigen)
    with jax.named_scope("first_exchange"):
        data = lax.all_to_all(data.reshape(64, 2, 2, 32, 128), ("x", "core", "zh", "y"), 0, 0, tiled=True)
    with jax.named_scope("middle"):
        data = middle(data.reshape(4, 2, 2, 4, 2, 2, 4, 8, 128))
    with jax.named_scope("second_exchange"):
        data = lax.all_to_all(data.reshape(32, 256, 128), ("zh", "zl", "x", "core"), 0, 0, tiled=True)
    with jax.named_scope("rows"):
        return row_transform(data)


def solution(mesh):
    fine = Mesh(mesh.devices.reshape(SIZES), AXES)
    col, row = AXES[:3], AXES[3:]
    return jax.shard_map(
        on_device,
        mesh=fine,
        in_specs=(P(None, col, row), P(col, row)),
        out_specs=P(None, AXES, None),
        check_vma=False,
    )
```

```python
import functools
import math

import jax
import jax.numpy as jnp
import ml_dtypes
import numpy as np
from jax import lax
from jax.experimental import pallas as pl
from jax.experimental.pallas import tpu as pltpu
from jax.sharding import Mesh, PartitionSpec as P

N = 8192
M = 8192
LOCAL = 512
WIDTH = 1024
BLOCK = 256
STEPS = WIDTH // BLOCK
PIECES = (32, 32, 64, 64, 64, 64, 64, 64, 64)
EARLY = 448

AXES = ("x", "zh", "core", "zl", "y")
SIZES = (4, 2, 2, 2, 4)

F32 = jnp.float32
BF16 = jnp.bfloat16


def halves(table):
    high = table.astype(np.float32).astype(ml_dtypes.bfloat16)
    low = (table - high.astype(np.float64)).astype(np.float32).astype(ml_dtypes.bfloat16)
    return high, low


def split(value):
    high = value.astype(BF16)
    low = (value - high.astype(F32)).astype(BF16)
    return high, low


def column_tables():
    e, r, m, j = np.ix_(np.arange(16), np.arange(4), np.arange(128), np.arange(128))
    angle = 2.0 * np.pi * ((4 * m + r) * (16 * j + e) % N) / N
    cosine, sine = np.cos(angle), np.sin(angle)
    table = np.concatenate([np.concatenate([cosine, sine], -1), np.concatenate([-sine, cosine], -1)], -2)
    return np.concatenate(halves(table), -1)


def row_tables():
    zh, zl, x, y = np.ix_(np.arange(2), np.arange(2), np.arange(4), np.arange(4))
    place = 8 * (4 * zl + y) + 2 * x + zh
    angle = 2.0 * np.pi * (np.arange(64)[:, None] * place.reshape(1, 64) % 64) / 64
    cosine, sine = np.cos(angle), np.sin(angle)
    real_part = np.stack([cosine, sine], -1).reshape(64, 128)
    imag_part = np.stack([-sine, cosine], -1).reshape(64, 128)
    high, low = halves(np.concatenate([real_part, imag_part], 0))
    first = np.concatenate([np.concatenate([high, high], 1), np.concatenate([low, np.zeros_like(low)], 1)], 0)
    angle = 2.0 * np.pi * np.outer(np.arange(64), np.arange(128)) / M
    twist = np.stack([np.cos(angle), -np.sin(angle)]).astype(np.float32)
    last = []
    for order in ([0, 1], [1, 0]):
        k = 2 * np.arange(64)[None, :] + np.array(order)[:, None]
        angle = 2.0 * np.pi * (np.outer(np.arange(128), k.reshape(128)) % 128) / 128
        cosine, sine = np.cos(angle), np.sin(angle)
        table = np.concatenate([np.concatenate([cosine, -sine], 1), np.concatenate([sine, cosine], 1)], 0)
        last.append(np.stack(halves(table)))
    return first, twist, np.stack(last)


def sine_polynomials():
    nodes = 0.25 * np.cos(np.pi * (np.arange(400) + 0.5) / 800)
    square = np.polynomial.chebyshev.Chebyshev.fit(
        nodes**2, np.sin(2 * np.pi * nodes) / nodes, 4, domain=[0, 1 / 16]
    ).convert(kind=np.polynomial.Polynomial, domain=[-1, 1], window=[-1, 1])
    cosine = np.polynomial.chebyshev.Chebyshev.fit(
        nodes**2, np.cos(2 * np.pi * nodes), 4, domain=[0, 1 / 16]
    ).convert(kind=np.polynomial.Polynomial, domain=[-1, 1], window=[-1, 1])
    scale = 2.0**-12
    return (
        [float(c) * scale ** (2 * i + 1) for i, c in enumerate(square.coef)],
        [float(c) * scale ** (2 * i) for i, c in enumerate(cosine.coef)],
    )


SINE, COSINE = sine_polynomials()


def horner(coefficients, value):
    total = jnp.full_like(value, coefficients[-1])
    for coefficient in coefficients[-2::-1]:
        total = total * value + coefficient
    return total


def dot(a, b):
    return jnp.dot(a, b, preferred_element_type=F32)


def draw(bits_0, bits_1, eigen):
    uniform = (bits_0.astype(F32) + 0.5) * 2.0**-12
    square = jnp.log(uniform) * eigen * (-2.0 / (N * M))
    radius = square * lax.rsqrt(square)
    past = bits_1.astype(F32) - 2047.5
    h = jnp.abs(past) - 1024.0
    square = h * h
    value_re = radius * (h * horner(SINE, square))
    value_im = jnp.where(past > 0, -radius, radius) * horner(COSINE, square)
    return value_re, value_im


def add(a, b):
    return a[0] + b[0], a[1] + b[1]


def sub(a, b):
    return a[0] - b[0], a[1] - b[1]


def turn_back(a):
    return a[1], -a[0]


def dft_4(a, b, c, d):
    even, odd = add(a, c), add(b, d)
    less, turned = sub(a, c), turn_back(sub(b, d))
    return add(even, odd), add(less, turned), sub(even, odd), sub(less, turned)


def spin(a, step):
    if step == 0:
        return a
    if step == 4:
        return turn_back(a)
    if step % 4 == 2:
        root = math.sqrt(0.5)
        a = ((a[0] + a[1]) * root, (a[1] - a[0]) * root)
        return a if step == 2 else turn_back(a)
    c, s = math.cos(math.pi * step / 8), math.sin(math.pi * step / 8)
    return a[0] * c + a[1] * s, a[1] * c - a[0] * s


def dft_16(v):
    first = [dft_4(v[e], v[4 + e], v[8 + e], v[12 + e]) for e in range(4)]
    second = [dft_4(*(spin(first[e][s], e * s) for e in range(4))) for s in range(4)]
    return [second[k % 4][k // 4] for k in range(16)]


IN_VMEM = pl.BlockSpec(memory_space=pltpu.VMEM)


def front_kernel(noise, eigen, all_tables, out, bits, eig, drawn, tables, values, arrived):
    moves, first = [], 0
    for g, count in enumerate(PIECES):
        rows = slice(first, first + count)
        for part in range(2):
            moves.append(pltpu.make_async_copy(noise.at[part, rows], bits.at[part, rows], arrived.at[3 * g + part]))
        moves.append(pltpu.make_async_copy(eigen.at[rows], eig.at[rows], arrived.at[3 * g + 2]))
        first += count
    x, zh, core = (lax.axis_index(name) for name in AXES[:3])
    digit = 8 * core + 4 * zh + 2 * (x % 2) + x // 2
    moves.append(pltpu.make_async_copy(all_tables.at[digit], tables, arrived.at[3 * len(PIECES)]))
    for move in moves:
        move.start()

    first = 0
    for g, count in enumerate(PIECES):
        for move in moves[3 * g : 3 * g + 3]:
            move.wait()
        if first < EARLY:

            def draws(i, carry, first=first):
                rows = pl.ds(pl.multiple_of(first + 32 * i, 32), 32)
                drawn[0, rows, :], drawn[1, rows, :] = draw(bits[0, rows, :], bits[1, rows, :], eig[rows, :])
                return carry

            lax.fori_loop(0, count // 32, draws, 0)
        first += count

    def prepare(i):
        columns = slice(BLOCK * i, BLOCK * (i + 1))
        parts = []
        for j in range(4):
            known = min(max(EARLY - 128 * j, 0), 128)
            old, new = slice(128 * j, 128 * j + known), slice(128 * j + known, 128 * (j + 1))
            part = [(drawn[0, old, columns], drawn[1, old, columns])] if known else []
            if known < 128:
                part.append(draw(bits[0, new, columns], bits[1, new, columns], eig[new, columns]))
            parts.append(part[0] if len(part) == 1 else tuple(jnp.concatenate(both, 0) for both in zip(*part)))
        for r, value in enumerate(dft_4(*parts)):
            for part in range(2):
                high, low = split(value[part])
                for at, half in ((0, high), (256, low)):
                    values[i, r, at + 128 * part : at + 128 * (part + 1), :] = half

    def multiply(i):
        for r in range(4):
            table = jnp.concatenate([tables[r, :, :256], tables[r, :, 256:]], 0)
            both = dot(table, values[i, r, :256, :])
            both = both[:256] + both[256:] + dot(tables[r, :, :256], values[i, r, 256:, :])
            for a in range(BLOCK // 128):
                for row in range(0, 256, 8):
                    part, zl, y, b = row // 128, row // 64 % 2, row // 16 % 4, row // 8 % 2
                    out[i, b, a, y, zl, part, r] = both[row : row + 8, 128 * a : 128 * (a + 1)]

    prepare(0)
    moves[-1].wait()
    for i in range(STEPS):
        if i + 1 < STEPS:
            prepare(i + 1)
        multiply(i)


def front(noise, eigen):
    operands = (noise, eigen, jnp.asarray(column_tables()))
    return pl.pallas_call(
        front_kernel,
        in_specs=[pl.BlockSpec(memory_space=pltpu.HBM)] * 3,
        out_specs=IN_VMEM,
        out_shape=jax.ShapeDtypeStruct((4, 2, 2, 4, 2, 2, 4, 8, 128), F32),
        scratch_shapes=[
            pltpu.VMEM((2, LOCAL, WIDTH), jnp.int32),
            pltpu.VMEM((LOCAL, WIDTH), F32),
            pltpu.VMEM((2, EARLY, WIDTH), F32),
            pltpu.VMEM((4, 256, 512), BF16),
            pltpu.VMEM((STEPS, 4, 512, BLOCK), BF16),
            pltpu.SemaphoreType.DMA((3 * len(PIECES) + 1,)),
        ],
        compiler_params=pltpu.CompilerParams(vmem_limit_bytes=32 * 2**20),
        cost_estimate=pl.CostEstimate(flops=2 * 10**9, bytes_accessed=12 * 2**20, transcendentals=0),
    )(*(pltpu.with_memory_space_constraint(value, pltpu.HBM) for value in operands))


def middle_kernel(data, out):
    def step(at, carry):
        for y, zl in ((y, zl) for y in range(4) for zl in range(2)):
            r, values = at, []
            for e in range(16):
                core, zh, xl, xh = e >> 3, e >> 2 & 1, e >> 1 & 1, e & 1
                index = (2 * xh + xl, core, zh, y, zl)
                values.append((data[*index, 0, r], data[*index, 1, r]))
            for k, value in enumerate(dft_16(values)):
                core, zh, xl, xh = k & 1, k >> 1 & 1, k >> 2 & 1, k >> 3
                place = 8 * zh + 4 * zl + 2 * xh + xl
                row = pl.multiple_of(512 * place + 256 * core + 64 * r, 64)
                for part in range(2):
                    out[pl.ds(row + 2 * y + part, 8, stride=8), :] = value[part]
        return carry

    lax.fori_loop(0, 4, step, 0)


def middle(data):
    return pl.pallas_call(
        middle_kernel,
        in_specs=[IN_VMEM],
        out_specs=IN_VMEM,
        out_shape=jax.ShapeDtypeStruct((8192, 128), F32),
        compiler_params=pltpu.CompilerParams(vmem_limit_bytes=32 * 2**20),
        cost_estimate=pl.CostEstimate(flops=10**7, bytes_accessed=8 * 2**20, transcendentals=0),
    )(data)


ROWS = 32
TOGETHER = 8


def row_kernel(data, first, twist, last, out, done, sent):
    def move(step, tile, part):
        row = pl.multiple_of(64 * ROWS * step + 512 * tile, 512)
        return pltpu.make_async_copy(
            done.at[part, pl.ds(row, 512)], out.at[part, pl.ds(row, 512)], sent.at[ROWS // 4 * step + 2 * tile + part]
        )

    left = lax.broadcasted_iota(jnp.int32, (64, 128), 1) < 64

    def run(step, carry):
        pieces = []
        for t in range(ROWS):
            pieces.append(data[:, ROWS * step // 32, t % 4, ROWS * step % 32 // 4 + t // 4].reshape(128, 128))
        high, low = split(jnp.concatenate(pieces, 1))
        sums = dot(first[...], jnp.concatenate([high, low], 0))
        sums = sums[:128] + sums[128:]
        for group in range(0, ROWS, TOGETHER):
            sides = []
            for side in range(2):
                turned = []
                for t in range(group + side, group + TOGETHER, 2):
                    at = slice(128 * t, 128 * (t + 1))
                    re, im = sums[:64, at], sums[64:, at]
                    turned.append(jnp.concatenate([re * twist[0] - im * twist[1], re * twist[1] + im * twist[0]], 1))
                high, low = split(jnp.concatenate(turned, 0))
                table = last[side, 0]
                sides.append(dot(high, table) + dot(low, table) + dot(high, last[side, 1]))
            for t in range(group, group + TOGETHER, 2):
                at = slice(32 * (t - group), 32 * (t - group) + 64)
                for part in range(2):
                    lanes = slice(128 * part, 128 * (part + 1))
                    even, odd = sides[0][at, lanes], sides[1][at, lanes]
                    whole = jnp.concatenate([jnp.where(left, even, odd), jnp.where(left, odd, even)], 0).T
                    row = pl.multiple_of(64 * ROWS * step, 64 * ROWS) + 512 * (t // 8) + t % 8
                    done[part, pl.ds(row, 64, stride=8), :] = jnp.where(left, whole[:64], whole[64:])
                    done[part, pl.ds(row + 1, 64, stride=8), :] = jnp.where(left, whole[64:], whole[:64])
                if t % 8 == 6:
                    for part in range(2):
                        move(step, t // 8, part).start()
        return carry

    lax.fori_loop(0, 64 // ROWS, run, 0)
    for step in range(64 // ROWS):
        for tile in range(ROWS // 8):
            for part in range(2):
                move(step, tile, part).wait()


def row_transform(data):
    tables = [jnp.asarray(table) for table in row_tables()]
    result = pl.pallas_call(
        row_kernel,
        in_specs=[IN_VMEM] * 4,
        out_specs=pl.BlockSpec(memory_space=pltpu.HBM),
        out_shape=jax.ShapeDtypeStruct((2, 4096, 128), F32),
        scratch_shapes=[pltpu.VMEM((2, 4096, 128), F32), pltpu.SemaphoreType.DMA((16,))],
        compiler_params=pltpu.CompilerParams(vmem_limit_bytes=20 * 2**20),
        cost_estimate=pl.CostEstimate(flops=3 * 10**9, bytes_accessed=9 * 2**20, transcendentals=0),
    )(data.reshape(16, 2, 4, 8, 8, 128), *tables)
    return result.reshape(2, 8, 64, 8, 128).transpose(0, 1, 3, 2, 4).reshape(2, 64, M)


def on_device(noise, eigen):
    with jax.named_scope("columns"):
        data = front(noise, eigen)
    with jax.named_scope("first_exchange"):
        data = lax.all_to_all(data.reshape(64, 2, 2, 32, 128), ("x", "core", "zh", "y"), 0, 0, tiled=True)
    with jax.named_scope("middle"):
        data = middle(data.reshape(4, 2, 2, 4, 2, 2, 4, 8, 128))
    with jax.named_scope("second_exchange"):
        data = lax.all_to_all(data.reshape(32, 256, 128), ("zh", "zl", "x", "core"), 0, 0, tiled=True)
    with jax.named_scope("rows"):
        return row_transform(data)


def solution(mesh):
    fine = Mesh(mesh.devices.reshape(SIZES), AXES)
    col, row = AXES[:3], AXES[3:]
    return jax.shard_map(
        on_device,
        mesh=fine,
        in_specs=(P(None, col, row), P(col, row)),
        out_specs=P(None, AXES, None),
        check_vma=False,
    )
```
